32 devices in a mesh: dp: 16 (over z, x, core), ctx: 2 (over y).
Axes of the slice: x: 2, y: 2, z: 4, core: 2. Of those that a mesh axis runs over, the one named last changes fastest.
Arguments:
- tokens: bfloat16 [16384, 1024], P(('dp', 'ctx')), may hold values from -6 to 6
- frame_index: int32 [16384], P(('dp', 'ctx')), may hold values from 0 to 31
- row_index: int32 [16384], P(('dp', 'ctx')), may hold values from 0 to 15
- column_index: int32 [16384], P(('dp', 'ctx')), may hold values from 0 to 15
- norm1_gain: bfloat16 [1024], P(('dp', 'ctx')), may hold values from 0.5 to 1.5
- norm1_bias: bfloat16 [1024], P(('dp', 'ctx')), may hold values from -3 to 3
- qkv_weight: bfloat16 [1024, 3072], P('dp', 'ctx'), may hold values from -0.1875 to 0.1875
- qkv_bias: bfloat16 [3072], P(('dp', 'ctx')), may hold values from -0.625 to 0.625
- proj_weight: bfloat16 [1024, 1024], P('dp', 'ctx'), may hold values from -1.5 to 1.5
- proj_bias: bfloat16 [1024], P(('dp', 'ctx')), may hold values from -3 to 3
- norm2_gain: bfloat16 [1024], P(('dp', 'ctx')), may hold values from 0.5 to 1.5
- norm2_bias: bfloat16 [1024], P(('dp', 'ctx')), may hold values from -3 to 3
- up_weight: bfloat16 [1024, 4096], P('dp', 'ctx'), may hold values from -0.1875 to 0.1875
- up_bias: bfloat16 [4096], P(('dp', 'ctx')), may hold values from -3 to 3
- down_weight: bfloat16 [4096, 1024], P('dp', 'ctx'), may hold values from -0.09375 to 0.09375
- down_bias: bfloat16 [1024], P(('dp', 'ctx')), may hold values from -3 to 3
- cotangent: bfloat16 [16384, 1024], P(('dp', 'ctx')), may hold values from -6 to 6
Outputs:
- block_out: bfloat16 [16384, 1024], P(('dp', 'ctx'))
- tokens_grad: bfloat16 [16384, 1024], P(('dp', 'ctx'))
- norm1_gain_grad: float32 [1024], P(('dp', 'ctx'))
- norm1_bias_grad: float32 [1024], P(('dp', 'ctx'))
- qkv_weight_grad: float32 [1024, 3072], P('dp', 'ctx')
- qkv_bias_grad: float32 [3072], P(('dp', 'ctx'))
- proj_weight_grad: float32 [1024, 1024], P('dp', 'ctx')
- proj_bias_grad: float32 [1024], P(('dp', 'ctx'))
- norm2_gain_grad: float32 [1024], P(('dp', 'ctx'))
- norm2_bias_grad: float32 [1024], P(('dp', 'ctx'))
- up_weight_grad: float32 [1024, 4096], P('dp', 'ctx')
- up_bias_grad: float32 [4096], P(('dp', 'ctx'))
- down_weight_grad: float32 [4096, 1024], P('dp', 'ctx')
- down_bias_grad: float32 [1024], P(('dp', 'ctx'))
The draws below stay inside these ranges and needn't reach their ends.
All inputs are finite; a program needn't handle non-finite values.
Results may differ from the reference program's by a relative error of at most 0.019.
Values may be sent and summed in bfloat16 or wider, within the bound.
No kernel may reach another device: no remote copies, remote signals or barrier semaphores. Data moves between devices by JAX's collectives and lax.ppermute only.
A program may use at most 192 MiB of HBM per device.

```python
import jax
import jax.numpy as jnp
from jax import lax

D = 1024
HEADS = 16
FF = 4096
LENGTH = 1024
PIECE = 512
SEQS = 1
TOKENS = 16384
N_DP = 16
N_CTX = 2


def with_ends(drawn, own_key, low, top_value):
    dims = drawn.shape
    spot = [jax.random.randint(jax.random.fold_in(own_key, axis), (), 0, dims[axis]) for axis in range(len(dims))]
    drawn = drawn.at[tuple(spot)].set(low)
    longest = dims.index(max(dims))
    spot[longest] = (spot[longest] + 1) % dims[longest]
    return drawn.at[tuple(spot)].set(top_value)


def shard_levels(rng, shape, shards, low, top_value):
    gain = 1.0
    for dim, parts in shards:
        heights = jax.random.uniform(jax.random.fold_in(jax.random.fold_in(rng, 6), dim), (parts,), jnp.float32, low / len(shards), top_value / len(shards))
        gain = gain * jnp.repeat(jnp.exp(heights), shape[dim] // parts).reshape((-1,) + (1,) * (len(shape) - 1 - dim))
    return gain


def noise(rng, extent, width, limit, shards=(), held_as=jnp.bfloat16):
    values = jax.random.normal(rng, extent, jnp.float32) * width
    if len(shards) > 0:
        values = shard_levels(rng, extent, shards, -0.22, 0.18) * values
    return jnp.clip(values, min=-limit, max=limit).astype(held_as)


def setup_inputs(seed: int = 0) -> dict:
    arg_keys = jax.random.split(jax.random.key(seed), 18)
    return {
        "tokens": noise(arg_keys[0], (TOKENS, D), 1.0, 6.0, ((0, 32),)),
        "frame_index": with_ends(jax.random.randint(arg_keys[1], (TOKENS,), 0, 32), jax.random.fold_in(arg_keys[1], 1), 0, 31).astype(jnp.int32),
        "row_index": with_ends(jax.random.randint(arg_keys[2], (TOKENS,), 0, 16), jax.random.fold_in(arg_keys[2], 1), 0, 15).astype(jnp.int32),
        "column_index": with_ends(jax.random.randint(arg_keys[3], (TOKENS,), 0, 16), jax.random.fold_in(arg_keys[3], 1), 0, 15).astype(jnp.int32),
        "norm1_gain": jnp.clip(1.0 + 0.1 * jax.random.normal(arg_keys[4], (D,), jnp.float32), 0.5, 1.5).astype(jnp.bfloat16),
        "norm1_bias": noise(arg_keys[5], (D,), 0.5, 3.0, ((0, 32),)),
        "qkv_weight": noise(arg_keys[6], (D, 3 * D), D ** -0.5, 0.1875, ((0, 16), (1, 2))),
        "qkv_bias": noise(arg_keys[7], (3 * D,), 0.1, 0.625, ((0, 32),)),
        "proj_weight": noise(arg_keys[8], (D, D), (D // 64) ** -0.5, 1.5, ((0, 16), (1, 2))),
        "proj_bias": noise(arg_keys[9], (D,), 0.5, 3.0, ((0, 32),)),
        "norm2_gain": jnp.clip(1.0 + 0.1 * jax.random.normal(arg_keys[10], (D,), jnp.float32), 0.5, 1.5).astype(jnp.bfloat16),
        "norm2_bias": noise(arg_keys[11], (D,), 0.5, 3.0, ((0, 32),)),
        "up_weight": noise(arg_keys[12], (D, FF), D ** -0.5, 0.1875, ((0, 16), (1, 2))),
        "up_bias": noise(arg_keys[13], (FF,), 0.5, 3.0, ((0, 32),)),
        "down_weight": noise(arg_keys[14], (FF, D), FF ** -0.5, 0.09375, ((0, 16), (1, 2))),
        "down_bias": noise(arg_keys[15], (D,), 0.5, 3.0, ((0, 32),)),
        "cotangent": noise(arg_keys[16], (TOKENS, D), 1.0, 6.0, ((0, 32),)),
    }


EPS = 1e-06
BEST = lax.Precision.HIGHEST

@jax.custom_vjp
def low(v):
    return lax.optimization_barrier(v.astype(jnp.bfloat16)).astype(jnp.float32)

@jax.custom_vjp
def low_back(v):
    return v

def low_keep(v):
    return (low(v), None)

def low_pass(kept, grad):
    return (grad,)

def back_keep(v):
    return (v, None)

def back_low(kept, grad):
    return (low(grad),)
low.defvjp(low_keep, low_pass)
low_back.defvjp(back_keep, back_low)

def norm_rows(values, gain_row, shift_row):
    row_mean = lax.optimization_barrier(jnp.mean(values, axis=-1, keepdims=True))
    centred = values - row_mean
    variance = lax.optimization_barrier(jnp.mean(centred * centred, axis=-1, keepdims=True))
    return centred * lax.rsqrt(variance + EPS) * gain_row + shift_row

def tables(frames, patch_rows, patch_columns, head_size):
    section = 2 * (head_size // 3 // 2)
    half_size = section // 2
    frequency = 1.0 / 10000.0 ** (jnp.arange(half_size).astype(jnp.float32) / half_size)
    cosines = []
    sines = []
    for place in (frames, patch_rows, patch_columns):
        angles = place.astype(jnp.float32)[..., None] * frequency
        cosines = cosines + [jnp.cos(angles), jnp.cos(angles)]
        sines = sines + [jnp.sin(angles), jnp.sin(angles)]
    spare = head_size - 3 * section
    cosines.append(jnp.ones(frames.shape + (spare,), jnp.float32))
    sines.append(jnp.zeros(frames.shape + (spare,), jnp.float32))
    return (jnp.concatenate(cosines, axis=-1), jnp.concatenate(sines, axis=-1))

def turn_half(values):
    head_size = values.shape[-1]
    section = 2 * (head_size // 3 // 2)
    half_size = section // 2
    pieces = []
    for part_number in range(3):
        begin = part_number * section
        pieces.append(-values[..., begin + half_size:begin + section])
        pieces.append(values[..., begin:begin + half_size])
    pieces.append(jnp.zeros_like(values[..., 3 * section:]))
    return jnp.concatenate(pieces, axis=-1)

def rotary(values, cosine_table, sine_table):
    return values * cosine_table + turn_half(values) * sine_table

def forward(params, block_in, cosine_table, sine_table):
    norm1_gain, norm1_bias, qkv_weight, qkv_bias, proj_weight, proj_bias, norm2_gain, norm2_bias, up_weight, up_bias, down_weight, down_bias = params
    clip_count, clip_length, model_width = block_in.shape
    head_size = model_width // HEADS
    score_scale = head_size ** (-0.5)
    head_shape = (clip_count, clip_length, HEADS, head_size)
    normed = low(norm_rows(block_in, norm1_gain, norm1_bias))
    projected = low_back(jnp.dot(normed, qkv_weight, precision=BEST) + qkv_bias)
    queries = low(rotary(projected[..., :model_width].reshape(head_shape), cosine_table, sine_table))
    keys_all = low(rotary(projected[..., model_width:2 * model_width].reshape(head_shape), cosine_table, sine_table))
    values_all = low(projected[..., 2 * model_width:].reshape(head_shape))

    def one_head(head_number):
        query_head = lax.dynamic_index_in_dim(queries, head_number, 2, keepdims=False)
        key_head = lax.dynamic_index_in_dim(keys_all, head_number, 2, keepdims=False)
        value_head = lax.dynamic_index_in_dim(values_all, head_number, 2, keepdims=False)
        scores = low_back(jnp.einsum('sqd,skd->sqk', query_head, key_head, precision=BEST) * score_scale)
        row_top = lax.optimization_barrier(jnp.max(scores, axis=-1, keepdims=True))
        weights = jnp.exp(scores - row_top)
        probs = low(weights / lax.optimization_barrier(jnp.sum(weights, axis=-1, keepdims=True)))
        return jnp.einsum('sqk,skd->sqd', probs, value_head, precision=BEST)
    attended = lax.map(jax.checkpoint(one_head), jnp.arange(HEADS, dtype=jnp.int32))
    attended = low(low_back(jnp.transpose(attended, (1, 2, 0, 3)).reshape(clip_count, clip_length, model_width)))
    branch = low_back(jnp.dot(attended, proj_weight, precision=BEST) + proj_bias)
    middle = block_in + branch
    second = low(norm_rows(middle, norm2_gain, norm2_bias))
    hidden = low_back(jnp.dot(second, up_weight, precision=BEST) + up_bias)
    active = low(jax.nn.gelu(hidden, approximate=False))
    output = low_back(jnp.dot(active, down_weight, precision=BEST) + down_bias)
    return middle + output

def reference(tokens, frame_index, row_index, column_index, norm1_gain, norm1_bias, qkv_weight, qkv_bias, proj_weight, proj_bias, norm2_gain, norm2_bias, up_weight, up_bias, down_weight, down_bias, cotangent):
    params = tuple((array.astype(jnp.float32) for array in (norm1_gain, norm1_bias, qkv_weight, qkv_bias, proj_weight, proj_bias, norm2_gain, norm2_bias, up_weight, up_bias, down_weight, down_bias)))
    model_width = tokens.shape[1]
    head_size = model_width // HEADS

    def arrange(array):
        tail = array.shape[1:]
        array = array.reshape((N_DP, N_CTX, SEQS, PIECE) + tail)
        array = jnp.swapaxes(array, 1, 2)
        return array.reshape((N_DP, SEQS, LENGTH) + tail)

    def restore(array):
        array = array.reshape((N_DP, SEQS, N_CTX, PIECE, model_width))
        array = jnp.swapaxes(array, 1, 2)
        return array.reshape((TOKENS, model_width))
    inputs_all = arrange(tokens.astype(jnp.float32))
    grads_all = arrange(cotangent.astype(jnp.float32))
    cosine_table, sine_table = tables(arrange(frame_index), arrange(row_index), arrange(column_index), head_size)
    cosine_table = cosine_table[..., None, :]
    sine_table = sine_table[..., None, :]

    def group_step(totals, group):
        block_in, block_grad, cosine_group, sine_group = group
        result, pull = jax.vjp(lambda prm, inp: forward(prm, inp, cosine_group, sine_group), params, block_in)
        param_grads, input_grad = pull(block_grad)
        totals = tuple((older + newer for older, newer in zip(totals, param_grads)))
        return (totals, (result, input_grad))
    start = tuple((jnp.zeros_like(array) for array in params))
    totals, outputs = lax.scan(group_step, start, (inputs_all, grads_all, cosine_table, sine_table))
    results, input_grads = outputs
    return (restore(results).astype(jnp.bfloat16), restore(input_grads).astype(jnp.bfloat16), totals[0], totals[1], totals[2], totals[3], totals[4], totals[5], totals[6], totals[7], totals[8], totals[9], totals[10], totals[11])
```

```python
import functools
import math

import jax
import jax.numpy as jnp
from jax import lax
from jax.experimental import pallas as pl
from jax.experimental.pallas import tpu as pltpu
from jax.sharding import Mesh
from jax.sharding import PartitionSpec as P

HEADS = 16
SPAN = 256
LEAST_LEN = 1024


EPS = 1e-06


def norm_rows(values, gain_row, shift_row):
    row_mean = jnp.mean(values, axis=-1, keepdims=True)
    centred = values - row_mean
    variance = jnp.mean(centred * centred, axis=-1, keepdims=True)
    return centred * lax.rsqrt(variance + EPS) * gain_row + shift_row


def tables(frames, patch_rows, patch_columns, head_size):
    section = 2 * (head_size // 3 // 2)
    half_size = section // 2
    frequency = 1.0 / 10000.0 ** (jnp.arange(half_size).astype(jnp.float32) / half_size)
    cosines = []
    sines = []
    for place in (frames, patch_rows, patch_columns):
        angles = place.astype(jnp.float32)[..., None] * frequency
        cosines = cosines + [jnp.cos(angles), jnp.cos(angles)]
        sines = sines + [jnp.sin(angles), jnp.sin(angles)]
    spare = head_size - 3 * section
    cosines.append(jnp.ones(frames.shape + (spare,), jnp.float32))
    sines.append(jnp.zeros(frames.shape + (spare,), jnp.float32))
    return (jnp.concatenate(cosines, axis=-1), jnp.concatenate(sines, axis=-1))


def turn_half(values):
    head_size = values.shape[-1]
    section = 2 * (head_size // 3 // 2)
    half_size = section // 2
    pieces = []
    for part_number in range(3):
        begin = part_number * section
        pieces.append(-values[..., begin + half_size : begin + section])
        pieces.append(values[..., begin : begin + half_size])
    pieces.append(jnp.zeros_like(values[..., 3 * section :]))
    return jnp.concatenate(pieces, axis=-1)


def rotary(values, cosine_table, sine_table):
    return values * cosine_table + turn_half(values) * sine_table


def rotary_back(values, cosine_table, sine_table):
    return values * cosine_table - turn_half(values * sine_table)


def shards(
    tokens,
    frame_index,
    row_index,
    column_index,
    norm1_gain,
    norm1_bias,
    qkv_weight,
    qkv_bias,
    proj_weight,
    proj_bias,
    norm2_gain,
    norm2_bias,
    up_weight,
    up_bias,
    down_weight,
    down_bias,
    cotangent,
):
    ctx_count = lax.axis_size("ctx")
    clip_length = max(LEAST_LEN, SPAN * ctx_count)
    piece_rows = clip_length // ctx_count
    rows_here, model_width = tokens.shape
    clip_count = rows_here // piece_rows
    head_size = model_width // HEADS
    score_scale = head_size ** (-0.5)
    head_shape = (clip_count, piece_rows, HEADS, head_size)
    long_shape = (clip_count, clip_length, HEADS, head_size)
    flat_shape = (clip_count, piece_rows, model_width)

    def gather_all():
        partial_value = (
            lax.all_gather(qkv_weight, "ctx", axis=1, tiled=True),
            lax.all_gather(proj_weight, "ctx", axis=1, tiled=True),
            lax.all_gather(up_weight, "ctx", axis=1, tiled=True),
            lax.all_gather(down_weight, "ctx", axis=1, tiled=True),
            lax.all_gather(norm1_gain, "ctx", axis=0, tiled=True),
            lax.all_gather(norm1_bias, "ctx", axis=0, tiled=True),
            lax.all_gather(qkv_bias, "ctx", axis=0, tiled=True),
            lax.all_gather(proj_bias, "ctx", axis=0, tiled=True),
            lax.all_gather(norm2_gain, "ctx", axis=0, tiled=True),
            lax.all_gather(norm2_bias, "ctx", axis=0, tiled=True),
            lax.all_gather(up_bias, "ctx", axis=0, tiled=True),
            lax.all_gather(down_bias, "ctx", axis=0, tiled=True),
        )
        return (
            lax.all_gather(partial_value[0], "dp", axis=0, tiled=True),
            lax.all_gather(partial_value[1], "dp", axis=0, tiled=True),
            lax.all_gather(partial_value[2], "dp", axis=0, tiled=True),
            lax.all_gather(partial_value[3], "dp", axis=0, tiled=True),
            lax.all_gather(partial_value[4], "dp", axis=0, tiled=True),
            lax.all_gather(partial_value[5], "dp", axis=0, tiled=True),
            lax.all_gather(partial_value[6], "dp", axis=0, tiled=True),
            lax.all_gather(partial_value[7], "dp", axis=0, tiled=True),
            lax.all_gather(partial_value[8], "dp", axis=0, tiled=True),
            lax.all_gather(partial_value[9], "dp", axis=0, tiled=True),
            lax.all_gather(partial_value[10], "dp", axis=0, tiled=True),
            lax.all_gather(partial_value[11], "dp", axis=0, tiled=True),
        )

    gathered = gather_all()
    (
        w_qkv,
        w_proj,
        w_up,
        w_down,
        gain_one,
        shift_one,
        bias_qkv,
        bias_proj,
        gain_two,
        shift_two,
        bias_up,
        bias_down,
    ) = gathered
    block_in = tokens.astype(jnp.float32).reshape(flat_shape)
    cosine_table, sine_table = tables(
        frame_index.reshape(clip_count, piece_rows),
        row_index.reshape(clip_count, piece_rows),
        column_index.reshape(clip_count, piece_rows),
        head_size,
    )
    cosine_table = cosine_table[:, :, None, :]
    sine_table = sine_table[:, :, None, :]
    normed = norm_rows(
        block_in, gain_one.astype(jnp.float32), shift_one.astype(jnp.float32)
    ).astype(jnp.bfloat16)
    projected = jnp.einsum(
        "spd,de->spe", normed, w_qkv, preferred_element_type=jnp.float32
    ) + bias_qkv.astype(jnp.float32)
    queries = rotary(
        projected[..., :model_width].reshape(head_shape), cosine_table, sine_table
    ).astype(jnp.bfloat16)
    keys_own = (
        rotary(
            projected[..., model_width : 2 * model_width].reshape(head_shape),
            cosine_table,
            sine_table,
        )
        .astype(jnp.bfloat16)
        .reshape(flat_shape)
    )
    values_own = projected[..., 2 * model_width :].astype(jnp.bfloat16)
    keys_all, values_all = (
        lax.all_gather(keys_own, "ctx", axis=1, tiled=True),
        lax.all_gather(values_own, "ctx", axis=1, tiled=True),
    )
    keys_all = keys_all.reshape(long_shape)
    values_all = values_all.reshape(long_shape)

    def head_forward(head_number):
        query_head = lax.dynamic_index_in_dim(queries, head_number, 2, keepdims=False)
        key_head = lax.dynamic_index_in_dim(keys_all, head_number, 2, keepdims=False)
        value_head = lax.dynamic_index_in_dim(values_all, head_number, 2, keepdims=False)
        scores = (
            jnp.einsum("sqd,skd->sqk", query_head, key_head, preferred_element_type=jnp.float32)
            * score_scale
        )
        row_top = jnp.max(scores, axis=-1, keepdims=True)
        weights = jnp.exp(scores - row_top)
        row_total = jnp.sum(weights, axis=-1, keepdims=True)
        weights_low = (weights / row_total).astype(jnp.bfloat16)
        result = jnp.einsum(
            "sqk,skd->sqd", weights_low, value_head, preferred_element_type=jnp.float32
        )
        return (result, (row_top + jnp.log(row_total))[..., 0])

    head_numbers = jnp.arange(HEADS, dtype=jnp.int32)
    attended, log_total = lax.map(head_forward, head_numbers)
    attended_low = jnp.transpose(attended, (1, 2, 0, 3)).reshape(flat_shape).astype(jnp.bfloat16)
    branch = jnp.einsum(
        "spd,de->spe", attended_low, w_proj, preferred_element_type=jnp.float32
    ) + bias_proj.astype(jnp.float32)
    middle = block_in + branch
    second = norm_rows(middle, gain_two.astype(jnp.float32), shift_two.astype(jnp.float32)).astype(
        jnp.bfloat16
    )
    hidden = jnp.einsum(
        "spd,df->spf", second, w_up, preferred_element_type=jnp.float32
    ) + bias_up.astype(jnp.float32)
    active = jax.nn.gelu(hidden, approximate=False).astype(jnp.bfloat16)
    output = jnp.einsum(
        "spf,fd->spd", active, w_down, preferred_element_type=jnp.float32
    ) + bias_down.astype(jnp.float32)
    block_out = (middle + output).astype(jnp.bfloat16).reshape(rows_here, model_width)
    backward_weights = gather_all()
    (
        w_qkv,
        w_proj,
        w_up,
        w_down,
        gain_one,
        shift_one,
        bias_qkv,
        bias_proj,
        gain_two,
        shift_two,
        bias_up,
        bias_down,
    ) = backward_weights
    out_low = cotangent.reshape(flat_shape)
    out_grad = out_low.astype(jnp.float32)
    grad_down_bias = jnp.sum(out_grad, axis=(0, 1))
    grad_down = jnp.einsum("spf,spd->fd", active, out_low, preferred_element_type=jnp.float32)
    active_grad = jnp.einsum("spd,fd->spf", out_low, w_down, preferred_element_type=jnp.float32)
    gelu_pull = jax.vjp(lambda inner: jax.nn.gelu(inner, approximate=False), hidden)[1]
    hidden_grad = gelu_pull(active_grad)[0].astype(jnp.bfloat16)
    grad_up_bias = jnp.sum(hidden_grad.astype(jnp.float32), axis=(0, 1))
    grad_up = jnp.einsum("spd,spf->df", second, hidden_grad, preferred_element_type=jnp.float32)
    second_grad = jnp.einsum("spf,df->spd", hidden_grad, w_up, preferred_element_type=jnp.float32)
    second_pull = jax.vjp(
        norm_rows, middle, gain_two.astype(jnp.float32), shift_two.astype(jnp.float32)
    )[1]
    middle_part, grad_gain_two, grad_shift_two = second_pull(second_grad)
    middle_grad = out_grad + middle_part
    branch_low = middle_grad.astype(jnp.bfloat16)
    grad_proj_bias = jnp.sum(branch_low.astype(jnp.float32), axis=(0, 1))
    grad_proj = jnp.einsum(
        "spd,spe->de", attended_low, branch_low, preferred_element_type=jnp.float32
    )
    attended_grad = (
        jnp.einsum("spe,de->spd", branch_low, w_proj, preferred_element_type=jnp.float32)
        .astype(jnp.bfloat16)
        .reshape(head_shape)
    )

    def head_backward(head_number):
        query_head = lax.dynamic_index_in_dim(queries, head_number, 2, keepdims=False)
        key_head = lax.dynamic_index_in_dim(keys_all, head_number, 2, keepdims=False)
        value_head = lax.dynamic_index_in_dim(values_all, head_number, 2, keepdims=False)
        grad_head = lax.dynamic_index_in_dim(attended_grad, head_number, 2, keepdims=False)
        log_head = lax.dynamic_index_in_dim(log_total, head_number, 0, keepdims=False)
        scores = (
            jnp.einsum("sqd,skd->sqk", query_head, key_head, preferred_element_type=jnp.float32)
            * score_scale
        )
        weights = jnp.exp(scores - log_head[..., None])
        weights_low = weights.astype(jnp.bfloat16)
        value_grad = jnp.einsum(
            "sqk,sqd->skd", weights_low, grad_head, preferred_element_type=jnp.float32
        )
        weight_grad = jnp.einsum(
            "sqd,skd->sqk", grad_head, value_head, preferred_element_type=jnp.float32
        )
        score_grad = (
            weights * (weight_grad - jnp.sum(weights * weight_grad, axis=-1, keepdims=True))
        ).astype(jnp.bfloat16)
        query_grad = (
            jnp.einsum("sqk,skd->sqd", score_grad, key_head, preferred_element_type=jnp.float32)
            * score_scale
        )
        key_grad = (
            jnp.einsum("sqk,sqd->skd", score_grad, query_head, preferred_element_type=jnp.float32)
            * score_scale
        )
        return (query_grad, key_grad, value_grad)

    query_grads, key_grads, value_grads = lax.map(head_backward, head_numbers)
    key_full = jnp.transpose(key_grads, (1, 2, 0, 3)).reshape(clip_count, clip_length, model_width)
    value_full = jnp.transpose(value_grads, (1, 2, 0, 3)).reshape(
        clip_count, clip_length, model_width
    )
    key_part, value_part = (
        lax.psum_scatter(
            key_full.astype(jnp.bfloat16), "ctx", scatter_dimension=1, tiled=True
        ).astype(jnp.float32),
        lax.psum_scatter(
            value_full.astype(jnp.bfloat16), "ctx", scatter_dimension=1, tiled=True
        ).astype(jnp.float32),
    )
    query_grads = jnp.transpose(query_grads, (1, 2, 0, 3))
    query_back = rotary_back(query_grads, cosine_table, sine_table).reshape(flat_shape)
    key_back = rotary_back(key_part.reshape(head_shape), cosine_table, sine_table).reshape(
        flat_shape
    )
    mixed_grad = jnp.concatenate([query_back, key_back, value_part], axis=-1).astype(jnp.bfloat16)
    grad_qkv_bias = jnp.sum(mixed_grad.astype(jnp.float32), axis=(0, 1))
    grad_qkv = jnp.einsum("spd,spe->de", normed, mixed_grad, preferred_element_type=jnp.float32)
    normed_grad = jnp.einsum("spe,de->spd", mixed_grad, w_qkv, preferred_element_type=jnp.float32)
    first_pull = jax.vjp(
        norm_rows, block_in, gain_one.astype(jnp.float32), shift_one.astype(jnp.float32)
    )[1]
    input_part, grad_gain_one, grad_shift_one = first_pull(normed_grad)
    tokens_grad = (middle_grad + input_part).astype(jnp.bfloat16).reshape(rows_here, model_width)
    summed = (
        lax.psum_scatter(
            grad_qkv.astype(jnp.bfloat16), "dp", scatter_dimension=0, tiled=True
        ).astype(jnp.float32),
        lax.psum_scatter(
            grad_proj.astype(jnp.bfloat16), "dp", scatter_dimension=0, tiled=True
        ).astype(jnp.float32),
        lax.psum_scatter(
            grad_up.astype(jnp.bfloat16), "dp", scatter_dimension=0, tiled=True
        ).astype(jnp.float32),
        lax.psum_scatter(
            grad_down.astype(jnp.bfloat16), "dp", scatter_dimension=0, tiled=True
        ).astype(jnp.float32),
        lax.psum_scatter(
            grad_gain_one.astype(jnp.bfloat16), "dp", scatter_dimension=0, tiled=True
        ).astype(jnp.float32),
        lax.psum_scatter(
            grad_shift_one.astype(jnp.bfloat16), "dp", scatter_dimension=0, tiled=True
        ).astype(jnp.float32),
        lax.psum_scatter(
            grad_qkv_bias.astype(jnp.bfloat16), "dp", scatter_dimension=0, tiled=True
        ).astype(jnp.float32),
        lax.psum_scatter(
            grad_proj_bias.astype(jnp.bfloat16), "dp", scatter_dimension=0, tiled=True
        ).astype(jnp.float32),
        lax.psum_scatter(
            grad_gain_two.astype(jnp.bfloat16), "dp", scatter_dimension=0, tiled=True
        ).astype(jnp.float32),
        lax.psum_scatter(
            grad_shift_two.astype(jnp.bfloat16), "dp", scatter_dimension=0, tiled=True
        ).astype(jnp.float32),
        lax.psum_scatter(
            grad_up_bias.astype(jnp.bfloat16), "dp", scatter_dimension=0, tiled=True
        ).astype(jnp.float32),
        lax.psum_scatter(
            grad_down_bias.astype(jnp.bfloat16), "dp", scatter_dimension=0, tiled=True
        ).astype(jnp.float32),
    )
    owned = (
        lax.psum_scatter(
            summed[0].astype(jnp.bfloat16), "ctx", scatter_dimension=1, tiled=True
        ).astype(jnp.float32),
        lax.psum_scatter(
            summed[1].astype(jnp.bfloat16), "ctx", scatter_dimension=1, tiled=True
        ).astype(jnp.float32),
        lax.psum_scatter(
            summed[2].astype(jnp.bfloat16), "ctx", scatter_dimension=1, tiled=True
        ).astype(jnp.float32),
        lax.psum_scatter(
            summed[3].astype(jnp.bfloat16), "ctx", scatter_dimension=1, tiled=True
        ).astype(jnp.float32),
        lax.psum_scatter(
            summed[4].astype(jnp.bfloat16), "ctx", scatter_dimension=0, tiled=True
        ).astype(jnp.float32),
        lax.psum_scatter(
            summed[5].astype(jnp.bfloat16), "ctx", scatter_dimension=0, tiled=True
        ).astype(jnp.float32),
        lax.psum_scatter(
            summed[6].astype(jnp.bfloat16), "ctx", scatter_dimension=0, tiled=True
        ).astype(jnp.float32),
        lax.psum_scatter(
            summed[7].astype(jnp.bfloat16), "ctx", scatter_dimension=0, tiled=True
        ).astype(jnp.float32),
        lax.psum_scatter(
            summed[8].astype(jnp.bfloat16), "ctx", scatter_dimension=0, tiled=True
        ).astype(jnp.float32),
        lax.psum_scatter(
            summed[9].astype(jnp.bfloat16), "ctx", scatter_dimension=0, tiled=True
        ).astype(jnp.float32),
        lax.psum_scatter(
            summed[10].astype(jnp.bfloat16), "ctx", scatter_dimension=0, tiled=True
        ).astype(jnp.float32),
        lax.psum_scatter(
            summed[11].astype(jnp.bfloat16), "ctx", scatter_dimension=0, tiled=True
        ).astype(jnp.float32),
    )
    return (
        block_out,
        tokens_grad,
        owned[4],
        owned[5],
        owned[0],
        owned[6],
        owned[1],
        owned[7],
        owned[8],
        owned[9],
        owned[2],
        owned[10],
        owned[3],
        owned[11],
    )


LOG2E = 1.4426950408889634
COST = 0.1
NT = (((1,), (1,)), ((), ()))
NN = (((1,), (0,)), ((), ()))
TN = (((0,), (0,)), ((), ()))
F32 = jnp.float32
BF16 = jnp.bfloat16
SWAP = [(0, 1), (1, 0)]
DIAGONAL = [(0, 0), (1, 2), (2, 1), (3, 3)]
ANYWHERE = pl.BlockSpec(memory_space=pl.ANY)
WHOLE = pl.BlockSpec(memory_space=pltpu.VMEM)
SCALARS = pl.BlockSpec(memory_space=pltpu.SMEM)


def shape_of(shape, kind):
    return jax.ShapeDtypeStruct(shape, kind)


def half_lanes(number, shape):
    lane = lax.broadcasted_iota(jnp.int32, shape, 1)
    width = shape[1] // 2
    return (lane < width) if number == 0 else (lane >= width)


def keep(mask, values):
    return jnp.where(mask, values, jnp.zeros_like(values))


def dot(first, second, dims, to=F32):
    return lax.dot_general(first, second, dims, preferred_element_type=F32).astype(to)


def kernel_call(
    body, inputs, in_specs, out_shapes, scratch=(), grid=None, out_specs=None, flops=0, exps=0, room=8
):
    def size(item):
        return item.size * item.dtype.itemsize

    total = sum(size(a) for a in inputs) + sum(size(s) for s in out_shapes)
    if out_specs is None:
        out_specs = [WHOLE] * len(out_shapes)
    need = room << 20
    if grid is None:
        need += sum(size(a) for a, spec in zip(inputs, in_specs) if spec is WHOLE)
        need += sum(size(a) for a, spec in zip(out_shapes, out_specs) if spec is WHOLE)
    for item in scratch:
        if getattr(item, "memory_space", None) == pltpu.VMEM:
            need += math.prod(item.shape) * jnp.dtype(item.dtype).itemsize
    extra = {} if grid is None else {"grid": grid}
    return pl.pallas_call(
        body,
        in_specs=in_specs,
        out_specs=out_specs,
        out_shape=out_shapes,
        scratch_shapes=list(scratch),
        compiler_params=pltpu.CompilerParams(vmem_limit_bytes=min(need, 56 << 20)),
        cost_estimate=pl.CostEstimate(
            flops=int(flops * COST),
            bytes_accessed=int(total * COST),
            transcendentals=int(exps * COST),
        ),
        **extra,
    )(*inputs)


def after(values, *others):
    return lax.optimization_barrier((values,) + others)[0]


def swap(values, axis):
    return lax.ppermute(values, axis, SWAP)


def ring(values, depth):
    return lax.ppermute(values, "z", [(i, (i + 1) % depth) for i in range(depth)])


def gather_first(block, depth):
    hops = [block]
    for _ in range(depth - 1):
        hops.append(ring(hops[-1], depth))
    one = jnp.stack([hop[0] for hop in hops])
    two = jnp.stack([hop[1] for hop in hops])
    one_x = swap(one, "x")
    two_y = swap(two, "y")
    one_y = swap(one, "y")
    two_x = swap(two, "x")
    one_xy = swap(one_x, "y")
    two_xy = swap(two_y, "x")
    arrays = [one, two, one_x, two_y, one_y, two_x, one_xy, two_xy]
    marks = [(0, 0, 0), (1, 0, 0), (0, 1, 0), (1, 0, 1), (0, 0, 1), (1, 1, 0), (0, 1, 1), (1, 1, 1)]
    parts = [
        (n, z, half, z, x, y)
        for n, (half, x, y) in enumerate(marks)
        for z in range(depth)
    ]
    return arrays, parts, hops[-1], (one_xy, two_xy)


def gather_middle(block, depth, hop_gate, swap_gate):
    one, two = block[0], block[1]
    hop = jnp.stack([one, swap(one, "x"), two, swap(two, "y")])
    hops = [hop]
    for _ in range(depth - 1):
        hops.append(ring(after(hops[-1], hop_gate), depth))
    arrays = []
    parts = []
    for z in range(depth):
        parts += [
            (len(arrays), 0, 0, z, 0, 0),
            (len(arrays), 1, 0, z, 1, 0),
            (len(arrays), 2, 1, z, 0, 0),
            (len(arrays), 3, 1, z, 0, 1),
        ]
        arrays.append(hops[z])
    step = max(depth // 2, 1)
    for begin in range(0, depth, step):
        group = hops[begin : begin + step]
        ones = swap(after(jnp.concatenate([hop[:2] for hop in group]), swap_gate[0]), "y")
        twos = swap(after(jnp.concatenate([hop[2:] for hop in group]), swap_gate[1]), "x")
        swap_gate = (ones, twos)
        for k in range(step):
            z = begin + k
            parts += [
                (len(arrays), 2 * k, 0, z, 0, 1),
                (len(arrays), 2 * k + 1, 0, z, 1, 1),
                (len(arrays) + 1, 2 * k, 1, z, 1, 0),
                (len(arrays) + 1, 2 * k + 1, 1, z, 1, 1),
            ]
        arrays += [ones, twos]
    return arrays, parts, hops[-1], swap_gate


def gather_single(block, depth, first, last, hop_gate, swap_gate):
    hops = [jnp.stack([block, swap(block, first)])]
    for _ in range(depth - 1):
        hops.append(ring(after(hops[-1], hop_gate), depth))
    arrays = []
    parts = []

    def part(array, index, z, near, far):
        x, y = (near, far) if first == "x" else (far, near)
        return (array, index, 0, z, x, y)

    for z in range(depth):
        parts += [part(len(arrays), k, z, k, 0) for k in range(2)]
        arrays.append(hops[z])
    step = max(depth // 2, 1)
    for begin in range(0, depth, step):
        group = jnp.concatenate(hops[begin : begin + step])
        for k in range(2 * step):
            parts.append(part(len(arrays), k, begin + k // 2, k % 2, 1))
        arrays.append(swap(after(group, swap_gate), last))
        swap_gate = arrays[-1]
    return arrays, parts


def place(where_ref, depth, z, x):
    z_number = lax.rem(where_ref[0] + (depth - z), depth)
    return 2 * z_number + lax.rem(where_ref[1] + x, 2)


def start_copies(pairs, sems):
    copies = [pltpu.make_async_copy(a, b, sems.at[n]) for n, (a, b) in enumerate(pairs)]
    for copy in copies:
        copy.start()
    return copies


def add_low(*terms):
    total = terms[0].astype(F32)
    for term in terms[1:]:
        total = total + term.astype(F32)
    return total.astype(BF16)


def near_first(depth):
    order = [i % depth for i in range(1, depth + 1)]
    split = max(depth // 2, 1)
    return order[:split], order[split:]


class Scatter:
    def __init__(self, sends, first, last, depth):
        self.arrived = [swap(send, first) for send in sends]
        self.last = last
        self.depth = depth
        self.spots = [(g, k) for g, group in enumerate(near_first(depth)) for k in range(len(group))]
        self.moving = None

    def terms(self, step):
        g, k = self.spots[step]
        found = [self.keeps[g][k], self.arrived[g][k]]
        if self.moving is not None:
            found.append(self.moving)
        return found

    def hop(self, step, gate):
        terms = self.terms(step)
        terms[0] = after(terms[0], gate)
        total = add_low(*terms)
        self.moving = ring(total, self.depth)
        return total

    def finish(self, gate):
        terms = self.terms(self.depth - 1)
        terms[0] = after(terms[0], gate)
        far = add_low(*[term[1] for term in terms])
        self.near = [term[0] for term in terms]
        self.other = swap(far, self.last)
        return far

    def result(self):
        return add_low(*self.near, self.other)


def turned(values, cosine, before, after):
    wide = cosine.shape[1]
    pieces = []
    for begin in range(0, values.shape[1], wide):
        piece = values[:, begin : begin + wide]
        pieces.append(
            piece * cosine
            + pltpu.roll(piece, wide - HALF, 1) * before
            + pltpu.roll(piece, HALF, 1) * after
        )
    return pieces


def turned_back(piece, cosine, before, after):
    wide = cosine.shape[1]
    return (
        piece * cosine
        + pltpu.roll(piece * before, HALF, 1)
        + pltpu.roll(piece * after, wide - HALF, 1)
    )


def normal(values):
    mean = jnp.mean(values, axis=-1, keepdims=True)
    centred = values - mean
    variance = jnp.mean(centred * centred, axis=-1, keepdims=True)
    inverse = lax.rsqrt(variance + EPS)
    return centred * inverse, inverse


def qkv_kernel(depth, parts, where_ref, own_ref, other_ref, gain_ref, shift_ref, bias_ref,
               cosine_ref, before_ref, after_ref, *rest):
    count = 1 + max(p[0] for p in parts)
    arrays = rest[:count]
    normed_ref, query_ref, key_ref, value_ref, weight, sems = rest[count:]
    y_own = where_ref[2]
    pairs = []
    rows = arrays[0].shape[1]
    wide = query_ref.shape[1]
    thin = wide // 2
    for n, i, half, z, x, y in parts:
        spot = pl.ds(pl.multiple_of(place(where_ref, depth, z, x) * rows, rows), rows)
        y_spot = lax.rem(y_own + y, 2)
        if half == 0:
            pairs.append((arrays[n].at[i], weight.at[y_spot, spot, pl.ds(0, wide)]))
        else:
            pairs.append((arrays[n].at[i, :, pl.ds(0, thin)], weight.at[y_spot, spot, pl.ds(wide, thin)]))
    copies = start_copies(pairs, sems)
    piece = own_ref.shape[0]
    for ref, base in ((own_ref, 0), (other_ref, piece)):
        for begin in range(0, piece, 256):
            hat, _ = normal(ref[pl.ds(begin, 256), :].astype(F32))
            normed_ref[pl.ds(base + begin, 256), :] = (hat * gain_ref[...] + shift_ref[...]).astype(BF16)
    for copy in copies:
        copy.wait()
    outs = [(query_ref, 0), (query_ref, thin), (key_ref, 0), (key_ref, thin), (value_ref, 0), (value_ref, thin)]
    for number, (ref, column) in enumerate(outs):
        y, spot = divmod(number, 3)
        for begin in range(0, 2 * piece, piece):
            lines = pl.ds(begin, piece)
            result = dot(normed_ref[lines, :], weight[y, :, pl.ds(spot * thin, thin)], NN)
            result = result + bias_ref[:, pl.ds(number * thin, thin)]
            if ref is value_ref:
                ref[lines, pl.ds(column, thin)] = result.astype(BF16)
            else:
                pieces = turned(result, cosine_ref[lines, :], before_ref[lines, :], after_ref[lines, :])
                for k, item in enumerate(pieces):
                    ref[lines, pl.ds(column + k * 128, 128)] = item.astype(BF16)


def attend_kernel(query_ref, key_ref, value_ref, out_ref, log_ref, *, block, scale):
    length, width = key_ref.shape
    keys = key_ref[...]
    values = value_ref[...]
    for number in range(2):
        mask = half_lanes(number, (length, width))
        key_half = keep(mask, keys)
        value_half = keep(mask, values)
        for start in range(0, length, block):
            rows = pl.ds(start, block)
            scores = dot(query_ref[rows, :], key_half, NT)
            top = jnp.max(scores, axis=1, keepdims=True)
            weights = jnp.exp2((scores - top) * scale)
            total = jnp.sum(weights, axis=1, keepdims=True)
            part = (dot(weights.astype(BF16), value_half, NN) / total).astype(BF16)
            if number == 0:
                out_ref[rows, :] = part
            else:
                out_ref[rows, :] = out_ref[rows, :] + part
            logs = top * scale + jnp.log2(total)
            turned_logs = jnp.transpose(jnp.broadcast_to(logs, (block, 128)))
            log_ref[0, number : number + 1, rows] = turned_logs[0:1, :]


def attend(queries, keys, values, head_size):
    length, width = queries.shape
    wide = 2 * head_size
    pairs = width // wide
    spec = pl.BlockSpec((length, wide), lambda i: (0, i))
    return kernel_call(
        functools.partial(attend_kernel, block=512, scale=LOG2E * head_size**-0.5),
        [queries, keys, values],
        [spec] * 3,
        [shape_of((length, width), BF16), shape_of((pairs, 2, length), F32)],
        grid=(pairs,),
        out_specs=[spec, pl.BlockSpec((1, 2, length), lambda i: (i, 0, 0))],
        flops=16 * length * length * width,
        exps=2 * pairs * length * length,
        room=28,
    )


def attend_back_kernel(
    query_ref, key_ref, value_ref, grad_ref, log_ref, cosine_ref, before_ref, after_ref,
    query_out, key_out, value_out, sum_out, key_sum, value_sum, query_sum, *, block, scale,
):
    length, width = key_ref.shape
    keys = key_ref[...]
    values = value_ref[...]
    for number in range(2):
        mask = half_lanes(number, (length, width))
        key_half = keep(mask, keys)
        value_half = keep(mask, values)
        block_mask = half_lanes(number, (block, width))
        for start in range(0, length, block):
            rows = pl.ds(start, block)
            query = query_ref[rows, :]
            grad = grad_ref[rows, :]
            scores = dot(key_half, query, NT)
            probs = jnp.exp2(scores * (scale * LOG2E) - log_ref[0, number : number + 1, rows])
            prob_grad = dot(value_half, grad, NT)
            mean = jnp.sum(probs * prob_grad, axis=0, keepdims=True)
            score_grad = (probs * (prob_grad - mean)).astype(BF16)
            value_part = dot(probs.astype(BF16), keep(block_mask, grad), NN)
            key_part = dot(score_grad, keep(block_mask, query), NN)
            query_part = dot(score_grad, key_half, TN)
            if number == 0 and start == 0:
                value_sum[...] = value_part
                key_sum[...] = key_part
            else:
                value_sum[...] += value_part
                key_sum[...] += key_part
            if number == 0:
                query_sum[rows, :] = query_part
            else:
                query_sum[rows, :] += query_part
    tables_here = (cosine_ref[...], before_ref[...], after_ref[...])
    for slot, (ref, value) in enumerate(
        (
            (query_out, turned_back(query_sum[...] * scale, *tables_here)),
            (key_out, turned_back(key_sum[...] * scale, *tables_here)),
            (value_out, value_sum[...]),
        )
    ):
        low = value.astype(BF16)
        ref[...] = low
        sum_out[slot : slot + 1, :] = jnp.sum(low.astype(F32), axis=0, keepdims=True)


def attend_back(queries, keys, values, grads, logs, turn, head_size, begin, end):
    length = queries.shape[0]
    wide = 2 * head_size
    width = (end - begin) * wide
    spec = pl.BlockSpec((length, wide), lambda i: (0, begin + i))
    out_spec = pl.BlockSpec((length, wide), lambda i: (0, i))
    whole = pl.BlockSpec((length, wide), lambda i: (0, 0))
    return kernel_call(
        functools.partial(attend_back_kernel, block=512, scale=head_size**-0.5),
        [queries, keys, values, grads, logs, *turn],
        [spec] * 4 + [pl.BlockSpec((1, 2, length), lambda i: (begin + i, 0, 0))] + [whole] * 3,
        [shape_of((length, width), BF16)] * 3 + [shape_of((8, width), F32)],
        grid=(end - begin,),
        out_specs=[out_spec] * 3 + [pl.BlockSpec((8, wide), lambda i: (0, i))],
        scratch=[pltpu.VMEM((length, wide), F32)] * 3,
        flops=40 * length * length * width,
        exps=(end - begin) * 2 * length * length,
        room=28,
    )


def load_proj(where_ref, depth, parts, arrays, weight, sems):
    pairs = []
    group = arrays[0].shape[1] // 2
    thin = weight.shape[2] // 2
    for n, i, half, z, x, y in parts:
        if half == 0:
            continue
        spot = pl.ds(pl.multiple_of(place(where_ref, depth, z, x) * group, group), group)
        y_spot = lax.rem(where_ref[2] + y, 2)
        for k in range(2):
            pairs.append(
                (
                    arrays[n].at[i, pl.ds(k * group, group), pl.ds(2 * thin - thin, thin)],
                    weight.at[y_spot, spot, pl.ds(k * thin, thin)],
                )
            )
    return start_copies(pairs, sems)


def proj_kernel(depth, parts, where_ref, attended_ref, *rest):
    count = 1 + max(p[0] for p in parts)
    arrays = rest[:count]
    keep_ref, send_ref, weight, sems = rest[count:]
    piece, width = keep_ref.shape
    for copy in load_proj(where_ref, depth, parts, arrays, weight, sems):
        copy.wait()
    half = width // 2
    for y in range(2):
        columns = pl.ds(y * half, half)
        send_ref[:, columns] = dot(attended_ref[pl.ds(piece, piece), :], weight[y], NN, BF16)
    for y in range(2):
        columns = pl.ds(y * half, half)
        keep_ref[:, columns] = dot(attended_ref[pl.ds(0, piece), :], weight[y], NN)


def proj_back_kernel(depth, parts, where_ref, own_ref, other_ref, *rest):
    count = 1 + max(p[0] for p in parts)
    arrays = rest[:count]
    out_ref, weight, sems = rest[count:]
    piece, width = own_ref.shape
    for copy in load_proj(where_ref, depth, parts, arrays, weight, sems):
        copy.wait()
    half = width // 2
    for ref, begin in ((own_ref, 0), (other_ref, piece)):
        total = dot(ref[:, pl.ds(0, half)], weight[0], NT) + dot(ref[:, pl.ds(half, half)], weight[1], NT)
        out_ref[pl.ds(begin, piece), :] = total.astype(BF16)


def middle_kernel(own_ref, keep_ref, other_ref, bias_ref, gain_ref, shift_ref, middle_ref, second_ref):
    for begin in range(0, own_ref.shape[0], 128):
        rows = pl.ds(begin, 128)
        middle = own_ref[rows, :].astype(F32) + keep_ref[rows, :] + other_ref[rows, :].astype(F32) + bias_ref[...]
        middle_ref[rows, :] = middle
        hat, _ = normal(middle)
        second_ref[rows, :] = (hat * gain_ref[...] + shift_ref[...]).astype(BF16)


def load_up(where_ref, depth, parts, arrays, weight, sems):
    pairs = []
    rows, wide = arrays[0].shape[1:]
    for n, i, half, z, x, y in parts:
        spot = pl.ds(pl.multiple_of(place(where_ref, depth, z, x) * rows, rows), rows)
        y_spot = lax.rem(where_ref[2] + y, 2)
        pairs.append((arrays[n].at[i], weight.at[y_spot, spot, pl.ds(half * wide, wide)]))
    return start_copies(pairs, sems)


def up_kernel(depth, parts, where_ref, own_ref, other_ref, bias_ref, *rest):
    count = 1 + max(p[0] for p in parts)
    arrays = rest[:count]
    second_ref, active_ref, slope_ref, weight, sems = rest[count:]
    copies = load_up(where_ref, depth, parts, arrays, weight, sems)
    piece = own_ref.shape[0]
    second_ref[pl.ds(0, piece), :] = own_ref[...]
    second_ref[pl.ds(piece, piece), :] = other_ref[...]
    for copy in copies:
        copy.wait()
    wide = weight.shape[2]
    for y in range(2):
        for column in range(0, wide, 256):
            for begin in range(0, 2 * piece, piece):
                rows = pl.ds(begin, piece)
                columns = pl.ds(y * wide + column, 256)
                hidden = dot(second_ref[rows, :], weight[y, :, pl.ds(column, 256)], NN) + bias_ref[:, columns]
                gate = 0.5 + 0.5 * lax.erf(hidden * 0.7071067811865476)
                active_ref[rows, columns] = (hidden * gate).astype(BF16)
                bell = jnp.exp2(hidden * hidden * (-0.5 * LOG2E)) * 0.3989422804014327
                slope_ref[rows, columns] = (gate + hidden * bell).astype(BF16)


def hidden_kernel(depth, parts, where_ref, grad_ref, slope_ref, *rest):
    count = 1 + max(p[0] for p in parts)
    arrays = rest[:count]
    out_ref, sum_ref, weight, sems = rest[count:]
    for copy in load_up(where_ref, depth, parts, arrays, weight, sems):
        copy.wait()
    half = grad_ref.shape[1] // 2
    for column in range(0, out_ref.shape[1], 512):
        columns = pl.ds(column, 512)
        total = dot(grad_ref[:, pl.ds(0, half)], weight[0, columns, :], NT)
        total = total + dot(grad_ref[:, pl.ds(half, half)], weight[1, columns, :], NT)
        low = (total * slope_ref[:, columns].astype(F32)).astype(BF16)
        out_ref[:, columns] = low
        sum_ref[0:1, columns] = jnp.sum(low.astype(F32), axis=0, keepdims=True)


def down_kernel(depth, parts, where_ref, active_ref, *rest):
    count = 1 + max(p[0] for p in parts)
    arrays = rest[:count]
    keep_ref, send_ref, weight, sems = rest[count:]
    piece, width = keep_ref.shape
    for copy in load_up(where_ref, depth, parts, arrays, weight, sems):
        copy.wait()
    half = width // 2
    for y in range(2):
        columns = pl.ds(y * half, half)
        send_ref[:, columns] = dot(active_ref[pl.ds(piece, piece), :], weight[y], NN, BF16)
        keep_ref[:, columns] = dot(active_ref[pl.ds(0, piece), :], weight[y], NN)


def up_back_kernel(depth, parts, where_ref, grad_ref, *rest):
    count = 1 + max(p[0] for p in parts)
    arrays = rest[:count]
    keep_ref, send_ref, weight, sems = rest[count:]
    piece, width = keep_ref.shape
    for copy in load_up(where_ref, depth, parts, arrays, weight, sems):
        copy.wait()
    wide = weight.shape[2]
    for ref, begin in ((send_ref, piece), (keep_ref, 0)):
        rows = pl.ds(begin, piece)
        for column in range(0, width, 512):
            columns = pl.ds(column, 512)
            total = dot(grad_ref[rows, pl.ds(0, wide)], weight[0, columns, :], NT)
            total = total + dot(grad_ref[rows, pl.ds(wide, wide)], weight[1, columns, :], NT)
            ref[:, columns] = total.astype(ref.dtype)


def middle_back_kernel(keep_ref, other_ref, middle_ref, grad_ref, gain_ref, middle_out, branch_out, sum_out):
    totals = [jnp.zeros((1, keep_ref.shape[1]), F32) for _ in range(4)]
    for begin in range(0, keep_ref.shape[0], 128):
        rows = pl.ds(begin, 128)
        grad = keep_ref[rows, :] + other_ref[rows, :].astype(F32)
        hat, inverse = normal(middle_ref[rows, :])
        scaled = grad * gain_ref[...]
        first = jnp.mean(scaled, axis=-1, keepdims=True)
        second = jnp.mean(scaled * hat, axis=-1, keepdims=True)
        outer = grad_ref[rows, :].astype(F32)
        result = outer + inverse * (scaled - first - hat * second)
        middle_out[rows, :] = result
        low = result.astype(BF16)
        branch_out[rows, :] = low
        for n, value in enumerate((grad * hat, grad, low.astype(F32), outer)):
            totals[n] = totals[n] + jnp.sum(value, axis=0, keepdims=True)
    for n in range(4):
        sum_out[n : n + 1, :] = totals[n]


def tokens_back_kernel(keep_ref, other_ref, own_ref, grad_ref, gain_ref, out_ref, sum_out):
    totals = [jnp.zeros((1, keep_ref.shape[1]), F32) for _ in range(2)]
    for begin in range(0, keep_ref.shape[0], 128):
        rows = pl.ds(begin, 128)
        grad = keep_ref[rows, :] + other_ref[rows, :].astype(F32)
        hat, inverse = normal(own_ref[rows, :].astype(F32))
        scaled = grad * gain_ref[...]
        first = jnp.mean(scaled, axis=-1, keepdims=True)
        second = jnp.mean(scaled * hat, axis=-1, keepdims=True)
        result = grad_ref[rows, :] + inverse * (scaled - first - hat * second)
        out_ref[rows, :] = result.astype(BF16)
        for n, value in enumerate((grad * hat, grad)):
            totals[n] = totals[n] + jnp.sum(value, axis=0, keepdims=True)
    for n in range(2):
        sum_out[n : n + 1, :] = totals[n]


def load_columns(where_ref, depth, source, scratch, rows, sems):
    pairs = []
    for x in range(2):
        for z in range(depth):
            spot = pl.ds(pl.multiple_of(place(where_ref, depth, z, x) * rows, rows), rows)
            pairs.append((source.at[:, spot], scratch.at[:, pl.ds((x * depth + z) * rows, rows)]))
    return start_copies(pairs, sems)


def rows_grad_kernel(depth, rows, sent, where_ref, act_ref, grad_ref, *rest):
    outs, scratch, sems = rest[:-2], rest[-2], rest[-1]
    pairs = []
    order = [z for group in near_first(depth) for z in group]
    for n, z in enumerate(order):
        spot = pl.ds(pl.multiple_of(place(where_ref, depth, z, sent) * rows, rows), rows)
        pairs.append((act_ref.at[:, spot], scratch.at[:, pl.ds(n * rows, rows)]))
    for copy in start_copies(pairs, sems):
        copy.wait()
    part = grad_ref.shape[1] // 2
    begin = 0
    for ref in outs:
        size = ref.shape[0]
        for y_near in range(2):
            y = lax.rem(where_ref[2] + y_near, 2)
            columns = pl.ds(pl.multiple_of(y * part, 128), part)
            result = dot(scratch[:, pl.ds(begin * rows, size * rows)], grad_ref[:, columns], TN, BF16)
            for k in range(size):
                ref[k, y_near] = result[k * rows : (k + 1) * rows]
        begin += size


def rows_grad(where, act, grad, depth, rows, sent):
    length, total = act.shape
    part = grad.shape[1] // 2
    return kernel_call(
        functools.partial(rows_grad_kernel, depth, rows, sent),
        [where, act, grad],
        [SCALARS, ANYWHERE, WHOLE],
        [shape_of((len(group), 2, rows, part), BF16) for group in near_first(depth)],
        scratch=[pltpu.VMEM((length, depth * rows), BF16), pltpu.SemaphoreType.DMA((depth,))],
        flops=length * total * grad.shape[1],
    )


def columns_grad_kernel(depth, rows, sent, where_ref, act_ref, grad_ref, *rest):
    outs, scratch, sems = rest[:-2], rest[-2], rest[-1]
    pairs = []
    order = [z for group in near_first(depth) for z in group]
    for n, z in enumerate(order):
        for x in range(2):
            spot = pl.ds(pl.multiple_of(place(where_ref, depth, z, x) * rows, rows), rows)
            pairs.append((act_ref.at[:, spot], scratch.at[:, pl.ds((2 * n + x) * rows, rows)]))
    for copy in start_copies(pairs, sems):
        copy.wait()
    part = grad_ref.shape[1] // 2
    begin = 0
    half = part // 2
    y = lax.rem(where_ref[2] + sent, 2)
    for ref in outs:
        size = ref.shape[0]
        for column in range(0, part, half):
            columns = pl.ds(pl.multiple_of(y * part + column, 128), half)
            result = dot(scratch[:, pl.ds(begin * rows, 2 * size * rows)], grad_ref[:, columns], TN, BF16)
            for k in range(size):
                for x in range(2):
                    line = (2 * k + x) * rows
                    ref[k, x, :, pl.ds(column, half)] = result[line : line + rows]
        begin += 2 * size


def columns_grad(where, act, grad, depth, rows, sent):
    length, total = act.shape
    part = grad.shape[1] // 2
    return kernel_call(
        functools.partial(columns_grad_kernel, depth, rows, sent),
        [where, act, grad],
        [SCALARS, ANYWHERE, WHOLE],
        [shape_of((len(group), 2, rows, part), BF16) for group in near_first(depth)],
        scratch=[pltpu.VMEM((length, total), BF16), pltpu.SemaphoreType.DMA((2 * depth,))],
        flops=length * total * grad.shape[1],
    )


def own_half(core, mine, other):
    first = core == 0
    return jnp.where(first, mine, other), jnp.where(first, other, mine)


def split_kernel(hidden_block, core_ref, qkv_ref, up_ref, qkv_mine, qkv_other, up_mine, up_other):
    core = core_ref[0]
    rows = qkv_ref.shape[0]
    low = lax.broadcasted_iota(jnp.int32, (rows, 128), 1) < 64
    for tile in range(qkv_ref.shape[1] // 256):
        one = qkv_ref[:, pl.ds(tile * 256, 128)].astype(F32)
        two = qkv_ref[:, pl.ds(tile * 256 + 128, 128)].astype(F32)
        even = jnp.where(low, one, pltpu.roll(two, 64, 1)).astype(BF16)
        odd = jnp.where(low, pltpu.roll(one, 64, 1), two).astype(BF16)
        mine, other = own_half(core, even, odd)
        qkv_mine[:, pl.ds(tile * 128, 128)] = mine
        qkv_other[:, pl.ds(tile * 128, 128)] = other
    for tile in range(up_ref.shape[1] // (2 * hidden_block)):
        even = up_ref[:, pl.ds(tile * 2 * hidden_block, hidden_block)]
        odd = up_ref[:, pl.ds((tile * 2 + 1) * hidden_block, hidden_block)]
        mine, other = own_half(core, even, odd)
        up_mine[:, pl.ds(tile * hidden_block, hidden_block)] = mine
        up_other[:, pl.ds(tile * hidden_block, hidden_block)] = other


def pack_kernel(core_ref, mine_ref, other_ref, *rest):
    extra, out_ref = rest[:-1], rest[-1]
    rows, columns = mine_ref.shape
    half = out_ref.shape[2]
    for ref, number in ((mine_ref, core_ref[0]), (other_ref, 1 - core_ref[0])):
        lines = pl.ds(pl.multiple_of(number * rows, rows), rows)
        out_ref[0, lines, :] = ref[:, pl.ds(0, half)]
        out_ref[1, lines, pl.ds(0, columns - half)] = ref[:, pl.ds(half, columns - half)]
    for ref in extra:
        thin = ref.shape[1] // 2
        for k in range(2):
            out_ref[1, pl.ds(k * rows, rows), pl.ds(half - thin, thin)] = ref[:, pl.ds(k * thin, thin)]


def join_heads_kernel(core_ref, mine_ref, other_ref, out_ref):
    rows = mine_ref.shape[0]
    low = lax.broadcasted_iota(jnp.int32, (rows, 128), 1) < 64
    for tile in range(mine_ref.shape[1] // 128):
        columns = pl.ds(tile * 128, 128)
        even, odd = own_half(core_ref[0], mine_ref[:, columns].astype(F32), other_ref[:, columns].astype(F32))
        out_ref[:, pl.ds(tile * 256, 128)] = jnp.where(low, even, pltpu.roll(odd, 64, 1))
        out_ref[:, pl.ds(tile * 256 + 128, 128)] = jnp.where(low, pltpu.roll(even, 64, 1), odd)


def join_blocks_kernel(block, core_ref, mine_ref, other_ref, out_ref):
    for tile in range(mine_ref.shape[1] // block):
        columns = pl.ds(tile * block, block)
        even, odd = own_half(core_ref[0], mine_ref[:, columns].astype(F32), other_ref[:, columns].astype(F32))
        out_ref[:, pl.ds(2 * tile * block, block)] = even
        out_ref[:, pl.ds((2 * tile + 1) * block, block)] = odd


def proj_grad_kernel(depth, where_ref, attended_ref, own_ref, other_ref, out_ref, scratch):
    piece = own_ref.shape[0]
    group = out_ref.shape[3] // 2
    thin = out_ref.shape[4]
    for y_near in range(2):
        y = lax.rem(where_ref[2] + y_near, 2)
        columns = pl.ds(pl.multiple_of(y * 2 * thin, 128), 2 * thin)
        result = dot(attended_ref[pl.ds(0, piece), :], own_ref[:, columns], TN)
        scratch[...] = result + dot(attended_ref[pl.ds(piece, piece), :], other_ref[:, columns], TN)
        for x in range(2):
            for z in range(depth):
                spot = pl.ds(pl.multiple_of(place(where_ref, depth, z, x) * group, group), group)
                block = scratch[spot, :].astype(BF16)
                for k in range(2):
                    out_ref[x, y_near, z, pl.ds(k * group, group), :] = block[:, k * thin : (k + 1) * thin]


def mixed_grad_kernel(depth, sent, where_ref, act_ref, *rest):
    count = len(rest) - 7
    pieces, (proj_ref, one_ref, two_ref, scratch, mixed, sems, mixed_sems) = rest[:count], rest[count:]
    rows = one_ref.shape[2]
    copies = load_columns(where_ref, depth, act_ref, scratch, rows, sems)
    size = pieces[0].shape[1]
    wide = size * count // 3
    thin = wide // 2
    copies += start_copies(
        [(ref, mixed.at[:, pl.ds(n * size, size)]) for n, ref in enumerate(pieces)],
        mixed_sems,
    )
    for copy in copies:
        copy.wait()
    part = wide + thin
    half = depth * rows
    y = lax.rem(where_ref[2] + sent, 2)
    columns = pl.ds(pl.multiple_of(y * part, 128), wide)
    for x in range(2):
        result = dot(scratch[:, pl.ds(x * half, half)], mixed[:, columns], TN, BF16)
        for z in range(depth):
            one_ref[x, z] = result[z * rows : (z + 1) * rows]
    for y_near in range(2):
        y = lax.rem(where_ref[2] + y_near, 2)
        columns = pl.ds(pl.multiple_of(y * part + wide, 128), thin)
        result = dot(scratch[:, pl.ds(sent * half, half)], mixed[:, columns], TN, BF16)
        for z in range(depth):
            two_ref[y_near, z, :, pl.ds(0, thin)] = result[z * rows : (z + 1) * rows]
            two_ref[y_near, z, :, pl.ds(thin, thin)] = proj_ref[sent, y_near, z]


def mixed_back_kernel(depth, parts, count, where_ref, *rest):
    pieces, rest = rest[:count], rest[count:]
    arrays = rest[: 1 + max(p[0] for p in parts)]
    keep_ref, send_ref, weight, sems = rest[len(arrays) :]
    pairs = []
    rows = arrays[0].shape[1]
    size = pieces[0].shape[1]
    wide = size * count // 3
    thin = wide // 2
    for n, i, half, z, x, y in parts:
        spot = pl.ds(pl.multiple_of(place(where_ref, depth, z, x) * rows, rows), rows)
        y_spot = lax.rem(where_ref[2] + y, 2)
        if half == 0:
            pairs.append((arrays[n].at[i], weight.at[y_spot, spot, pl.ds(0, wide)]))
        else:
            pairs.append((arrays[n].at[i, :, pl.ds(0, thin)], weight.at[y_spot, spot, pl.ds(wide, thin)]))
    for copy in start_copies(pairs, sems):
        copy.wait()
    piece, width = keep_ref.shape
    for ref, begin in ((send_ref, piece), (keep_ref, 0)):
        lines = pl.ds(begin, piece)
        for column in range(0, width, 512):
            columns = pl.ds(column, 512)
            total = None
            for n, item in enumerate(pieces):
                y, spot = divmod(n * size, wide + thin)
                term = dot(item[lines, :], weight[y, columns, pl.ds(spot, size)], NT)
                total = term if total is None else total + term
            ref[:, columns] = total.astype(ref.dtype)


HALF = 10


def turn_tables(places, head_size, wide):
    section = 2 * (head_size // 3 // 2)
    half_size = section // 2
    lane = jnp.arange(wide) % head_size
    number = lane // section
    spot = lane % section
    frequency = 1.0 / 10000.0 ** ((spot % half_size).astype(F32) / half_size)
    place_of = jnp.where(
        number[None, :] == 0,
        places[:, 0:1],
        jnp.where(number[None, :] == 1, places[:, 1:2], places[:, 2:3]),
    )
    angles = place_of.astype(F32) * frequency[None, :]
    live = (number < 3)[None, :]
    cosine = jnp.where(live, jnp.cos(angles), 1.0)
    sine = jnp.where(live, jnp.sin(angles), 0.0)
    low = (spot < half_size)[None, :]
    return cosine, jnp.where(low, -sine, 0.0), jnp.where(low, 0.0, sine)


def ordered(index, first, second, axis=0):
    low = jnp.where(index == 0, first, second)
    high = jnp.where(index == 0, second, first)
    return jnp.stack([low, high], axis=axis)


def taken(values, index, axis):
    return lax.dynamic_index_in_dim(values, index, axis, keepdims=False)


def fast_shards(
    tokens,
    frame_index,
    row_index,
    column_index,
    norm1_gain,
    norm1_bias,
    qkv_weight,
    qkv_bias,
    proj_weight,
    proj_bias,
    norm2_gain,
    norm2_bias,
    up_weight,
    up_bias,
    down_weight,
    down_bias,
    cotangent,
):
    core = lax.axis_index("core")
    depth = lax.axis_size("z")
    where = jnp.stack([lax.axis_index("z"), lax.axis_index("x"), lax.axis_index("y")]).astype(jnp.int32)
    everyone = ("z", "x", "core", "y")
    count = 8 * depth
    piece, width = tokens.shape
    length = 2 * piece
    head_size = width // HEADS
    local = width // 2
    hidden_block = down_weight.shape[0]

    cores = jnp.stack([core]).astype(jnp.int32)
    up_rows = width // (2 * depth)
    shard_rows = qkv_weight.shape[0]
    part_qkv = 3 * local // 2
    part_up = up_weight.shape[1] // 2
    block_kind = shape_of((2, up_rows, local), BF16)

    qkv_mine, qkv_other, up_mine, up_other = kernel_call(
        functools.partial(split_kernel, hidden_block),
        [cores, qkv_weight, up_weight],
        [SCALARS, WHOLE, WHOLE],
        [shape_of((shard_rows, part_qkv), BF16)] * 2 + [shape_of((shard_rows, part_up), BF16)] * 2,
    )
    (first_block,) = kernel_call(
        pack_kernel,
        [cores, qkv_mine, swap(qkv_other, "core"), proj_weight],
        [SCALARS] + [WHOLE] * 3,
        [block_kind],
    )
    (up_block,) = kernel_call(
        pack_kernel, [cores, up_mine, swap(up_other, "core")], [SCALARS] + [WHOLE] * 2, [block_kind]
    )
    first_arrays, first_parts, hop_gate, swap_gate = gather_first(first_block, depth)
    tokens_own = lax.ppermute(tokens, ("core", "y"), DIAGONAL)
    grad_own = lax.ppermute(after(cotangent, tokens_own), ("core", "y"), DIAGONAL)
    up_arrays, up_parts, hop_gate, swap_gate = gather_middle(up_block, depth, hop_gate, swap_gate)
    down_arrays, down_parts = gather_single(down_weight, depth, "y", "x", hop_gate, swap_gate[1])

    small = jnp.concatenate(
        [norm1_gain, norm1_bias, norm2_gain, norm2_bias, proj_bias, down_bias, qkv_bias, up_bias]
    )
    small = after(small, first_block)
    used = small.shape[0]
    small = jnp.broadcast_to(
        jnp.concatenate([small.astype(F32), jnp.zeros((512 - used,), F32)]), (count, 512)
    )
    small = lax.all_to_all(small, everyone, split_axis=0, concat_axis=0, tiled=True)
    each = norm1_gain.shape[0]
    gain_one, shift_one, gain_two, shift_two, bias_proj, bias_down = [
        small[:, i * each : (i + 1) * each].reshape(1, width) for i in range(6)
    ]
    spot = 6 * each
    bias_qkv = small[:, spot : spot + qkv_bias.shape[0]].reshape(-1, 2, head_size)
    spot += qkv_bias.shape[0]
    bias_up = small[:, spot : spot + up_bias.shape[0]].reshape(-1, 2, hidden_block)
    bias_qkv = taken(bias_qkv, core, 1).reshape(1, -1)
    bias_up = taken(bias_up, core, 1).reshape(1, -1)

    places = jnp.stack([frame_index, row_index, column_index], axis=0)
    places = lax.ppermute(places, ("core", "y"), DIAGONAL)
    places = jnp.concatenate([places, swap(places, "core")], axis=1).T
    tokens_other = swap(tokens_own, "core")
    grad_full = jnp.concatenate([grad_own, swap(grad_own, "core")])
    turn = turn_tables(places, head_size, 2 * head_size)

    part_count = len(first_parts)
    dma = pltpu.SemaphoreType.DMA
    normed, queries, keys, values = kernel_call(
        functools.partial(qkv_kernel, depth, first_parts),
        [where, tokens_own, tokens_other, gain_one, shift_one, bias_qkv, *turn, *first_arrays],
        [SCALARS] + [WHOLE] * 8 + [ANYWHERE] * len(first_arrays),
        [shape_of((length, width), BF16)] + [shape_of((length, local), BF16)] * 3,
        scratch=[pltpu.VMEM((2, width, 3 * local // 2), BF16), dma((part_count,))],
        flops=2 * length * width * 3 * local,
    )
    attended, logs = attend(queries, keys, values, head_size)
    proj_scratch = [pltpu.VMEM((2, local, width // 2), BF16), dma((part_count,))]
    partial = [shape_of((piece, width), F32), shape_of((piece, width), BF16)]
    kept, sent = kernel_call(
        functools.partial(proj_kernel, depth, first_parts),
        [where, attended, *first_arrays],
        [SCALARS, WHOLE] + [ANYWHERE] * len(first_arrays),
        partial,
        scratch=proj_scratch,
        flops=2 * length * width * local,
    )
    middle, second_own = kernel_call(
        middle_kernel,
        [tokens_own, kept, swap(sent, "core"), bias_proj, gain_two, shift_two],
        [WHOLE] * 6,
        partial,
    )
    hidden_size = bias_up.shape[1]
    up_scratch = [pltpu.VMEM((2, width, hidden_size // 2), BF16), dma((len(up_parts),))]
    second, active, slope = kernel_call(
        functools.partial(up_kernel, depth, up_parts),
        [where, second_own, swap(second_own, "core"), bias_up, *up_arrays],
        [SCALARS] + [WHOLE] * 3 + [ANYWHERE] * len(up_arrays),
        [shape_of((length, width), BF16)] + [shape_of((length, hidden_size), BF16)] * 2,
        scratch=up_scratch,
        flops=2 * length * width * hidden_size,
        exps=length * hidden_size,
    )
    sends = rows_grad(where, active, grad_full, depth, hidden_block, 1)
    down_sum = Scatter(sends, "x", "y", depth)
    down_scratch = [pltpu.VMEM((2, hidden_size, width // 2), BF16), dma((len(down_parts),))]
    hidden_grad, up_sums = kernel_call(
        functools.partial(hidden_kernel, depth, down_parts),
        [where, grad_full, after(slope, *sends), *down_arrays],
        [SCALARS] + [WHOLE] * 2 + [ANYWHERE] * len(down_arrays),
        [shape_of((length, hidden_size), BF16), shape_of((8, hidden_size), F32)],
        scratch=down_scratch,
        flops=2 * length * width * hidden_size,
    )
    sends = columns_grad(where, second, hidden_grad, depth, up_rows, 1)
    up_sum = Scatter(sends, "y", "x", depth)
    down_sum.keeps = rows_grad(where, after(active, *sends), grad_full, depth, hidden_block, 0)
    kept, sent = kernel_call(
        functools.partial(up_back_kernel, depth, up_parts),
        [where, after(hidden_grad, *down_sum.keeps), *up_arrays],
        [SCALARS, WHOLE] + [ANYWHERE] * len(up_arrays),
        partial,
        scratch=up_scratch,
        flops=2 * length * width * hidden_size,
    )
    up_sum.keeps = columns_grad(where, after(second, sent), hidden_grad, depth, up_rows, 0)
    gate = down_sum.hop(0, up_sum.keeps[0])
    middle_grad, branch_own, middle_sums = kernel_call(
        middle_back_kernel,
        [after(kept, gate), swap(sent, "core"), middle, grad_own, gain_two],
        [WHOLE] * 5,
        partial + [shape_of((8, width), F32)],
    )
    branch_other = swap(branch_own, "core")
    (attended_grad,) = kernel_call(
        functools.partial(proj_back_kernel, depth, first_parts),
        [where, branch_own, branch_other, *first_arrays],
        [SCALARS] + [WHOLE] * 2 + [ANYWHERE] * len(first_arrays),
        [shape_of((length, local), BF16)],
        scratch=proj_scratch,
        flops=2 * length * width * local,
    )
    (proj_blocks,) = kernel_call(
        functools.partial(proj_grad_kernel, depth),
        [where, attended, after(branch_own, attended_grad), branch_other],
        [SCALARS] + [WHOLE] * 3,
        [shape_of((2, 2, depth, up_rows, width // 4), BF16)],
        scratch=[pltpu.VMEM((local, width // 2), F32)],
        flops=2 * length * width * local,
    )
    pairs = local // (2 * head_size)
    gate = down_sum.hop(1, proj_blocks)
    first_grads = attend_back(
        queries, keys, values, after(attended_grad, gate), logs, turn, head_size, 0, pairs // 2
    )
    gate = (down_sum.hop(2, first_grads[0]), up_sum.hop(0, first_grads[0]))
    second_grads = attend_back(
        queries, keys, values, after(attended_grad, *gate), logs, turn, head_size, pairs // 2, pairs
    )
    mixed_pieces = [group[n] for n in range(3) for group in (first_grads, second_grads)]
    mixed_sums = jnp.concatenate([first_grads[3][:3], second_grads[3][:3]], axis=1)

    def mixed_weight_grad(sent_number, gate):
        block = (2, depth, up_rows, local)
        return kernel_call(
            functools.partial(mixed_grad_kernel, depth, sent_number),
            [where, after(normed, gate), *mixed_pieces, proj_blocks],
            [SCALARS] + [ANYWHERE] * (1 + len(mixed_pieces)) + [WHOLE],
            [shape_of(block, BF16)] * 2,
            scratch=[
                pltpu.VMEM((length, width), BF16),
                pltpu.VMEM((length, 3 * local), BF16),
                dma((2 * depth,)),
                dma((len(mixed_pieces),)),
            ],
            flops=length * width * 3 * local,
        )

    one_send, two_send = mixed_weight_grad(1, second_grads[0])
    one_near = swap(one_send, "y")
    two_near = swap(two_send, "x")
    gate = (up_sum.hop(1, two_send), down_sum.finish(two_send))
    kept, sent = kernel_call(
        functools.partial(mixed_back_kernel, depth, first_parts, len(mixed_pieces)),
        [where, after(mixed_pieces[0], *gate), *mixed_pieces[1:], *first_arrays],
        [SCALARS] + [WHOLE] * len(mixed_pieces) + [ANYWHERE] * len(first_arrays),
        partial,
        scratch=[pltpu.VMEM((2, width, 3 * local // 2), BF16), dma((part_count,))],
        flops=2 * length * width * 3 * local,
    )
    sent_other = swap(sent, "core")
    one_keep, two_keep = mixed_weight_grad(0, sent)
    gate = up_sum.hop(2, two_keep)
    tokens_grad, first_sums = kernel_call(
        tokens_back_kernel,
        [after(kept, gate), sent_other, tokens_own, middle_grad, gain_one],
        [WHOLE] * 5,
        [shape_of((piece, width), BF16), shape_of((8, width), F32)],
    )
    one_far = add_low(after(one_keep[1], tokens_grad), one_near[1])
    two_far = add_low(after(two_keep[1], tokens_grad), two_near[1])
    one_last = swap(one_far, "x")
    two_last = swap(two_far, "y")
    kept, sent = kernel_call(
        functools.partial(down_kernel, depth, down_parts),
        [where, after(active, one_far, two_far), *down_arrays],
        [SCALARS, WHOLE] + [ANYWHERE] * len(down_arrays),
        partial,
        scratch=down_scratch,
        flops=2 * length * width * hidden_size,
    )
    up_sum.finish(sent)
    block_out = (middle + (kept + swap(sent, "core").astype(F32)) + bias_down).astype(BF16)
    block_out = lax.ppermute(block_out, ("core", "y"), DIAGONAL)
    tokens_grad = lax.ppermute(tokens_grad, ("core", "y"), DIAGONAL)
    one = add_low(one_keep[0], one_near[0], one_last)
    two = add_low(two_keep[0], two_near[0], two_last)
    both = jnp.stack([one, two], axis=1)
    moving = both[1 % depth]
    for step in range(1, depth):
        moving = add_low(both[(step + 1) % depth], ring(moving, depth))
    grad_first = moving
    grad_down = down_sum.result()
    grad_up = up_sum.result()

    def spread(vector, group):
        parts = vector.reshape(-1, 1, group)
        pair = jnp.arange(2).reshape(1, 2, 1) == core
        return jnp.where(pair, parts, 0.0).reshape(-1)

    vectors = [
        first_sums[0],
        first_sums[1],
        middle_sums[0],
        middle_sums[1],
        middle_sums[2],
        middle_sums[3],
        spread(mixed_sums[:3].reshape(-1), head_size),
        spread(up_sums[0], hidden_block),
    ]
    packed = jnp.concatenate([v.reshape(count, -1) for v in vectors], axis=1)
    packed = jnp.pad(packed, ((0, 0), (0, 512 - packed.shape[1])))
    packed = lax.all_to_all(packed, everyone, split_axis=0, concat_axis=0, tiled=True)
    packed = jnp.sum(packed, axis=0)
    pieces = []
    spot = 0
    for v in vectors:
        size = v.shape[0] // count
        pieces.append(packed[spot : spot + size])
        spot += size

    def joined(body, block):
        rows = block.shape[0] // 2
        pair = block.reshape(2, rows, -1)
        (whole,) = kernel_call(
            body,
            [cores, taken(pair, core, 0), swap(taken(pair, 1 - core, 0), "core")],
            [SCALARS, WHOLE, WHOLE],
            [shape_of((rows, 2 * block.shape[1]), F32)],
        )
        return whole

    grad_proj = grad_first[1][:, part_qkv - local :].astype(F32)
    group = grad_proj.shape[0] // 2
    grad_proj = jnp.concatenate([grad_proj[:group], grad_proj[group:]], axis=1)
    grad_qkv = jnp.concatenate([grad_first[0], grad_first[1][:, : part_qkv - local]], axis=1)
    grad_qkv = joined(join_heads_kernel, grad_qkv)
    grad_up = joined(functools.partial(join_blocks_kernel, hidden_block), grad_up)
    return (
        block_out,
        tokens_grad,
        pieces[0],
        pieces[1],
        grad_qkv,
        pieces[6],
        grad_proj,
        pieces[4],
        pieces[2],
        pieces[3],
        grad_up,
        pieces[7],
        grad_down.astype(F32),
        pieces[5],
    )


def solution(mesh):
    ctx_count = mesh.shape["ctx"]
    dp_count = mesh.shape["dp"]
    if ctx_count == 2 and dp_count % 4 == 0:
        mesh = Mesh(
            mesh.devices.reshape(dp_count // 4, 2, 2, 2), ("z", "x", "core", "y")
        )
        dp = ("z", "x", "core")
        ctx = "y"
        every = P(dp + (ctx,))
        body = fast_shards
    else:
        dp = "dp"
        ctx = "ctx"
        every = P((dp, ctx))
        body = shards
    rows = P(every[0], None)
    matrix = P(dp, ctx)
    return jax.shard_map(
        body,
        mesh=mesh,
        in_specs=(
            rows,
            every,
            every,
            every,
            every,
            every,
            matrix,
            every,
            matrix,
            every,
            every,
            every,
            matrix,
            every,
            matrix,
            every,
            rows,
        ),
        out_specs=(
            rows,
            rows,
            every,
            every,
            matrix,
            every,
            matrix,
            every,
            every,
            every,
            matrix,
            every,
            matrix,
            every,
        ),
        check_vma=False,
    )
```

```python
import functools
import math

import jax
import jax.numpy as jnp
from jax import lax
from jax.experimental import pallas as pl
from jax.experimental.pallas import tpu as pltpu
from jax.sharding import Mesh
from jax.sharding import PartitionSpec as P

HEADS = 16
SPAN = 256
LEAST_LEN = 1024


EPS = 1e-06


def norm_rows(values, gain_row, shift_row):
    row_mean = jnp.mean(values, axis=-1, keepdims=True)
    centred = values - row_mean
    variance = jnp.mean(centred * centred, axis=-1, keepdims=True)
    return centred * lax.rsqrt(variance + EPS) * gain_row + shift_row


def tables(frames, patch_rows, patch_columns, head_size):
    section = 2 * (head_size // 3 // 2)
    half_size = section // 2
    frequency = 1.0 / 10000.0 ** (jnp.arange(half_size).astype(jnp.float32) / half_size)
    cosines = []
    sines = []
    for place in (frames, patch_rows, patch_columns):
        angles = place.astype(jnp.float32)[..., None] * frequency
        cosines = cosines + [jnp.cos(angles), jnp.cos(angles)]
        sines = sines + [jnp.sin(angles), jnp.sin(angles)]
    spare = head_size - 3 * section
    cosines.append(jnp.ones(frames.shape + (spare,), jnp.float32))
    sines.append(jnp.zeros(frames.shape + (spare,), jnp.float32))
    return (jnp.concatenate(cosines, axis=-1), jnp.concatenate(sines, axis=-1))


def turn_half(values):
    head_size = values.shape[-1]
    section = 2 * (head_size // 3 // 2)
    half_size = section // 2
    pieces = []
    for part_number in range(3):
        begin = part_number * section
        pieces.append(-values[..., begin + half_size : begin + section])
        pieces.append(values[..., begin : begin + half_size])
    pieces.append(jnp.zeros_like(values[..., 3 * section :]))
    return jnp.concatenate(pieces, axis=-1)


def rotary(values, cosine_table, sine_table):
    return values * cosine_table + turn_half(values) * sine_table


def rotary_back(values, cosine_table, sine_table):
    return values * cosine_table - turn_half(values * sine_table)


def shards(
    tokens,
    frame_index,
    row_index,
    column_index,
    norm1_gain,
    norm1_bias,
    qkv_weight,
    qkv_bias,
    proj_weight,
    proj_bias,
    norm2_gain,
    norm2_bias,
    up_weight,
    up_bias,
    down_weight,
    down_bias,
    cotangent,
):
    ctx_count = lax.axis_size("ctx")
    clip_length = max(LEAST_LEN, SPAN * ctx_count)
    piece_rows = clip_length // ctx_count
    rows_here, model_width = tokens.shape
    clip_count = rows_here // piece_rows
    head_size = model_width // HEADS
    score_scale = head_size ** (-0.5)
    head_shape = (clip_count, piece_rows, HEADS, head_size)
    long_shape = (clip_count, clip_length, HEADS, head_size)
    flat_shape = (clip_count, piece_rows, model_width)

    def gather_all():
        partial_value = (
            lax.all_gather(qkv_weight, "ctx", axis=1, tiled=True),
            lax.all_gather(proj_weight, "ctx", axis=1, tiled=True),
            lax.all_gather(up_weight, "ctx", axis=1, tiled=True),
            lax.all_gather(down_weight, "ctx", axis=1, tiled=True),
            lax.all_gather(norm1_gain, "ctx", axis=0, tiled=True),
            lax.all_gather(norm1_bias, "ctx", axis=0, tiled=True),
            lax.all_gather(qkv_bias, "ctx", axis=0, tiled=True),
            lax.all_gather(proj_bias, "ctx", axis=0, tiled=True),
            lax.all_gather(norm2_gain, "ctx", axis=0, tiled=True),
            lax.all_gather(norm2_bias, "ctx", axis=0, tiled=True),
            lax.all_gather(up_bias, "ctx", axis=0, tiled=True),
            lax.all_gather(down_bias, "ctx", axis=0, tiled=True),
        )
        return (
            lax.all_gather(partial_value[0], "dp", axis=0, tiled=True),
            lax.all_gather(partial_value[1], "dp", axis=0, tiled=True),
            lax.all_gather(partial_value[2], "dp", axis=0, tiled=True),
            lax.all_gather(partial_value[3], "dp", axis=0, tiled=True),
            lax.all_gather(partial_value[4], "dp", axis=0, tiled=True),
            lax.all_gather(partial_value[5], "dp", axis=0, tiled=True),
            lax.all_gather(partial_value[6], "dp", axis=0, tiled=True),
            lax.all_gather(partial_value[7], "dp", axis=0, tiled=True),
            lax.all_gather(partial_value[8], "dp", axis=0, tiled=True),
            lax.all_gather(partial_value[9], "dp", axis=0, tiled=True),
            lax.all_gather(partial_value[10], "dp", axis=0, tiled=True),
            lax.all_gather(partial_value[11], "dp", axis=0, tiled=True),
        )

    gathered = gather_all()
    (
        w_qkv,
        w_proj,
        w_up,
        w_down,
        gain_one,
        shift_one,
        bias_qkv,
        bias_proj,
        gain_two,
        shift_two,
        bias_up,
        bias_down,
    ) = gathered
    block_in = tokens.astype(jnp.float32).reshape(flat_shape)
    cosine_table, sine_table = tables(
        frame_index.reshape(clip_count, piece_rows),
        row_index.reshape(clip_count, piece_rows),
        column_index.reshape(clip_count, piece_rows),
        head_size,
    )
    cosine_table = cosine_table[:, :, None, :]
    sine_table = sine_table[:, :, None, :]
    normed = norm_rows(
        block_in, gain_one.astype(jnp.float32), shift_one.astype(jnp.float32)
    ).astype(jnp.bfloat16)
    projected = jnp.einsum(
        "spd,de->spe", normed, w_qkv, preferred_element_type=jnp.float32
    ) + bias_qkv.astype(jnp.float32)
    queries = rotary(
        projected[..., :model_width].reshape(head_shape), cosine_table, sine_table
    ).astype(jnp.bfloat16)
    keys_own = (
        rotary(
            projected[..., model_width : 2 * model_width].reshape(head_shape),
            cosine_table,
            sine_table,
        )
        .astype(jnp.bfloat16)
        .reshape(flat_shape)
    )
    values_own = projected[..., 2 * model_width :].astype(jnp.bfloat16)
    keys_all, values_all = (
        lax.all_gather(keys_own, "ctx", axis=1, tiled=True),
        lax.all_gather(values_own, "ctx", axis=1, tiled=True),
    )
    keys_all = keys_all.reshape(long_shape)
    values_all = values_all.reshape(long_shape)

    def head_forward(head_number):
        query_head = lax.dynamic_index_in_dim(queries, head_number, 2, keepdims=False)
        key_head = lax.dynamic_index_in_dim(keys_all, head_number, 2, keepdims=False)
        value_head = lax.dynamic_index_in_dim(values_all, head_number, 2, keepdims=False)
        scores = (
            jnp.einsum("sqd,skd->sqk", query_head, key_head, preferred_element_type=jnp.float32)
            * score_scale
        )
        row_top = jnp.max(scores, axis=-1, keepdims=True)
        weights = jnp.exp(scores - row_top)
        row_total = jnp.sum(weights, axis=-1, keepdims=True)
        weights_low = (weights / row_total).astype(jnp.bfloat16)
        result = jnp.einsum(
            "sqk,skd->sqd", weights_low, value_head, preferred_element_type=jnp.float32
        )
        return (result, (row_top + jnp.log(row_total))[..., 0])

    head_numbers = jnp.arange(HEADS, dtype=jnp.int32)
    attended, log_total = lax.map(head_forward, head_numbers)
    attended_low = jnp.transpose(attended, (1, 2, 0, 3)).reshape(flat_shape).astype(jnp.bfloat16)
    branch = jnp.einsum(
        "spd,de->spe", attended_low, w_proj, preferred_element_type=jnp.float32
    ) + bias_proj.astype(jnp.float32)
    middle = block_in + branch
    second = norm_rows(middle, gain_two.astype(jnp.float32), shift_two.astype(jnp.float32)).astype(
        jnp.bfloat16
    )
    hidden = jnp.einsum(
        "spd,df->spf", second, w_up, preferred_element_type=jnp.float32
    ) + bias_up.astype(jnp.float32)
    active = jax.nn.gelu(hidden, approximate=False).astype(jnp.bfloat16)
    output = jnp.einsum(
        "spf,fd->spd", active, w_down, preferred_element_type=jnp.float32
    ) + bias_down.astype(jnp.float32)
    block_out = (middle + output).astype(jnp.bfloat16).reshape(rows_here, model_width)
    backward_weights = gather_all()
    (
        w_qkv,
        w_proj,
        w_up,
        w_down,
        gain_one,
        shift_one,
        bias_qkv,
        bias_proj,
        gain_two,
        shift_two,
        bias_up,
        bias_down,
    ) = backward_weights
    out_low = cotangent.reshape(flat_shape)
    out_grad = out_low.astype(jnp.float32)
    grad_down_bias = jnp.sum(out_grad, axis=(0, 1))
    grad_down = jnp.einsum("spf,spd->fd", active, out_low, preferred_element_type=jnp.float32)
    active_grad = jnp.einsum("spd,fd->spf", out_low, w_down, preferred_element_type=jnp.float32)
    gelu_pull = jax.vjp(lambda inner: jax.nn.gelu(inner, approximate=False), hidden)[1]
    hidden_grad = gelu_pull(active_grad)[0].astype(jnp.bfloat16)
    grad_up_bias = jnp.sum(hidden_grad.astype(jnp.float32), axis=(0, 1))
    grad_up = jnp.einsum("spd,spf->df", second, hidden_grad, preferred_element_type=jnp.float32)
    second_grad = jnp.einsum("spf,df->spd", hidden_grad, w_up, preferred_element_type=jnp.float32)
    second_pull = jax.vjp(
        norm_rows, middle, gain_two.astype(jnp.float32), shift_two.astype(jnp.float32)
    )[1]
    middle_part, grad_gain_two, grad_shift_two = second_pull(second_grad)
    middle_grad = out_grad + middle_part
    branch_low = middle_grad.astype(jnp.bfloat16)
    grad_proj_bias = jnp.sum(branch_low.astype(jnp.float32), axis=(0, 1))
    grad_proj = jnp.einsum(
        "spd,spe->de", attended_low, branch_low, preferred_element_type=jnp.float32
    )
    attended_grad = (
        jnp.einsum("spe,de->spd", branch_low, w_proj, preferred_element_type=jnp.float32)
        .astype(jnp.bfloat16)
        .reshape(head_shape)
    )

    def head_backward(head_number):
        query_head = lax.dynamic_index_in_dim(queries, head_number, 2, keepdims=False)
        key_head = lax.dynamic_index_in_dim(keys_all, head_number, 2, keepdims=False)
        value_head = lax.dynamic_index_in_dim(values_all, head_number, 2, keepdims=False)
        grad_head = lax.dynamic_index_in_dim(attended_grad, head_number, 2, keepdims=False)
        log_head = lax.dynamic_index_in_dim(log_total, head_number, 0, keepdims=False)
        scores = (
            jnp.einsum("sqd,skd->sqk", query_head, key_head, preferred_element_type=jnp.float32)
            * score_scale
        )
        weights = jnp.exp(scores - log_head[..., None])
        weights_low = weights.astype(jnp.bfloat16)
        value_grad = jnp.einsum(
            "sqk,sqd->skd", weights_low, grad_head, preferred_element_type=jnp.float32
        )
        weight_grad = jnp.einsum(
            "sqd,skd->sqk", grad_head, value_head, preferred_element_type=jnp.float32
        )
        score_grad = (
            weights * (weight_grad - jnp.sum(weights * weight_grad, axis=-1, keepdims=True))
        ).astype(jnp.bfloat16)
        query_grad = (
            jnp.einsum("sqk,skd->sqd", score_grad, key_head, preferred_element_type=jnp.float32)
            * score_scale
        )
        key_grad = (
            jnp.einsum("sqk,sqd->skd", score_grad, query_head, preferred_element_type=jnp.float32)
            * score_scale
        )
        return (query_grad, key_grad, value_grad)

    query_grads, key_grads, value_grads = lax.map(head_backward, head_numbers)
    key_full = jnp.transpose(key_grads, (1, 2, 0, 3)).reshape(clip_count, clip_length, model_width)
    value_full = jnp.transpose(value_grads, (1, 2, 0, 3)).reshape(
        clip_count, clip_length, model_width
    )
    key_part, value_part = (
        lax.psum_scatter(
            key_full.astype(jnp.bfloat16), "ctx", scatter_dimension=1, tiled=True
        ).astype(jnp.float32),
        lax.psum_scatter(
            value_full.astype(jnp.bfloat16), "ctx", scatter_dimension=1, tiled=True
        ).astype(jnp.float32),
    )
    query_grads = jnp.transpose(query_grads, (1, 2, 0, 3))
    query_back = rotary_back(query_grads, cosine_table, sine_table).reshape(flat_shape)
    key_back = rotary_back(key_part.reshape(head_shape), cosine_table, sine_table).reshape(
        flat_shape
    )
    mixed_grad = jnp.concatenate([query_back, key_back, value_part], axis=-1).astype(jnp.bfloat16)
    grad_qkv_bias = jnp.sum(mixed_grad.astype(jnp.float32), axis=(0, 1))
    grad_qkv = jnp.einsum("spd,spe->de", normed, mixed_grad, preferred_element_type=jnp.float32)
    normed_grad = jnp.einsum("spe,de->spd", mixed_grad, w_qkv, preferred_element_type=jnp.float32)
    first_pull = jax.vjp(
        norm_rows, block_in, gain_one.astype(jnp.float32), shift_one.astype(jnp.float32)
    )[1]
    input_part, grad_gain_one, grad_shift_one = first_pull(normed_grad)
    tokens_grad = (middle_grad + input_part).astype(jnp.bfloat16).reshape(rows_here, model_width)
    summed = (
        lax.psum_scatter(
            grad_qkv.astype(jnp.bfloat16), "dp", scatter_dimension=0, tiled=True
        ).astype(jnp.float32),
        lax.psum_scatter(
            grad_proj.astype(jnp.bfloat16), "dp", scatter_dimension=0, tiled=True
        ).astype(jnp.float32),
        lax.psum_scatter(
            grad_up.astype(jnp.bfloat16), "dp", scatter_dimension=0, tiled=True
        ).astype(jnp.float32),
        lax.psum_scatter(
            grad_down.astype(jnp.bfloat16), "dp", scatter_dimension=0, tiled=True
        ).astype(jnp.float32),
        lax.psum_scatter(
            grad_gain_one.astype(jnp.bfloat16), "dp", scatter_dimension=0, tiled=True
        ).astype(jnp.float32),
        lax.psum_scatter(
            grad_shift_one.astype(jnp.bfloat16), "dp", scatter_dimension=0, tiled=True
        ).astype(jnp.float32),
        lax.psum_scatter(
            grad_qkv_bias.astype(jnp.bfloat16), "dp", scatter_dimension=0, tiled=True
        ).astype(jnp.float32),
        lax.psum_scatter(
            grad_proj_bias.astype(jnp.bfloat16), "dp", scatter_dimension=0, tiled=True
        ).astype(jnp.float32),
        lax.psum_scatter(
            grad_gain_two.astype(jnp.bfloat16), "dp", scatter_dimension=0, tiled=True
        ).astype(jnp.float32),
        lax.psum_scatter(
            grad_shift_two.astype(jnp.bfloat16), "dp", scatter_dimension=0, tiled=True
        ).astype(jnp.float32),
        lax.psum_scatter(
            grad_up_bias.astype(jnp.bfloat16), "dp", scatter_dimension=0, tiled=True
        ).astype(jnp.float32),
        lax.psum_scatter(
            grad_down_bias.astype(jnp.bfloat16), "dp", scatter_dimension=0, tiled=True
        ).astype(jnp.float32),
    )
    owned = (
        lax.psum_scatter(
            summed[0].astype(jnp.bfloat16), "ctx", scatter_dimension=1, tiled=True
        ).astype(jnp.float32),
        lax.psum_scatter(
            summed[1].astype(jnp.bfloat16), "ctx", scatter_dimension=1, tiled=True
        ).astype(jnp.float32),
        lax.psum_scatter(
            summed[2].astype(jnp.bfloat16), "ctx", scatter_dimension=1, tiled=True
        ).astype(jnp.float32),
        lax.psum_scatter(
            summed[3].astype(jnp.bfloat16), "ctx", scatter_dimension=1, tiled=True
        ).astype(jnp.float32),
        lax.psum_scatter(
            summed[4].astype(jnp.bfloat16), "ctx", scatter_dimension=0, tiled=True
        ).astype(jnp.float32),
        lax.psum_scatter(
            summed[5].astype(jnp.bfloat16), "ctx", scatter_dimension=0, tiled=True
        ).astype(jnp.float32),
        lax.psum_scatter(
            summed[6].astype(jnp.bfloat16), "ctx", scatter_dimension=0, tiled=True
        ).astype(jnp.float32),
        lax.psum_scatter(
            summed[7].astype(jnp.bfloat16), "ctx", scatter_dimension=0, tiled=True
        ).astype(jnp.float32),
        lax.psum_scatter(
            summed[8].astype(jnp.bfloat16), "ctx", scatter_dimension=0, tiled=True
        ).astype(jnp.float32),
        lax.psum_scatter(
            summed[9].astype(jnp.bfloat16), "ctx", scatter_dimension=0, tiled=True
        ).astype(jnp.float32),
        lax.psum_scatter(
            summed[10].astype(jnp.bfloat16), "ctx", scatter_dimension=0, tiled=True
        ).astype(jnp.float32),
        lax.psum_scatter(
            summed[11].astype(jnp.bfloat16), "ctx", scatter_dimension=0, tiled=True
        ).astype(jnp.float32),
    )
    return (
        block_out,
        tokens_grad,
        owned[4],
        owned[5],
        owned[0],
        owned[6],
        owned[1],
        owned[7],
        owned[8],
        owned[9],
        owned[2],
        owned[10],
        owned[3],
        owned[11],
    )


LOG2E = 1.4426950408889634
COST = 0.001
NT = (((1,), (1,)), ((), ()))
NN = (((1,), (0,)), ((), ()))
TN = (((0,), (0,)), ((), ()))
F32 = jnp.float32
BF16 = jnp.bfloat16
SWAP = [(0, 1), (1, 0)]
DIAGONAL = [(1, 2), (2, 1)]
ANYWHERE = pl.BlockSpec(memory_space=pl.ANY)
WHOLE = pl.BlockSpec(memory_space=pltpu.VMEM)
SHARES = 1
LINES = 128
SCALARS = pl.BlockSpec(memory_space=pltpu.SMEM)


def shape_of(shape, kind):
    return jax.ShapeDtypeStruct(shape, kind)


def half_lanes(number, shape):
    lane = lax.broadcasted_iota(jnp.int32, shape, 1)
    width = shape[1] // 2
    return (lane < width) if number == 0 else (lane >= width)


def keep(mask, values):
    return jnp.where(mask, values, jnp.zeros_like(values))


def dot(first, second, dims, to=F32):
    return lax.dot_general(first, second, dims, preferred_element_type=F32).astype(to)


def kernel_call(
    body, inputs, in_specs, out_shapes, scratch=(), grid=None, out_specs=None, flops=0, exps=0, room=8
):
    def size(item):
        return item.size * item.dtype.itemsize

    total = sum(size(a) for a in inputs) + sum(size(s) for s in out_shapes)
    if out_specs is None:
        out_specs = [WHOLE] * len(out_shapes)
    need = room << 20
    if grid is None:
        need += sum(size(a) for a, spec in zip(inputs, in_specs) if spec is WHOLE)
        need += sum(size(a) for a, spec in zip(out_shapes, out_specs) if spec is WHOLE)
    for item in scratch:
        if getattr(item, "memory_space", None) == pltpu.VMEM:
            need += math.prod(item.shape) * jnp.dtype(item.dtype).itemsize
    extra = {} if grid is None else {"grid": grid}
    return pl.pallas_call(
        body,
        in_specs=in_specs,
        out_specs=out_specs,
        out_shape=out_shapes,
        scratch_shapes=list(scratch),
        compiler_params=pltpu.CompilerParams(vmem_limit_bytes=min(need, 56 << 20)),
        cost_estimate=pl.CostEstimate(
            flops=int(flops * COST),
            bytes_accessed=int(total * COST),
            transcendentals=int(exps * COST),
        ),
        **extra,
    )(*inputs)


def merged_call(*steps, room=8):
    counts = [(len(a), len(o), len(c)) for _, a, _, o, c in steps]
    inputs = sum(c[0] for c in counts)
    outs = sum(c[1] for c in counts)

    def body(*refs):
        i, o, c = 0, inputs, inputs + outs
        for (step_body, *_), (ni, no, nc) in zip(steps, counts):
            step_body(*refs[i : i + ni], *refs[o : o + no], *refs[c : c + nc])
            i, o, c = i + ni, o + no, c + nc

    found = kernel_call(
        body,
        [a for step in steps for a in step[1]],
        [a for step in steps for a in step[2]],
        [a for step in steps for a in step[3]],
        scratch=[a for step in steps for a in step[4]],
        room=room,
    )
    results = []
    for _, no, _ in counts:
        results.append(found[:no])
        found = found[no:]
    return results


def after(values, *others):
    return lax.optimization_barrier((values,) + others)[0]


def swap(values, axis):
    return lax.ppermute(values, axis, SWAP)


def swap_each(pieces):
    return [swap(piece, "core") for piece in pieces]


def put_rows(refs, columns, value):
    rows = refs[0].shape[0]
    for k, ref in enumerate(refs):
        ref[:, columns] = value[k * rows : (k + 1) * rows].astype(ref.dtype)


def ring(values, depth):
    return lax.ppermute(values, "z", [(i, (i + 1) % depth) for i in range(depth)])


def place(depth, z, x):
    z_number = lax.rem(lax.axis_index("z") + (depth - z), depth)
    return 2 * z_number + lax.rem(lax.axis_index("x") + x, 2)


def y_place(y):
    return lax.rem(lax.axis_index("y") + y, 2)


def start_copies(pairs, sems):
    copies = [pltpu.make_async_copy(a, b, sems.at[n]) for n, (a, b) in enumerate(pairs)]
    for copy in copies:
        copy.start()
    return copies


def join_kernel(spans, *refs):
    out_ref, sems = refs[-2:]
    pairs = []
    spot = 0
    for n, begin, count in spans:
        pairs.append((refs[n].at[pl.ds(begin, count)], out_ref.at[pl.ds(spot, count)]))
        spot += count
    for copy in start_copies(pairs, sems):
        copy.wait()


def join(arrays, spans):
    total = sum(span[2] for span in spans)
    (out,) = kernel_call(
        functools.partial(join_kernel, spans),
        arrays,
        [ANYWHERE] * len(arrays),
        [shape_of((total,) + arrays[0].shape[1:], arrays[0].dtype)],
        out_specs=[ANYWHERE],
        scratch=[pltpu.SemaphoreType.DMA((len(spans),))],
    )
    return out


def choose_kernel(own_ref, other_ref, out_ref, sem):
    stays = lax.axis_index("core") == lax.axis_index("y")

    @pl.when(stays)
    def _():
        copy = pltpu.make_async_copy(own_ref, out_ref, sem)
        copy.start()
        copy.wait()

    @pl.when(jnp.logical_not(stays))
    def _():
        copy = pltpu.make_async_copy(other_ref, out_ref, sem)
        copy.start()
        copy.wait()


def trade(values):
    return lax.ppermute(values, ("core", "y"), DIAGONAL)


def choose(own, other):
    (out,) = kernel_call(
        choose_kernel,
        [own, other],
        [ANYWHERE] * 2,
        [shape_of(own.shape, own.dtype)],
        scratch=[pltpu.SemaphoreType.DMA],
    )
    return out


def add_kernel(*refs):
    total = None
    for ref in refs[:-1]:
        value = ref[(0,) * (len(ref.shape) - 2)].astype(F32)
        total = value if total is None else total + value
    refs[-1][0] = total.astype(refs[-1].dtype)


def add_blocks(terms, kind=BF16):
    array, prefix = terms[0]
    number, rows, columns = array.shape[len(prefix) :]

    def spec(prefix):
        return pl.BlockSpec((1,) * len(prefix) + (1, rows, columns), lambda i: prefix + (i, 0, 0))

    (out,) = kernel_call(
        add_kernel,
        [array for array, _ in terms],
        [spec(tuple(prefix)) for _, prefix in terms],
        [shape_of((number, rows, columns), kind)],
        grid=(number,),
        out_specs=[spec(())],
    )
    return out


def near_first(depth):
    order = [i % depth for i in range(1, depth + 1)]
    split = max(depth // 2, 1)
    return order[:split], order[split:]


class Scatter:
    def __init__(self, sends, first, last, depth):
        self.sends = sends
        self.arrived = []
        self.first = first
        self.last = last
        self.depth = depth
        self.spots = [(g, k) for g, group in enumerate(near_first(depth)) for k in range(len(group))]
        self.moving = None

    def send(self, *gates):
        block = after(self.sends[len(self.arrived)], *gates)
        self.arrived.append(swap(block, self.first))
        return self.arrived[-1]

    def terms(self, step):
        g, k = self.spots[step]
        found = [(self.keeps[g], (k,)), (self.arrived[g], (k,))]
        if self.moving is not None:
            found.append((self.moving, ()))
        return found

    def hop(self, step, *gates):
        terms = self.terms(step)
        terms[0] = (after(terms[0][0], *gates), terms[0][1])
        total = add_blocks(terms)
        self.moving = ring(total, self.depth)
        return total

    def finish(self, *gates):
        found = self.terms(self.depth - 1)
        found[0] = (after(found[0][0], *gates), found[0][1])
        far, near = [], []
        for array, prefix in found:
            rows, columns = array.shape[-2:]
            lead = 1
            for size in array.shape[:-2]:
                lead *= size
            begin = prefix[0] * 2 if prefix else 0
            flat = array.reshape(lead, 1, rows, columns)
            far.append((flat, (begin + 1,)))
            near.append((flat, (begin,)))
        total = add_blocks(far)
        self.near = near
        self.other = swap(total, self.last)
        return total

    def rest(self):
        return self.near + [(self.other, ())]


def turned(values, cosine, before, after):
    wide = cosine.shape[1]
    pieces = []
    for begin in range(0, values.shape[1], wide):
        piece = values[:, begin : begin + wide]
        pieces.append(
            piece * cosine
            + pltpu.roll(piece, wide - HALF, 1) * before
            + pltpu.roll(piece, HALF, 1) * after
        )
    return pieces


def turned_back(piece, cosine, before, after):
    wide = cosine.shape[1]
    return (
        piece * cosine
        + pltpu.roll(piece * before, HALF, 1)
        + pltpu.roll(piece * after, wide - HALF, 1)
    )


def normal(values):
    mean = jnp.mean(values, axis=-1, keepdims=True)
    centred = values - mean
    variance = jnp.mean(centred * centred, axis=-1, keepdims=True)
    inverse = lax.rsqrt(variance + EPS)
    return centred * inverse, inverse


def qkv_kernel(depth, parts, own_ref, other_ref, rows_ref, bias_ref,
               cosine_ref, before_ref, after_ref, *rest):
    count = 1 + max(p[0] for p in parts)
    arrays = rest[:count]
    normed_ref, query_ref, key_ref, value_ref, weight, sems = rest[count:]
    pairs = []
    rows = arrays[0].shape[1]
    wide = query_ref.shape[1]
    thin = wide // 2
    for n, i, half, z, x, y in parts:
        spot = pl.ds(pl.multiple_of(place(depth, z, x) * rows, rows), rows)
        y_spot = y_place(y)
        if half == 0:
            pairs.append((arrays[n].at[i], weight.at[y_spot, spot, pl.ds(0, wide)]))
        else:
            pairs.append((arrays[n].at[i, :, pl.ds(0, thin)], weight.at[y_spot, spot, pl.ds(wide, thin)]))
    copies = start_copies(pairs, sems)
    piece = own_ref.shape[0]
    for ref, base in ((own_ref, 0), (other_ref, piece)):
        for begin in range(0, piece, 256):
            hat, _ = normal(ref[pl.ds(begin, 256), :].astype(F32))
            normed_ref[pl.ds(base + begin, 256), :] = (hat * rows_ref[0:1, :] + rows_ref[1:2, :]).astype(BF16)
    for copy in copies:
        copy.wait()
    outs = [(query_ref, 0), (query_ref, thin), (key_ref, 0), (key_ref, thin), (value_ref, 0), (value_ref, thin)]
    for number, (ref, column) in enumerate(outs):
        y, spot = divmod(number, 3)
        for begin in range(0, 2 * piece, piece):
            lines = pl.ds(begin, piece)
            result = dot(normed_ref[lines, :], weight[y, :, pl.ds(spot * thin, thin)], NN)
            result = result + bias_ref[:, pl.ds(number * thin, thin)]
            if ref is value_ref:
                ref[lines, pl.ds(column, thin)] = result.astype(BF16)
            else:
                pieces = turned(result, cosine_ref[lines, :], before_ref[lines, :], after_ref[lines, :])
                for k, item in enumerate(pieces):
                    ref[lines, pl.ds(column + k * 128, 128)] = item.astype(BF16)


def attend_kernel(query_ref, key_ref, value_ref, out_ref, log_ref, *, block, scale):
    length, width = key_ref.shape
    keys = key_ref[...]
    values = value_ref[...]
    for number in range(2):
        mask = half_lanes(number, (length, width))
        key_half = keep(mask, keys)
        value_half = keep(mask, values)
        for start in range(0, length, block):
            rows = pl.ds(start, block)
            scores = dot(query_ref[rows, :], key_half, NT)
            top = jnp.max(scores, axis=1, keepdims=True)
            weights = jnp.exp2((scores - top) * scale)
            total = jnp.sum(weights, axis=1, keepdims=True)
            part = (dot(weights.astype(BF16), value_half, NN) / total).astype(BF16)
            if number == 0:
                out_ref[rows, :] = part
            else:
                out_ref[rows, :] = out_ref[rows, :] + part
            logs = top * scale + jnp.log2(total)
            turned_logs = jnp.transpose(jnp.broadcast_to(logs, (block, 128)))
            log_ref[0, number : number + 1, rows] = turned_logs[0:1, :]


def attend(queries, keys, values, head_size):
    length, width = queries.shape
    wide = 2 * head_size
    pairs = width // wide
    spec = pl.BlockSpec((length, wide), lambda i: (0, i))
    return kernel_call(
        functools.partial(attend_kernel, block=512, scale=LOG2E * head_size**-0.5),
        [queries, keys, values],
        [spec] * 3,
        [shape_of((length, width), BF16), shape_of((pairs, 2, length), F32)],
        grid=(pairs,),
        out_specs=[spec, pl.BlockSpec((1, 2, length), lambda i: (i, 0, 0))],
        flops=16 * length * length * width,
        exps=2 * pairs * length * length,
        room=28,
    )


def attend_back_kernel(
    query_ref, key_ref, value_ref, grad_ref, log_ref, cosine_ref, before_ref, after_ref,
    query_out, key_out, value_out, sum_out, key_sum, value_sum, query_sum, *, block, scale,
):
    length, width = key_ref.shape
    keys = key_ref[...]
    values = value_ref[...]
    for number in range(2):
        mask = half_lanes(number, (length, width))
        key_half = keep(mask, keys)
        value_half = keep(mask, values)
        block_mask = half_lanes(number, (block, width))
        for start in range(0, length, block):
            rows = pl.ds(start, block)
            query = query_ref[rows, :]
            grad = grad_ref[rows, :]
            scores = dot(key_half, query, NT)
            probs = jnp.exp2(scores * (scale * LOG2E) - log_ref[0, number : number + 1, rows])
            prob_grad = dot(value_half, grad, NT)
            mean = jnp.sum(probs * prob_grad, axis=0, keepdims=True)
            score_grad = (probs * (prob_grad - mean)).astype(BF16)
            value_part = dot(probs.astype(BF16), keep(block_mask, grad), NN)
            key_part = dot(score_grad, keep(block_mask, query), NN)
            query_part = dot(score_grad, key_half, TN)
            if number == 0 and start == 0:
                value_sum[...] = value_part
                key_sum[...] = key_part
            else:
                value_sum[...] += value_part
                key_sum[...] += key_part
            if number == 0:
                query_sum[rows, :] = query_part
            else:
                query_sum[rows, :] += query_part
    tables_here = (cosine_ref[...], before_ref[...], after_ref[...])
    for slot, (ref, value) in enumerate(
        (
            (query_out, turned_back(query_sum[...] * scale, *tables_here)),
            (key_out, turned_back(key_sum[...] * scale, *tables_here)),
            (value_out, value_sum[...]),
        )
    ):
        low = value.astype(BF16)
        ref[...] = low
        sum_out[slot : slot + 1, :] = jnp.sum(low.astype(F32), axis=0, keepdims=True)


def attend_back(queries, keys, values, grads, logs, turn, head_size, begin, end):
    length = queries.shape[0]
    wide = 2 * head_size
    width = (end - begin) * wide
    spec = pl.BlockSpec((length, wide), lambda i: (0, begin + i))
    out_spec = pl.BlockSpec((length, wide), lambda i: (0, i))
    whole = pl.BlockSpec((length, wide), lambda i: (0, 0))
    return kernel_call(
        functools.partial(attend_back_kernel, block=512, scale=head_size**-0.5),
        [queries, keys, values, grads, logs, *turn],
        [spec] * 4 + [pl.BlockSpec((1, 2, length), lambda i: (begin + i, 0, 0))] + [whole] * 3,
        [shape_of((length, width), BF16)] * 3 + [shape_of((8, width), F32)],
        grid=(end - begin,),
        out_specs=[out_spec] * 3 + [pl.BlockSpec((8, wide), lambda i: (0, i))],
        scratch=[pltpu.VMEM((length, wide), F32)] * 3,
        flops=40 * length * length * width,
        exps=(end - begin) * 2 * length * length,
        room=28,
    )


def load_proj(depth, parts, arrays, weight, sems):
    pairs = []
    group = arrays[0].shape[1] // 2
    thin = weight.shape[2] // 2
    for n, i, half, z, x, y in parts:
        if half == 0:
            continue
        spot = pl.ds(pl.multiple_of(place(depth, z, x) * group, group), group)
        y_spot = y_place(y)
        for k in range(2):
            pairs.append(
                (
                    arrays[n].at[i, pl.ds(k * group, group), pl.ds(2 * thin - thin, thin)],
                    weight.at[y_spot, spot, pl.ds(k * thin, thin)],
                )
            )
    return start_copies(pairs, sems)


def proj_kernel(depth, parts, attended_ref, *rest):
    count = 1 + max(p[0] for p in parts)
    arrays = rest[:count]
    keep_ref, *sends = rest[count:-2]
    weight, sems = rest[-2:]
    piece, width = keep_ref.shape
    for copy in load_proj(depth, parts, arrays, weight, sems):
        copy.wait()
    half = width // 2
    for y in range(2):
        columns = pl.ds(y * half, half)
        put_rows(sends, columns, dot(attended_ref[pl.ds(piece, piece), :], weight[y], NN))
    for y in range(2):
        columns = pl.ds(y * half, half)
        keep_ref[:, columns] = dot(attended_ref[pl.ds(0, piece), :], weight[y], NN)


def proj_back_kernel(depth, parts, attended_ref, *rest):
    halves, rest = rest[: 2 * SHARES], rest[2 * SHARES :]
    count = 1 + max(p[0] for p in parts)
    arrays = rest[:count]
    out_ref, blocks_ref, weight, scratch, branch, sems, branch_sems = rest[count:]
    copies = start_copies(
        [(ref, branch.at[pl.ds(n * ref.shape[0], ref.shape[0])]) for n, ref in enumerate(halves)], branch_sems
    )
    copies += load_proj(depth, parts, arrays, weight, sems)
    for copy in copies:
        copy.wait()
    length, width = branch.shape
    group = blocks_ref.shape[3] // 2
    thin = blocks_ref.shape[4]
    for y_near in range(2):
        columns = pl.ds(pl.multiple_of(y_place(y_near) * 2 * thin, 128), 2 * thin)
        scratch[...] = dot(attended_ref[...], branch[:, columns], TN)
        for x in range(2):
            for z in range(depth):
                spot = pl.ds(pl.multiple_of(place(depth, z, x) * group, group), group)
                block = scratch[spot, :].astype(BF16)
                for k in range(2):
                    blocks_ref[x, y_near, z, pl.ds(k * group, group), :] = block[:, k * thin : (k + 1) * thin]
    half = width // 2
    for begin in range(0, length, length // 2):
        rows = pl.ds(begin, length // 2)
        total = dot(branch[rows, pl.ds(0, half)], weight[0], NT) + dot(branch[rows, pl.ds(half, half)], weight[1], NT)
        out_ref[rows, :] = total.astype(BF16)


def middle_kernel(own_ref, keep_ref, rows_ref, *rest):
    others, (middle_ref, *seconds) = rest[:SHARES], rest[SHARES:]
    size = others[0].shape[0]
    for begin in range(0, SHARES * size, LINES):
        k = begin // size
        rows = pl.ds(begin, LINES)
        lines = pl.ds(begin % size, LINES)
        middle = own_ref[rows, :].astype(F32) + keep_ref[rows, :] + others[k][lines, :].astype(F32) + rows_ref[4:5, :]
        middle_ref[rows, :] = middle
        hat, _ = normal(middle)
        seconds[k][lines, :] = (hat * rows_ref[2:3, :] + rows_ref[3:4, :]).astype(BF16)


def load_up(depth, parts, arrays, weight, sems):
    pairs = []
    rows, wide = arrays[0].shape[1:]
    for n, i, half, z, x, y in parts:
        spot = pl.ds(pl.multiple_of(place(depth, z, x) * rows, rows), rows)
        y_spot = y_place(y)
        pairs.append((arrays[n].at[i], weight.at[y_spot, spot, pl.ds(half * wide, wide)]))
    return start_copies(pairs, sems)


def up_kernel(depth, parts, bias_ref, *rest):
    halves, rest = rest[: 2 * SHARES], rest[2 * SHARES :]
    count = 1 + max(p[0] for p in parts)
    arrays = rest[:count]
    second_ref, active_ref, slope_ref, weight, sems = rest[count:]
    copies = load_up(depth, parts, arrays, weight, sems)
    size = halves[0].shape[0]
    piece = size * SHARES
    for n, ref in enumerate(halves):
        second_ref[pl.ds(n * size, size), :] = ref[...]
    for copy in copies:
        copy.wait()
    wide = weight.shape[2]
    for y in range(2):
        for column in range(0, wide, 256):
            for begin in range(0, 2 * piece, piece):
                rows = pl.ds(begin, piece)
                columns = pl.ds(y * wide + column, 256)
                hidden = dot(second_ref[rows, :], weight[y, :, pl.ds(column, 256)], NN) + bias_ref[:, columns]
                gate = 0.5 + 0.5 * lax.erf(hidden * 0.7071067811865476)
                active_ref[rows, columns] = (hidden * gate).astype(BF16)
                bell = jnp.exp2(hidden * hidden * (-0.5 * LOG2E)) * 0.3989422804014327
                slope_ref[rows, columns] = (gate + hidden * bell).astype(BF16)


def load_down(depth, parts, arrays, weight, sems):
    pairs = []
    rows = arrays[0].shape[1]
    for n, i, half, z, x, y in parts:
        line = place(depth, z, x) * (2 * rows) + half * rows
        spot = pl.ds(pl.multiple_of(line, rows), rows)
        pairs.append((arrays[n].at[i], weight.at[y_place(y), spot]))
    return start_copies(pairs, sems)


def hidden_kernel(depth, parts, rows, own_ref, other_ref, slope_ref, act_ref, *rest):
    count = 1 + max(p[0] for p in parts)
    arrays = rest[:count]
    out_ref, sum_ref, *blocks = rest[count:-6]
    weight, grad, scratch, sems, grad_sems, act_sems = rest[-6:]
    piece = own_ref.shape[0]
    copies = start_copies(
        [(own_ref, grad.at[pl.ds(0, piece)]), (other_ref, grad.at[pl.ds(piece, piece)])], grad_sems
    )
    copies += load_down(depth, parts, arrays, weight, sems)
    for copy in copies:
        copy.wait()
    half = own_ref.shape[1] // 2
    for column in range(0, out_ref.shape[1], 512):
        columns = pl.ds(column, 512)
        total = dot(grad[:, pl.ds(0, half)], weight[0, columns, :], NT)
        total = total + dot(grad[:, pl.ds(half, half)], weight[1, columns, :], NT)
        low = (total * slope_ref[:, columns].astype(F32)).astype(BF16)
        out_ref[:, columns] = low
        sum_ref[0:1, columns] = jnp.sum(low.astype(F32), axis=0, keepdims=True)
    columns_grad_kernel(depth, rows, 1, act_ref, out_ref, *blocks, scratch, act_sems)


def down_kernel(depth, parts, active_ref, *rest):
    count = 1 + max(p[0] for p in parts)
    arrays = rest[:count]
    keep_ref, *sends = rest[count:-2]
    weight, sems = rest[-2:]
    piece, width = keep_ref.shape
    for copy in load_down(depth, parts, arrays, weight, sems):
        copy.wait()
    half = width // 2
    for y in range(2):
        columns = pl.ds(y * half, half)
        put_rows(sends, columns, dot(active_ref[pl.ds(piece, piece), :], weight[y], NN))
        keep_ref[:, columns] = dot(active_ref[pl.ds(0, piece), :], weight[y], NN)


def up_back_kernel(depth, parts, grad_ref, *rest):
    count = 1 + max(p[0] for p in parts)
    arrays = rest[:count]
    keep_ref, *sends = rest[count:-2]
    weight, sems = rest[-2:]
    piece, width = keep_ref.shape
    for copy in load_up(depth, parts, arrays, weight, sems):
        copy.wait()
    wide = weight.shape[2]
    for refs, begin in ((sends, piece), ([keep_ref], 0)):
        rows = pl.ds(begin, piece)
        for column in range(0, width, 512):
            columns = pl.ds(column, 512)
            total = dot(grad_ref[rows, pl.ds(0, wide)], weight[0, columns, :], NT)
            total = total + dot(grad_ref[rows, pl.ds(wide, wide)], weight[1, columns, :], NT)
            put_rows(refs, columns, total)


def middle_back_kernel(keep_ref, middle_ref, grad_ref, rows_ref, *rest):
    others, (middle_out, *branches, sum_out) = rest[:SHARES], rest[SHARES:]
    totals = [jnp.zeros((1, keep_ref.shape[1]), F32) for _ in range(4)]
    size = others[0].shape[0]
    for begin in range(0, SHARES * size, LINES):
        k = begin // size
        rows = pl.ds(begin, LINES)
        lines = pl.ds(begin % size, LINES)
        grad = keep_ref[rows, :] + others[k][lines, :].astype(F32)
        hat, inverse = normal(middle_ref[rows, :])
        scaled = grad * rows_ref[2:3, :]
        first = jnp.mean(scaled, axis=-1, keepdims=True)
        second = jnp.mean(scaled * hat, axis=-1, keepdims=True)
        outer = grad_ref[rows, :].astype(F32)
        result = outer + inverse * (scaled - first - hat * second)
        middle_out[rows, :] = result
        low = result.astype(BF16)
        branches[k][lines, :] = low
        for n, value in enumerate((grad * hat, grad, low.astype(F32), outer)):
            totals[n] = totals[n] + jnp.sum(value, axis=0, keepdims=True)
    for n in range(4):
        sum_out[n : n + 1, :] = totals[n]


def out_kernel(middle_ref, keep_ref, rows_ref, *rest):
    others, (out_ref,) = rest[:SHARES], rest[SHARES:]
    size = others[0].shape[0]
    for begin in range(0, SHARES * size, LINES):
        k = begin // size
        rows = pl.ds(begin, LINES)
        lines = pl.ds(begin % size, LINES)
        total = middle_ref[rows, :] + (keep_ref[rows, :] + others[k][lines, :].astype(F32)) + rows_ref[5:6, :]
        out_ref[rows, :] = total.astype(BF16)


def tokens_back_kernel(keep_ref, own_ref, grad_ref, rows_ref, *rest):
    others, (out_ref, sum_out) = rest[:SHARES], rest[SHARES:]
    totals = [jnp.zeros((1, keep_ref.shape[1]), F32) for _ in range(2)]
    size = others[0].shape[0]
    for begin in range(0, SHARES * size, LINES):
        k = begin // size
        rows = pl.ds(begin, LINES)
        lines = pl.ds(begin % size, LINES)
        grad = keep_ref[rows, :] + others[k][lines, :].astype(F32)
        hat, inverse = normal(own_ref[rows, :].astype(F32))
        scaled = grad * rows_ref[0:1, :]
        first = jnp.mean(scaled, axis=-1, keepdims=True)
        second = jnp.mean(scaled * hat, axis=-1, keepdims=True)
        result = grad_ref[rows, :] + inverse * (scaled - first - hat * second)
        out_ref[rows, :] = result.astype(BF16)
        for n, value in enumerate((grad * hat, grad)):
            totals[n] = totals[n] + jnp.sum(value, axis=0, keepdims=True)
    for n in range(2):
        sum_out[n : n + 1, :] = totals[n]


def load_columns(depth, source, scratch, rows, sems):
    pairs = []
    for x in range(2):
        for z in range(depth):
            spot = pl.ds(pl.multiple_of(place(depth, z, x) * rows, rows), rows)
            pairs.append((source.at[:, spot], scratch.at[:, pl.ds((x * depth + z) * rows, rows)]))
    return start_copies(pairs, sems)


def rows_grad_kernel(depth, rows, sent, act_ref, own_ref, other_ref, *rest):
    outs, (scratch, grad, sems, grad_sems) = rest[:-4], rest[-4:]
    piece = own_ref.shape[0]
    copies = start_copies(
        [(own_ref, grad.at[pl.ds(0, piece)]), (other_ref, grad.at[pl.ds(piece, piece)])], grad_sems
    )
    pairs = []
    order = [z for group in near_first(depth) for z in group]
    for n, z in enumerate(order):
        spot = pl.ds(pl.multiple_of(place(depth, z, sent) * rows, rows), rows)
        pairs.append((act_ref.at[:, spot], scratch.at[:, pl.ds(n * rows, rows)]))
    copies += start_copies(pairs, sems)
    for copy in copies:
        copy.wait()
    part = grad.shape[1] // 2
    begin = 0
    for ref in outs:
        size = ref.shape[0]
        for y_near in range(2):
            columns = pl.ds(pl.multiple_of(y_place(y_near) * part, 128), part)
            result = dot(scratch[:, pl.ds(begin * rows, size * rows)], grad[:, columns], TN, BF16)
            for k in range(size):
                ref[k, y_near] = result[k * rows : (k + 1) * rows]
        begin += size


def rows_grad(act, grad_own, grad_other, depth, rows, sent):
    length = act.shape[0]
    width = grad_own.shape[1]
    return (
        functools.partial(rows_grad_kernel, depth, rows, sent),
        [act, grad_own, grad_other],
        [ANYWHERE] * 3,
        [shape_of((len(group), 2, rows, width // 2), BF16) for group in near_first(depth)],
        [
            pltpu.VMEM((length, depth * rows), BF16),
            pltpu.VMEM((length, width), BF16),
            pltpu.SemaphoreType.DMA((depth,)),
            pltpu.SemaphoreType.DMA((2,)),
        ],
    )


def columns_grad_kernel(depth, rows, sent, act_ref, grad_ref, *rest):
    outs, scratch, sems = rest[:-2], rest[-2], rest[-1]
    pairs = []
    order = [z for group in near_first(depth) for z in group]
    for n, z in enumerate(order):
        for x in range(2):
            spot = pl.ds(pl.multiple_of(place(depth, z, x) * rows, rows), rows)
            pairs.append((act_ref.at[:, spot], scratch.at[:, pl.ds((2 * n + x) * rows, rows)]))
    for copy in start_copies(pairs, sems):
        copy.wait()
    part = grad_ref.shape[1] // 2
    begin = 0
    half = part // 2
    y = y_place(sent)
    for ref in outs:
        size = ref.shape[0]
        for column in range(0, part, half):
            columns = pl.ds(pl.multiple_of(y * part + column, 128), half)
            result = dot(scratch[:, pl.ds(begin * rows, 2 * size * rows)], grad_ref[:, columns], TN, BF16)
            for k in range(size):
                for x in range(2):
                    line = (2 * k + x) * rows
                    ref[k, x, :, pl.ds(column, half)] = result[line : line + rows]
        begin += 2 * size


def columns_grad(act, grad, depth, rows, sent):
    length, total = act.shape
    part = grad.shape[1] // 2
    return (
        functools.partial(columns_grad_kernel, depth, rows, sent),
        [act, grad],
        [ANYWHERE, WHOLE],
        [shape_of((len(group), 2, rows, part), BF16) for group in near_first(depth)],
        [pltpu.VMEM((length, total), BF16), pltpu.SemaphoreType.DMA((2 * depth,))],
    )


def own_half(core, mine, other):
    first = core == 0
    return jnp.where(first, mine, other), jnp.where(first, other, mine)


def split_kernel(hidden_block, qkv_ref, up_ref, qkv_mine, qkv_other, up_mine, up_other):
    core = lax.axis_index("core")
    rows = qkv_ref.shape[0]
    low = lax.broadcasted_iota(jnp.int32, (rows, 128), 1) < 64
    for tile in range(qkv_ref.shape[1] // 256):
        one = qkv_ref[:, pl.ds(tile * 256, 128)].astype(F32)
        two = qkv_ref[:, pl.ds(tile * 256 + 128, 128)].astype(F32)
        even = jnp.where(low, one, pltpu.roll(two, 64, 1)).astype(BF16)
        odd = jnp.where(low, pltpu.roll(one, 64, 1), two).astype(BF16)
        mine, other = own_half(core, even, odd)
        qkv_mine[:, pl.ds(tile * 128, 128)] = mine
        qkv_other[:, pl.ds(tile * 128, 128)] = other
    for tile in range(up_ref.shape[1] // (2 * hidden_block)):
        even = up_ref[:, pl.ds(tile * 2 * hidden_block, hidden_block)]
        odd = up_ref[:, pl.ds((tile * 2 + 1) * hidden_block, hidden_block)]
        mine, other = own_half(core, even, odd)
        up_mine[:, pl.ds(tile * hidden_block, hidden_block)] = mine
        up_other[:, pl.ds(tile * hidden_block, hidden_block)] = other


def pack_kernel(mine_ref, other_ref, *rest):
    extra, out_ref = rest[:-1], rest[-1]
    rows, columns = mine_ref.shape
    half = out_ref.shape[2]
    for ref, number in ((mine_ref, lax.axis_index("core")), (other_ref, 1 - lax.axis_index("core"))):
        lines = pl.ds(pl.multiple_of(number * rows, rows), rows)
        out_ref[0, lines, :] = ref[:, pl.ds(0, half)]
        out_ref[1, lines, pl.ds(0, columns - half)] = ref[:, pl.ds(half, columns - half)]
    for ref in extra:
        thin = ref.shape[1] // 2
        for k in range(2):
            out_ref[1, pl.ds(k * rows, rows), pl.ds(half - thin, thin)] = ref[:, pl.ds(k * thin, thin)]


def join_heads_kernel(mine_ref, other_ref, out_ref):
    rows = mine_ref.shape[0]
    low = lax.broadcasted_iota(jnp.int32, (rows, 128), 1) < 64
    for tile in range(mine_ref.shape[1] // 128):
        columns = pl.ds(tile * 128, 128)
        even, odd = own_half(lax.axis_index("core"), mine_ref[:, columns].astype(F32), other_ref[:, columns].astype(F32))
        out_ref[:, pl.ds(tile * 256, 128)] = jnp.where(low, even, pltpu.roll(odd, 64, 1))
        out_ref[:, pl.ds(tile * 256 + 128, 128)] = jnp.where(low, pltpu.roll(even, 64, 1), odd)


def join_blocks_kernel(block, mine_ref, other_ref, out_ref):
    for tile in range(mine_ref.shape[1] // block):
        columns = pl.ds(tile * block, block)
        even, odd = own_half(lax.axis_index("core"), mine_ref[:, columns].astype(F32), other_ref[:, columns].astype(F32))
        out_ref[:, pl.ds(2 * tile * block, block)] = even
        out_ref[:, pl.ds((2 * tile + 1) * block, block)] = odd


def mixed_grad_kernel(depth, sent, act_ref, *rest):
    count = len(rest) - 9
    pieces, (proj_ref, *outs) = rest[:count], rest[count : count + 5]
    scratch, mixed, sems, mixed_sems = rest[count + 5 :]
    rows = outs[0].shape[1]
    copies = load_columns(depth, act_ref, scratch, rows, sems)
    size = pieces[0].shape[1]
    wide = size * count // 3
    thin = wide // 2
    copies += start_copies(
        [(ref, mixed.at[:, pl.ds(n * size, size)]) for n, ref in enumerate(pieces)],
        mixed_sems,
    )
    for copy in copies:
        copy.wait()
    part = wide + thin
    half = depth * rows
    columns = pl.ds(pl.multiple_of(y_place(sent) * part, 128), wide)
    for x in range(2):
        result = dot(scratch[:, pl.ds(x * half, half)], mixed[:, columns], TN, BF16)
        for z in range(depth):
            outs[1 - x][z] = result[z * rows : (z + 1) * rows]
    for y_near in range(2):
        columns = pl.ds(pl.multiple_of(y_place(y_near) * part + wide, 128), thin)
        result = dot(scratch[:, pl.ds(sent * half, half)], mixed[:, columns], TN, BF16)
        for z in range(depth):
            outs[3 - y_near][z, :, pl.ds(0, thin)] = result[z * rows : (z + 1) * rows]
            outs[3 - y_near][z, :, pl.ds(thin, thin)] = proj_ref[sent, y_near, z]


def mixed_back_kernel(depth, parts, count, *rest):
    pieces, rest = rest[:count], rest[count:]
    arrays = rest[: 1 + max(p[0] for p in parts)]
    keep_ref, *sends = rest[len(arrays) : -4]
    weight, mixed, sems, mixed_sems = rest[-4:]
    pairs = []
    rows = arrays[0].shape[1]
    size = pieces[0].shape[1]
    wide = size * count // 3
    thin = wide // 2
    copies = start_copies(
        [(ref, mixed.at[:, pl.ds(n * size, size)]) for n, ref in enumerate(pieces)], mixed_sems
    )
    for n, i, half, z, x, y in parts:
        spot = pl.ds(pl.multiple_of(place(depth, z, x) * rows, rows), rows)
        y_spot = y_place(y)
        if half == 0:
            pairs.append((arrays[n].at[i], weight.at[y_spot, spot, pl.ds(0, wide)]))
        else:
            pairs.append((arrays[n].at[i, :, pl.ds(0, thin)], weight.at[y_spot, spot, pl.ds(wide, thin)]))
    copies += start_copies(pairs, sems)
    for copy in copies:
        copy.wait()
    piece, width = keep_ref.shape
    part = wide + thin
    for refs, begin in ((sends, piece), ([keep_ref], 0)):
        lines = pl.ds(begin, piece)
        for column in range(0, width, 512):
            columns = pl.ds(column, 512)
            total = dot(mixed[lines, pl.ds(0, part)], weight[0, columns, :], NT)
            total = total + dot(mixed[lines, pl.ds(part, part)], weight[1, columns, :], NT)
            put_rows(refs, columns, total)


def sum_of(refs):
    total = None
    for ref in refs:
        value = ref[(0,) * (len(ref.shape) - 2)].astype(F32)
        total = value if total is None else total + value
    return total


def core_rows(values_ref, rows, mine_ref, send_ref):
    core = lax.axis_index("core")
    mine_ref[...] = values_ref[pl.ds(pl.multiple_of(core * rows, rows), rows), :]
    send_ref[...] = values_ref[pl.ds(pl.multiple_of((1 - core) * rows, rows), rows), :].astype(BF16)


def finish_up_kernel(*refs):
    mine_ref, send_ref, total = refs[-3:]
    total[...] = sum_of(refs[:-3])
    core_rows(total, mine_ref.shape[0], mine_ref, send_ref)


def finish_down_kernel(*refs):
    refs[-1][...] = sum_of(refs[:-1])


def hop_first_kernel(*refs):
    out_ref = refs[-1]
    ones, twos = refs[0:3], refs[3:6]
    for half, group in ((0, ones), (1, twos)):
        total = sum_of(group)
        if len(refs) > 7:
            total = total + refs[6][half].astype(F32)
        out_ref[half] = total.astype(BF16)


def finish_first_kernel(*refs):
    moving = refs[6]
    mine_ref, send_ref, proj_ref, total = refs[7:]
    one = sum_of(refs[0:3]) + moving[0].astype(F32)
    two = sum_of(refs[3:6]) + moving[1].astype(F32)
    wide = one.shape[1]
    thin = total.shape[1] - wide
    total[:, pl.ds(0, wide)] = one
    total[:, pl.ds(wide, thin)] = two[:, :thin]
    core_rows(total, mine_ref.shape[0], mine_ref, send_ref)
    group = proj_ref.shape[0]
    for k in range(2):
        proj_ref[:, pl.ds(k * (wide - thin), wide - thin)] = two[k * group : (k + 1) * group, thin:]


def first_terms(keeps, nears, lasts, z):
    arrays, specs = [], []
    for keep_one, near, last in zip(keeps, nears, lasts):
        rows, columns = last.shape[-2:]
        arrays += [keep_one, near, last]
        specs += [pl.BlockSpec((1, rows, columns), lambda i: (z, 0, 0))] * 3
    return arrays, specs


def same(shape):
    return pl.BlockSpec(shape, lambda i: (0,) * len(shape))


EACH = 32
ROW = 512


def params_kernel(count, head_size, hidden_block, in_ref, rows_ref, qkv_ref, up_ref):
    core = lax.axis_index("core")
    row = lax.broadcasted_iota(jnp.int32, (count, 128), 0)
    lane = lax.broadcasted_iota(jnp.int32, (count, 128), 1)
    per = 128 // EACH
    for i in range(6):
        tile = in_ref[:, pl.ds(i // per * 128, 128)]
        shift = (128 - i % per * EACH) % 128
        first = jnp.where(lane < EACH, pltpu.roll(tile, shift, 1) if shift else tile, 0.0)
        wide = first
        for k in range(1, per):
            wide = wide + pltpu.roll(first, k * EACH, 1)
        for k in range(count // per):
            picked = jnp.where(row == k * per + lane // EACH, wide, 0.0)
            rows_ref[i : i + 1, pl.ds(k * 128, 128)] = jnp.sum(picked, axis=0, keepdims=True)
    one_lane = lax.broadcasted_iota(jnp.int32, (1, 128), 1)
    size = 3 * EACH
    low = one_lane < head_size
    for t in range(qkv_ref.shape[1] // 128):
        pair = []
        for k in (2 * t, 2 * t + 1):
            tile = jnp.zeros((1, 128), F32)
            for d in range(k * 128 // size, (k * 128 + 127) // size + 1):
                offset = d * size - k * 128
                value = in_ref[d : d + 1, pl.ds(256, 128)]
                value = pltpu.roll(value, offset % 128, 1) if offset % 128 else value
                tile = jnp.where((one_lane >= offset) & (one_lane < offset + size), value, tile)
            pair.append(tile)
        even = jnp.where(low, pair[0], pltpu.roll(pair[1], head_size, 1))
        odd = jnp.where(low, pltpu.roll(pair[0], head_size, 1), pair[1])
        qkv_ref[:, pl.ds(t * 128, 128)] = jnp.where(core == 0, even, odd)
    tiles = hidden_block // 128
    for t in range(up_ref.shape[1] // 128):
        m, q = divmod(t, tiles)
        spots = [2 * m * tiles + q, (2 * m + 1) * tiles + q]
        even, odd = [in_ref[d : d + 1, pl.ds(384, 128)] for d in spots]
        up_ref[:, pl.ds(t * 128, 128)] = jnp.where(core == 0, even, odd)


def small_kernel(count, head_size, hidden_block, mixed_count, *refs):
    first_ref, middle_ref, up_ref = refs[:3]
    mixed_refs = refs[3 : 3 + mixed_count]
    out_ref = refs[-1]
    core = lax.axis_index("core")
    row = lax.broadcasted_iota(jnp.int32, (count, 128), 0)
    lane = lax.broadcasted_iota(jnp.int32, (count, 128), 1)
    per = 128 // EACH
    vectors = [(first_ref, 0), (first_ref, 1), (middle_ref, 0), (middle_ref, 1), (middle_ref, 2), (middle_ref, 3)]
    tiles = [jnp.zeros((count, 128), F32) for _ in range(2)]
    for i, (ref, line) in enumerate(vectors):
        spread = jnp.zeros((count, 128), F32)
        for k in range(count // per):
            spread = jnp.where(row // per == k, ref[line : line + 1, pl.ds(k * 128, 128)], spread)
        moved = spread
        for k in range(per):
            shift = (i % per - k) * EACH % 128
            if shift:
                moved = jnp.where(row % per == k, pltpu.roll(spread, shift, 1), moved)
        tiles[i // per] = jnp.where(lane // EACH == i % per, moved, tiles[i // per])
    for n, tile in enumerate(tiles):
        out_ref[:, pl.ds(n * 128, 128)] = tile
    one_lane = lax.broadcasted_iota(jnp.int32, (1, 128), 1)
    low = one_lane < head_size
    size = 3 * EACH
    globals_ = []
    for line in range(3):
        for ref in mixed_refs:
            for k in range(ref.shape[1] // 128):
                value = ref[line : line + 1, pl.ds(k * 128, 128)]
                other = pltpu.roll(value, head_size, 1)
                even = core == 0
                globals_.append(jnp.where(low == even, jnp.where(even, value, other), 0.0))
                globals_.append(jnp.where(low == even, jnp.where(even, other, value), 0.0))
    for d in range(count):
        total = jnp.zeros((1, 128), F32)
        for k in range(d * size // 128, (d * size + size - 1) // 128 + 1):
            offset = k * 128 - d * size
            value = pltpu.roll(globals_[k], offset % 128, 1) if offset % 128 else globals_[k]
            inside = (one_lane >= offset) & (one_lane < offset + 128) & (one_lane < size)
            total = jnp.where(inside, value, total)
        out_ref[d : d + 1, pl.ds(256, 128)] = total
    steps = hidden_block // 128
    for t in range(up_ref.shape[1] // 128):
        m, q = divmod(t, steps)
        value = up_ref[0:1, pl.ds(t * 128, 128)]
        for p in range(2):
            d = (2 * m + p) * steps + q
            out_ref[d : d + 1, pl.ds(384, 128)] = jnp.where(core == p, value, 0.0)


HALF = 10


def turn_tables(places, head_size, wide):
    section = 2 * (head_size // 3 // 2)
    half_size = section // 2
    lane = jnp.arange(wide) % head_size
    number = lane // section
    spot = lane % section
    frequency = 1.0 / 10000.0 ** ((spot % half_size).astype(F32) / half_size)
    place_of = jnp.where(
        number[None, :] == 0,
        places[:, 0:1],
        jnp.where(number[None, :] == 1, places[:, 1:2], places[:, 2:3]),
    )
    angles = place_of.astype(F32) * frequency[None, :]
    live = (number < 3)[None, :]
    cosine = jnp.where(live, jnp.cos(angles), 1.0)
    sine = jnp.where(live, jnp.sin(angles), 0.0)
    low = (spot < half_size)[None, :]
    return cosine, jnp.where(low, -sine, 0.0), jnp.where(low, 0.0, sine)


def fast_shards(
    tokens,
    frame_index,
    row_index,
    column_index,
    norm1_gain,
    norm1_bias,
    qkv_weight,
    qkv_bias,
    proj_weight,
    proj_bias,
    norm2_gain,
    norm2_bias,
    up_weight,
    up_bias,
    down_weight,
    down_bias,
    cotangent,
):
    depth = lax.axis_size("z")
    everyone = ("z", "x", "core", "y")
    count = 8 * depth
    piece, width = tokens.shape
    length = 2 * piece
    head_size = width // HEADS
    local = width // 2
    hidden_block = down_weight.shape[0]
    hidden_size = up_weight.shape[1]
    up_rows = width // (2 * depth)
    shard_rows = qkv_weight.shape[0]
    part_qkv = 3 * local // 2
    part_up = up_weight.shape[1] // 2
    block_kind = shape_of((2, up_rows, local), BF16)
    step = max(depth // 2, 1)
    dma = pltpu.SemaphoreType.DMA
    shares = [shape_of((piece // SHARES, width), BF16)] * SHARES
    partial = [shape_of((piece, width), F32)] + shares

    qkv_mine, qkv_other, up_mine, up_other = kernel_call(
        functools.partial(split_kernel, hidden_block),
        [qkv_weight, up_weight],
        [WHOLE, WHOLE],
        [shape_of((shard_rows, part_qkv), BF16)] * 2 + [shape_of((shard_rows, part_up), BF16)] * 2,
    )
    (first_block,) = kernel_call(
        pack_kernel, [qkv_mine, swap(qkv_other, "core"), proj_weight], [WHOLE] * 3, [block_kind]
    )
    now = (first_block,)

    def at(values):
        return after(values, *now)

    def packed_small():
        return jnp.concatenate(
            [
                at(item)
                for item in (norm1_gain, norm1_bias, norm2_gain, norm2_bias, proj_bias, down_bias)
            ]
            + [jnp.zeros((256 - 6 * EACH,), BF16), qkv_bias, jnp.zeros((EACH,), BF16), up_bias]
        )

    hops = [first_block, ring(first_block, depth)]
    tokens_traded = trade(at(tokens))
    places = jnp.stack([frame_index, row_index, column_index], axis=0)
    places_traded = trade(at(places))
    small = packed_small()
    up_other = swap(at(up_other), "core")
    now = (hops[1], up_other, small)
    hops.append(ring(at(hops[1]), depth))
    grad_traded = trade(at(cotangent))
    (up_block,) = kernel_call(pack_kernel, [at(up_mine), up_other], [WHOLE] * 2, [block_kind])
    now = (hops[2], up_block, tokens_traded)
    while len(hops) < depth:
        hops.append(ring(at(hops[-1]), depth))

    def far_halves(block):
        block = at(block)
        return [block, swap(block[0], "x")[None], swap(block[1], "y")[None]]

    def doubled(parts):
        return join([at(parts[0])] + parts[1:], [(0, 0, 1), (1, 0, 1), (0, 1, 1), (2, 0, 1)])

    def two_halves(hops):
        return [join([at(hops[0])] + hops[1:], [(n, half, 1) for n in range(depth)]) for half in range(2)]

    small = jnp.broadcast_to(at(small).astype(F32), (count, ROW))
    small = lax.all_to_all(small, everyone, split_axis=0, concat_axis=0, tiled=True)
    places = choose(at(places), places_traded)
    places = jnp.concatenate([places, swap(places, "core")], axis=1).T
    grad_own = choose(at(cotangent), grad_traded)
    tokens_own = choose(at(tokens), tokens_traded)
    tokens_other = swap(tokens_own, "core")
    now = (hops[-1], tokens_other, places, grad_own, small)

    one, two = two_halves(hops)
    one_x = swap(one, "x")
    two_y = swap(two, "y")
    one_y = swap(one, "y")
    two_x = swap(two, "x")
    up_hops = [up_block, ring(at(up_block), depth)]
    turn = turn_tables(at(places), head_size, 2 * head_size)
    grad_other = swap(at(grad_own), "core")
    now = (one_x, two_y, up_hops[-1], grad_other, *turn)
    one_xy = swap(at(one_x), "y")
    two_xy = swap(at(two_y), "x")
    up_hops.append(ring(at(up_hops[-1]), depth))
    params, bias_qkv, bias_up = kernel_call(
        functools.partial(params_kernel, count, head_size, hidden_block),
        [at(small)],
        [WHOLE],
        [shape_of((8, width), F32), shape_of((1, 3 * local), F32), shape_of((1, hidden_size), F32)],
    )
    now = (one_y, two_x, up_hops[-1], params)
    while len(up_hops) < depth:
        up_hops.append(ring(at(up_hops[-1]), depth))
    down_far = far_halves(down_weight.reshape(2, hidden_block // 2, -1))
    now = (one_xy, two_xy, up_hops[-1], *down_far)

    first_arrays = [one, two, one_x, two_y, one_y, two_x, one_xy, two_xy]
    marks = [(0, 0, 0), (1, 0, 0), (0, 1, 0), (1, 0, 1), (0, 0, 1), (1, 1, 0), (0, 1, 1), (1, 1, 1)]
    first_parts = [
        (n, z, half, z, x, y) for n, (half, x, y) in enumerate(marks) for z in range(depth)
    ]
    part_count = len(first_parts)
    pair_parts = []
    for z in range(depth):
        pair_parts += [(z, 0, 0, z, 0, 0), (z, 1, 0, z, 1, 0), (z, 2, 1, z, 0, 0), (z, 3, 1, z, 0, 1)]
        array = depth + 2 * (z // step)
        k = z % step
        pair_parts += [
            (array, 2 * k, 0, z, 0, 1),
            (array, 2 * k + 1, 0, z, 1, 1),
            (array + 1, 2 * k, 1, z, 1, 0),
            (array + 1, 2 * k + 1, 1, z, 1, 1),
        ]
    pair_count = len(pair_parts)

    up_one, up_two = two_halves(up_hops)
    down_hops = [doubled(down_far)]
    up_one_x = swap(up_one, "x")
    up_two_y = swap(up_two, "y")
    up_one_y = swap(up_one, "y")
    up_two_x = swap(up_two, "x")
    down_hops.append(ring(down_hops[0], depth))
    normed, queries, keys, values = kernel_call(
        functools.partial(qkv_kernel, depth, first_parts),
        [after(tokens_own, up_one, up_two, down_hops[0]), tokens_other, params, bias_qkv, *turn, *first_arrays],
        [WHOLE] * 7 + [ANYWHERE] * len(first_arrays),
        [shape_of((length, width), BF16)] + [shape_of((length, local), BF16)] * 3,
        scratch=[pltpu.VMEM((2, width, 3 * local // 2), BF16), dma((part_count,))],
    )
    now = (normed, up_one_x, up_two_y, down_hops[-1])
    up_one_xy = swap(at(up_one_x), "y")
    up_two_xy = swap(at(up_two_y), "x")
    up_arrays = [up_one, up_two, up_one_x, up_two_y, up_one_y, up_two_x, up_one_xy, up_two_xy]
    down_hops.append(ring(at(down_hops[-1]), depth))
    attended, logs = attend(at(queries), keys, values, head_size)
    now = (attended, up_one_y, up_two_x, up_one_xy, up_two_xy, down_hops[-1])

    def last_pair(group):
        ones = join([at(group[0])] + group[1:], [(n, 0, 2) for n in range(len(group))])
        twos = join([at(group[0])] + group[1:], [(n, 2, 2) for n in range(len(group))])
        return ones, twos

    def last_swaps(pair):
        return [swap(at(pair[0]), "y"), swap(at(pair[1]), "x")]

    while len(down_hops) < depth:
        down_hops.append(ring(at(down_hops[-1]), depth))
    near_pair = last_pair(down_hops[:step])
    near = last_swaps(near_pair)
    proj_scratch = [pltpu.VMEM((2, local, width // 2), BF16), dma((part_count,))]
    kept, *sent = kernel_call(
        functools.partial(proj_kernel, depth, first_parts),
        [after(attended, *near_pair), *first_arrays],
        [WHOLE] + [ANYWHERE] * len(first_arrays),
        partial,
        scratch=proj_scratch,
    )
    middle, *second_own = kernel_call(
        middle_kernel, [tokens_own, kept, params, *swap_each(sent)], [WHOLE] * (3 + SHARES), partial
    )
    second_other = swap_each(second_own)
    now = (*second_own, down_hops[-1])
    far_pair = last_pair(down_hops[step:])
    far = last_swaps(far_pair)
    down_arrays = down_hops + near + far
    up_scratch = [pltpu.VMEM((2, width, hidden_size // 2), BF16), dma((part_count,))]
    second, active, slope = kernel_call(
        functools.partial(up_kernel, depth, first_parts),
        [after(bias_up, *far_pair), *second_own, *second_other, *up_arrays],
        [WHOLE] * (1 + 2 * SHARES) + [ANYWHERE] * len(up_arrays),
        [shape_of((length, width), BF16)] + [shape_of((length, hidden_size), BF16)] * 2,
        scratch=up_scratch,
    )
    (down_sends,) = merged_call(
        rows_grad(active, grad_own, grad_other, depth, hidden_block, 1)
    )
    down_sum = Scatter(down_sends, "x", "y", depth)
    now = (*down_sends, *far_pair)
    down_sum.send()
    down_sum.send()
    down_scratch = [pltpu.VMEM((2, hidden_size, width // 2), BF16), dma((pair_count,))]
    hidden_grad, up_sums, *up_sends = kernel_call(
        functools.partial(hidden_kernel, depth, pair_parts, up_rows),
        [grad_own, grad_other, at(slope), second, *down_arrays],
        [ANYWHERE] * 2 + [WHOLE] + [ANYWHERE] * (1 + len(down_arrays)),
        [shape_of((length, hidden_size), BF16), shape_of((8, hidden_size), F32)]
        + [shape_of((len(group), 2, up_rows, hidden_size // 2), BF16) for group in near_first(depth)],
        scratch=[
            down_scratch[0],
            pltpu.VMEM((length, width), BF16),
            pltpu.VMEM((length, width), BF16),
            down_scratch[1],
            dma((2,)),
            dma((2 * depth,)),
        ],
    )
    up_sum = Scatter(up_sends, "y", "x", depth)
    up_sum.send()
    up_sum.send()
    now = tuple(up_sends)
    (kept, *sent), down_sum.keeps = merged_call(
        (
            functools.partial(up_back_kernel, depth, first_parts),
            [at(hidden_grad), *up_arrays],
            [WHOLE] + [ANYWHERE] * len(up_arrays),
            partial,
            up_scratch,
        ),
        rows_grad(active, grad_own, grad_other, depth, hidden_block, 0),
    )
    sent_other = swap_each(sent)
    gate = down_sum.hop(0, down_sum.keeps[0])
    (middle_grad, *branch_own, middle_sums), up_sum.keeps = merged_call(
        (
            middle_back_kernel,
            [after(kept, gate), middle, grad_own, params, *sent_other],
            [WHOLE] * (4 + SHARES),
            partial + [shape_of((8, width), F32)],
            [],
        ),
        columns_grad(second, hidden_grad, depth, up_rows, 0),
    )
    branch_other = swap_each(branch_own)
    attended_grad, proj_blocks = kernel_call(
        functools.partial(proj_back_kernel, depth, first_parts),
        [after(attended, *up_sum.keeps), *branch_own, *branch_other, *first_arrays],
        [WHOLE] + [ANYWHERE] * (2 * SHARES + len(first_arrays)),
        [shape_of((length, local), BF16), shape_of((2, 2, depth, up_rows, width // 4), BF16)],
        scratch=[
            proj_scratch[0],
            pltpu.VMEM((local, width // 2), F32),
            pltpu.VMEM((length, width), BF16),
            proj_scratch[1],
            dma((2 * SHARES,)),
        ],
    )
    pairs = local // (2 * head_size)
    groups = []

    def attend_next(*gates):
        k = len(groups)
        grads = after(attended_grad, *gates)
        groups.append(attend_back(queries, keys, values, grads, logs, turn, head_size, k, k + 1))
        return groups[-1][0]

    gate = attended_grad
    while len(groups) < pairs - 3:
        gate = attend_next(gate)
    gate = attend_next(down_sum.hop(1, gate))
    gate = attend_next(gate)
    gate = attend_next(down_sum.hop(2, gate), up_sum.arrived[0])
    mixed_pieces = [group[n] for n in range(3) for group in groups]

    def mixed_weight_grad(sent_number, *gates):
        block = (depth, up_rows, local)
        return (
            functools.partial(mixed_grad_kernel, depth, sent_number),
            [after(normed, *gates), *mixed_pieces, proj_blocks],
            [ANYWHERE] * (1 + len(mixed_pieces)) + [WHOLE],
            [shape_of(block, BF16)] * 4,
            [
                pltpu.VMEM((length, width), BF16),
                pltpu.VMEM((length, 3 * local), BF16),
                dma((2 * depth,)),
                dma((len(mixed_pieces),)),
            ],
        )

    ((one_far, one_near, two_far, two_near),) = merged_call(mixed_weight_grad(1, gate))
    now = (one_far,)
    fars = [swap(one_far, "y"), swap(two_far, "x")]
    gate = up_sum.hop(0, *now, down_sum.moving)
    (kept, *sent), keeps = merged_call(
        (
            functools.partial(mixed_back_kernel, depth, first_parts, len(mixed_pieces)),
            [after(mixed_pieces[0], gate, up_sum.arrived[1]), *mixed_pieces[1:], *first_arrays],
            [ANYWHERE] * (len(mixed_pieces) + len(first_arrays)),
            partial,
            [
                pltpu.VMEM((2, width, 3 * local // 2), BF16),
                pltpu.VMEM((length, 3 * local), BF16),
                dma((part_count,)),
                dma((len(mixed_pieces),)),
            ],
        ),
        mixed_weight_grad(0),
    )
    sent_other = swap_each([after(item, *fars, up_sum.moving) for item in sent])
    now = (keeps[0], *fars, up_sum.moving)
    fars = [add_blocks([(at(keep_one), ()), (arrived, ())]) for keep_one, arrived in zip(keeps[::2], fars)]
    lasts = [swap(fars[0], "x"), swap(fars[1], "y")]
    nears = [swap(after(one_near, *fars), "y"), swap(after(two_near, *fars), "x")]
    up_sum.hop(1, *now)
    (tokens_grad, first_sums), (kept, *sent) = merged_call(
        (
            tokens_back_kernel,
            [after(kept, *fars), tokens_own, middle_grad, params, *sent_other],
            [WHOLE] * (4 + SHARES),
            [shape_of((piece, width), BF16), shape_of((8, width), F32)],
            [],
        ),
        (
            functools.partial(down_kernel, depth, pair_parts),
            [active, *down_arrays],
            [WHOLE] + [ANYWHERE] * len(down_arrays),
            partial,
            down_scratch,
        ),
    )
    now = (tokens_grad, *lasts, *nears, up_sum.moving)
    keeps = keeps[1::2]
    moving = None

    def first_hop(n):
        arrays, specs = first_terms(keeps, nears, lasts, n)
        if moving is not None:
            arrays.append(moving)
            specs.append(same(block_kind.shape))
        arrays[0] = at(arrays[0])
        (total,) = kernel_call(
            hop_first_kernel, arrays, specs, [block_kind], grid=(1,), out_specs=[same(block_kind.shape)]
        )
        return total, ring(total, depth)

    sent_other = swap_each([at(item) for item in sent])
    (small,) = kernel_call(
        functools.partial(small_kernel, count, head_size, hidden_block, len(groups)),
        [at(first_sums), middle_sums, up_sums] + [group[3] for group in groups],
        [WHOLE] * (3 + len(groups)),
        [shape_of((count, ROW), F32)],
    )
    for n in range(1, depth):
        total, moving = first_hop(n)
        if n == 1:
            small = lax.all_to_all(after(small, total), everyone, split_axis=0, concat_axis=0, tiled=True)
            (block_out,) = kernel_call(
                out_kernel,
                [middle, after(kept, total, small), params, *sent_other],
                [WHOLE] * (3 + SHARES),
                [shape_of((piece, width), BF16)],
            )
            now = (moving, block_out, small)
        elif n == 2:
            block_traded = trade(after(block_out, total))
            tokens_traded = trade(after(tokens_grad, total))
            up_sum.hop(2, total)
            now = (moving, down_sum.finish(total), tokens_traded, block_traded)
        else:
            tokens_out = choose(tokens_grad, after(tokens_traded, total))
            block_done = choose(block_out, after(block_traded, total))
            now = (moving, up_sum.finish(total), tokens_out, block_done)
    arrays, specs = first_terms(keeps, nears, lasts, 0)
    arrays[0] = at(arrays[0])
    out_shapes = [
        shape_of((shard_rows, part_qkv), F32),
        shape_of((shard_rows, part_qkv), BF16),
        shape_of(proj_weight.shape, F32),
    ]
    mine, sent, grad_proj = kernel_call(
        finish_first_kernel,
        arrays + [moving],
        specs + [same(block_kind.shape)],
        out_shapes,
        grid=(1,),
        out_specs=[same(kind.shape) for kind in out_shapes],
        scratch=[pltpu.VMEM((2 * shard_rows, part_qkv), F32)],
    )
    (grad_qkv,) = kernel_call(
        join_heads_kernel,
        [mine, swap(sent, "core")],
        [WHOLE] * 2,
        [shape_of(qkv_weight.shape, F32)],
    )
    small = jnp.sum(small, axis=0)

    def rest_of(scatter):
        arrays, specs = [], []
        for array, prefix in scatter.rest():
            lead = tuple(prefix) + (0,) * (array.ndim - len(prefix) - 2)
            arrays.append(array)
            specs.append(
                pl.BlockSpec((1,) * len(lead) + array.shape[-2:], lambda i, lead=lead: lead + (0, 0))
            )
        return arrays, specs

    arrays, specs = rest_of(up_sum)
    out_shapes = [shape_of((shard_rows, part_up), F32), shape_of((shard_rows, part_up), BF16)]
    mine, sent = kernel_call(
        finish_up_kernel,
        arrays,
        specs,
        out_shapes,
        grid=(1,),
        out_specs=[same(kind.shape) for kind in out_shapes],
        scratch=[pltpu.VMEM((2 * shard_rows, part_up), F32)],
    )
    (grad_up,) = kernel_call(
        functools.partial(join_blocks_kernel, hidden_block),
        [mine, swap(sent, "core")],
        [WHOLE] * 2,
        [shape_of(up_weight.shape, F32)],
    )
    arrays, specs = rest_of(down_sum)
    (grad_down,) = kernel_call(
        finish_down_kernel,
        arrays,
        specs,
        [shape_of(down_weight.shape, F32)],
        grid=(1,),
        out_specs=[same(down_weight.shape)],
    )

    def part(begin, size):
        return small[begin : begin + size]

    return (
        block_done,
        tokens_out,
        part(0, EACH),
        part(EACH, EACH),
        grad_qkv,
        part(256, 3 * EACH),
        grad_proj,
        part(4 * EACH, EACH),
        part(2 * EACH, EACH),
        part(3 * EACH, EACH),
        grad_up,
        part(384, 4 * EACH),
        grad_down,
        part(5 * EACH, EACH),
    )


def solution(mesh):
    ctx_count = mesh.shape["ctx"]
    dp_count = mesh.shape["dp"]
    if ctx_count == 2 and dp_count % 4 == 0:
        mesh = Mesh(
            mesh.devices.reshape(dp_count // 4, 2, 2, 2), ("z", "x", "core", "y")
        )
        dp = ("z", "x", "core")
        ctx = "y"
        every = P(dp + (ctx,))
        body = fast_shards
    else:
        dp = "dp"
        ctx = "ctx"
        every = P((dp, ctx))
        body = shards
    rows = P(every[0], None)
    matrix = P(dp, ctx)
    return jax.shard_map(
        body,
        mesh=mesh,
        in_specs=(
            rows,
            every,
            every,
            every,
            every,
            every,
            matrix,
            every,
            matrix,
            every,
            every,
            every,
            matrix,
            every,
            matrix,
            every,
            rows,
        ),
        out_specs=(
            rows,
            rows,
            every,
            every,
            matrix,
            every,
            matrix,
            every,
            every,
            every,
            matrix,
            every,
            matrix,
            every,
        ),
        check_vma=False,
    )
```

```python
import functools
import math

import jax
import jax.numpy as jnp
from jax import lax
from jax.experimental import pallas as pl
from jax.experimental.pallas import tpu as pltpu
from jax.sharding import Mesh
from jax.sharding import PartitionSpec as P

HEADS = 16
SPAN = 256
LEAST_LEN = 1024


EPS = 1e-06


def norm_rows(values, gain_row, shift_row):
    row_mean = jnp.mean(values, axis=-1, keepdims=True)
    centred = values - row_mean
    variance = jnp.mean(centred * centred, axis=-1, keepdims=True)
    return centred * lax.rsqrt(variance + EPS) * gain_row + shift_row


def tables(frames, patch_rows, patch_columns, head_size):
    section = 2 * (head_size // 3 // 2)
    half_size = section // 2
    frequency = 1.0 / 10000.0 ** (jnp.arange(half_size).astype(jnp.float32) / half_size)
    cosines = []
    sines = []
    for place in (frames, patch_rows, patch_columns):
        angles = place.astype(jnp.float32)[..., None] * frequency
        cosines = cosines + [jnp.cos(angles), jnp.cos(angles)]
        sines = sines + [jnp.sin(angles), jnp.sin(angles)]
    spare = head_size - 3 * section
    cosines.append(jnp.ones(frames.shape + (spare,), jnp.float32))
    sines.append(jnp.zeros(frames.shape + (spare,), jnp.float32))
    return (jnp.concatenate(cosines, axis=-1), jnp.concatenate(sines, axis=-1))


def turn_half(values):
    head_size = values.shape[-1]
    section = 2 * (head_size // 3 // 2)
    half_size = section // 2
    pieces = []
    for part_number in range(3):
        begin = part_number * section
        pieces.append(-values[..., begin + half_size : begin + section])
        pieces.append(values[..., begin : begin + half_size])
    pieces.append(jnp.zeros_like(values[..., 3 * section :]))
    return jnp.concatenate(pieces, axis=-1)


def rotary(values, cosine_table, sine_table):
    return values * cosine_table + turn_half(values) * sine_table


def rotary_back(values, cosine_table, sine_table):
    return values * cosine_table - turn_half(values * sine_table)


def shards(
    tokens,
    frame_index,
    row_index,
    column_index,
    norm1_gain,
    norm1_bias,
    qkv_weight,
    qkv_bias,
    proj_weight,
    proj_bias,
    norm2_gain,
    norm2_bias,
    up_weight,
    up_bias,
    down_weight,
    down_bias,
    cotangent,
):
    ctx_count = lax.axis_size("ctx")
    clip_length = max(LEAST_LEN, SPAN * ctx_count)
    piece_rows = clip_length // ctx_count
    rows_here, model_width = tokens.shape
    clip_count = rows_here // piece_rows
    head_size = model_width // HEADS
    score_scale = head_size ** (-0.5)
    head_shape = (clip_count, piece_rows, HEADS, head_size)
    long_shape = (clip_count, clip_length, HEADS, head_size)
    flat_shape = (clip_count, piece_rows, model_width)

    def gather_all():
        partial_value = (
            lax.all_gather(qkv_weight, "ctx", axis=1, tiled=True),
            lax.all_gather(proj_weight, "ctx", axis=1, tiled=True),
            lax.all_gather(up_weight, "ctx", axis=1, tiled=True),
            lax.all_gather(down_weight, "ctx", axis=1, tiled=True),
            lax.all_gather(norm1_gain, "ctx", axis=0, tiled=True),
            lax.all_gather(norm1_bias, "ctx", axis=0, tiled=True),
            lax.all_gather(qkv_bias, "ctx", axis=0, tiled=True),
            lax.all_gather(proj_bias, "ctx", axis=0, tiled=True),
            lax.all_gather(norm2_gain, "ctx", axis=0, tiled=True),
            lax.all_gather(norm2_bias, "ctx", axis=0, tiled=True),
            lax.all_gather(up_bias, "ctx", axis=0, tiled=True),
            lax.all_gather(down_bias, "ctx", axis=0, tiled=True),
        )
        return (
            lax.all_gather(partial_value[0], "dp", axis=0, tiled=True),
            lax.all_gather(partial_value[1], "dp", axis=0, tiled=True),
            lax.all_gather(partial_value[2], "dp", axis=0, tiled=True),
            lax.all_gather(partial_value[3], "dp", axis=0, tiled=True),
            lax.all_gather(partial_value[4], "dp", axis=0, tiled=True),
            lax.all_gather(partial_value[5], "dp", axis=0, tiled=True),
            lax.all_gather(partial_value[6], "dp", axis=0, tiled=True),
            lax.all_gather(partial_value[7], "dp", axis=0, tiled=True),
            lax.all_gather(partial_value[8], "dp", axis=0, tiled=True),
            lax.all_gather(partial_value[9], "dp", axis=0, tiled=True),
            lax.all_gather(partial_value[10], "dp", axis=0, tiled=True),
            lax.all_gather(partial_value[11], "dp", axis=0, tiled=True),
        )

    gathered = gather_all()
    (
        w_qkv,
        w_proj,
        w_up,
        w_down,
        gain_one,
        shift_one,
        bias_qkv,
        bias_proj,
        gain_two,
        shift_two,
        bias_up,
        bias_down,
    ) = gathered
    block_in = tokens.astype(jnp.float32).reshape(flat_shape)
    cosine_table, sine_table = tables(
        frame_index.reshape(clip_count, piece_rows),
        row_index.reshape(clip_count, piece_rows),
        column_index.reshape(clip_count, piece_rows),
        head_size,
    )
    cosine_table = cosine_table[:, :, None, :]
    sine_table = sine_table[:, :, None, :]
    normed = norm_rows(
        block_in, gain_one.astype(jnp.float32), shift_one.astype(jnp.float32)
    ).astype(jnp.bfloat16)
    projected = jnp.einsum(
        "spd,de->spe", normed, w_qkv, preferred_element_type=jnp.float32
    ) + bias_qkv.astype(jnp.float32)
    queries = rotary(
        projected[..., :model_width].reshape(head_shape), cosine_table, sine_table
    ).astype(jnp.bfloat16)
    keys_own = (
        rotary(
            projected[..., model_width : 2 * model_width].reshape(head_shape),
            cosine_table,
            sine_table,
        )
        .astype(jnp.bfloat16)
        .reshape(flat_shape)
    )
    values_own = projected[..., 2 * model_width :].astype(jnp.bfloat16)
    keys_all, values_all = (
        lax.all_gather(keys_own, "ctx", axis=1, tiled=True),
        lax.all_gather(values_own, "ctx", axis=1, tiled=True),
    )
    keys_all = keys_all.reshape(long_shape)
    values_all = values_all.reshape(long_shape)

    def head_forward(head_number):
        query_head = lax.dynamic_index_in_dim(queries, head_number, 2, keepdims=False)
        key_head = lax.dynamic_index_in_dim(keys_all, head_number, 2, keepdims=False)
        value_head = lax.dynamic_index_in_dim(values_all, head_number, 2, keepdims=False)
        scores = (
            jnp.einsum("sqd,skd->sqk", query_head, key_head, preferred_element_type=jnp.float32)
            * score_scale
        )
        row_top = jnp.max(scores, axis=-1, keepdims=True)
        weights = jnp.exp(scores - row_top)
        row_total = jnp.sum(weights, axis=-1, keepdims=True)
        weights_low = (weights / row_total).astype(jnp.bfloat16)
        result = jnp.einsum(
            "sqk,skd->sqd", weights_low, value_head, preferred_element_type=jnp.float32
        )
        return (result, (row_top + jnp.log(row_total))[..., 0])

    head_numbers = jnp.arange(HEADS, dtype=jnp.int32)
    attended, log_total = lax.map(head_forward, head_numbers)
    attended_low = jnp.transpose(attended, (1, 2, 0, 3)).reshape(flat_shape).astype(jnp.bfloat16)
    branch = jnp.einsum(
        "spd,de->spe", attended_low, w_proj, preferred_element_type=jnp.float32
    ) + bias_proj.astype(jnp.float32)
    middle = block_in + branch
    second = norm_rows(middle, gain_two.astype(jnp.float32), shift_two.astype(jnp.float32)).astype(
        jnp.bfloat16
    )
    hidden = jnp.einsum(
        "spd,df->spf", second, w_up, preferred_element_type=jnp.float32
    ) + bias_up.astype(jnp.float32)
    active = jax.nn.gelu(hidden, approximate=False).astype(jnp.bfloat16)
    output = jnp.einsum(
        "spf,fd->spd", active, w_down, preferred_element_type=jnp.float32
    ) + bias_down.astype(jnp.float32)
    block_out = (middle + output).astype(jnp.bfloat16).reshape(rows_here, model_width)
    backward_weights = gather_all()
    (
        w_qkv,
        w_proj,
        w_up,
        w_down,
        gain_one,
        shift_one,
        bias_qkv,
        bias_proj,
        gain_two,
        shift_two,
        bias_up,
        bias_down,
    ) = backward_weights
    out_low = cotangent.reshape(flat_shape)
    out_grad = out_low.astype(jnp.float32)
    grad_down_bias = jnp.sum(out_grad, axis=(0, 1))
    grad_down = jnp.einsum("spf,spd->fd", active, out_low, preferred_element_type=jnp.float32)
    active_grad = jnp.einsum("spd,fd->spf", out_low, w_down, preferred_element_type=jnp.float32)
    gelu_pull = jax.vjp(lambda inner: jax.nn.gelu(inner, approximate=False), hidden)[1]
    hidden_grad = gelu_pull(active_grad)[0].astype(jnp.bfloat16)
    grad_up_bias = jnp.sum(hidden_grad.astype(jnp.float32), axis=(0, 1))
    grad_up = jnp.einsum("spd,spf->df", second, hidden_grad, preferred_element_type=jnp.float32)
    second_grad = jnp.einsum("spf,df->spd", hidden_grad, w_up, preferred_element_type=jnp.float32)
    second_pull = jax.vjp(
        norm_rows, middle, gain_two.astype(jnp.float32), shift_two.astype(jnp.float32)
    )[1]
    middle_part, grad_gain_two, grad_shift_two = second_pull(second_grad)
    middle_grad = out_grad + middle_part
    branch_low = middle_grad.astype(jnp.bfloat16)
    grad_proj_bias = jnp.sum(branch_low.astype(jnp.float32), axis=(0, 1))
    grad_proj = jnp.einsum(
        "spd,spe->de", attended_low, branch_low, preferred_element_type=jnp.float32
    )
    attended_grad = (
        jnp.einsum("spe,de->spd", branch_low, w_proj, preferred_element_type=jnp.float32)
        .astype(jnp.bfloat16)
        .reshape(head_shape)
    )

    def head_backward(head_number):
        query_head = lax.dynamic_index_in_dim(queries, head_number, 2, keepdims=False)
        key_head = lax.dynamic_index_in_dim(keys_all, head_number, 2, keepdims=False)
        value_head = lax.dynamic_index_in_dim(values_all, head_number, 2, keepdims=False)
        grad_head = lax.dynamic_index_in_dim(attended_grad, head_number, 2, keepdims=False)
        log_head = lax.dynamic_index_in_dim(log_total, head_number, 0, keepdims=False)
        scores = (
            jnp.einsum("sqd,skd->sqk", query_head, key_head, preferred_element_type=jnp.float32)
            * score_scale
        )
        weights = jnp.exp(scores - log_head[..., None])
        weights_low = weights.astype(jnp.bfloat16)
        value_grad = jnp.einsum(
            "sqk,sqd->skd", weights_low, grad_head, preferred_element_type=jnp.float32
        )
        weight_grad = jnp.einsum(
            "sqd,skd->sqk", grad_head, value_head, preferred_element_type=jnp.float32
        )
        score_grad = (
            weights * (weight_grad - jnp.sum(weights * weight_grad, axis=-1, keepdims=True))
        ).astype(jnp.bfloat16)
        query_grad = (
            jnp.einsum("sqk,skd->sqd", score_grad, key_head, preferred_element_type=jnp.float32)
            * score_scale
        )
        key_grad = (
            jnp.einsum("sqk,sqd->skd", score_grad, query_head, preferred_element_type=jnp.float32)
            * score_scale
        )
        return (query_grad, key_grad, value_grad)

    query_grads, key_grads, value_grads = lax.map(head_backward, head_numbers)
    key_full = jnp.transpose(key_grads, (1, 2, 0, 3)).reshape(clip_count, clip_length, model_width)
    value_full = jnp.transpose(value_grads, (1, 2, 0, 3)).reshape(
        clip_count, clip_length, model_width
    )
    key_part, value_part = (
        lax.psum_scatter(
            key_full.astype(jnp.bfloat16), "ctx", scatter_dimension=1, tiled=True
        ).astype(jnp.float32),
        lax.psum_scatter(
            value_full.astype(jnp.bfloat16), "ctx", scatter_dimension=1, tiled=True
        ).astype(jnp.float32),
    )
    query_grads = jnp.transpose(query_grads, (1, 2, 0, 3))
    query_back = rotary_back(query_grads, cosine_table, sine_table).reshape(flat_shape)
    key_back = rotary_back(key_part.reshape(head_shape), cosine_table, sine_table).reshape(
        flat_shape
    )
    mixed_grad = jnp.concatenate([query_back, key_back, value_part], axis=-1).astype(jnp.bfloat16)
    grad_qkv_bias = jnp.sum(mixed_grad.astype(jnp.float32), axis=(0, 1))
    grad_qkv = jnp.einsum("spd,spe->de", normed, mixed_grad, preferred_element_type=jnp.float32)
    normed_grad = jnp.einsum("spe,de->spd", mixed_grad, w_qkv, preferred_element_type=jnp.float32)
    first_pull = jax.vjp(
        norm_rows, block_in, gain_one.astype(jnp.float32), shift_one.astype(jnp.float32)
    )[1]
    input_part, grad_gain_one, grad_shift_one = first_pull(normed_grad)
    tokens_grad = (middle_grad + input_part).astype(jnp.bfloat16).reshape(rows_here, model_width)
    summed = (
        lax.psum_scatter(
            grad_qkv.astype(jnp.bfloat16), "dp", scatter_dimension=0, tiled=True
        ).astype(jnp.float32),
        lax.psum_scatter(
            grad_proj.astype(jnp.bfloat16), "dp", scatter_dimension=0, tiled=True
        ).astype(jnp.float32),
        lax.psum_scatter(
            grad_up.astype(jnp.bfloat16), "dp", scatter_dimension=0, tiled=True
        ).astype(jnp.float32),
        lax.psum_scatter(
            grad_down.astype(jnp.bfloat16), "dp", scatter_dimension=0, tiled=True
        ).astype(jnp.float32),
        lax.psum_scatter(
            grad_gain_one.astype(jnp.bfloat16), "dp", scatter_dimension=0, tiled=True
        ).astype(jnp.float32),
        lax.psum_scatter(
            grad_shift_one.astype(jnp.bfloat16), "dp", scatter_dimension=0, tiled=True
        ).astype(jnp.float32),
        lax.psum_scatter(
            grad_qkv_bias.astype(jnp.bfloat16), "dp", scatter_dimension=0, tiled=True
        ).astype(jnp.float32),
        lax.psum_scatter(
            grad_proj_bias.astype(jnp.bfloat16), "dp", scatter_dimension=0, tiled=True
        ).astype(jnp.float32),
        lax.psum_scatter(
            grad_gain_two.astype(jnp.bfloat16), "dp", scatter_dimension=0, tiled=True
        ).astype(jnp.float32),
        lax.psum_scatter(
            grad_shift_two.astype(jnp.bfloat16), "dp", scatter_dimension=0, tiled=True
        ).astype(jnp.float32),
        lax.psum_scatter(
            grad_up_bias.astype(jnp.bfloat16), "dp", scatter_dimension=0, tiled=True
        ).astype(jnp.float32),
        lax.psum_scatter(
            grad_down_bias.astype(jnp.bfloat16), "dp", scatter_dimension=0, tiled=True
        ).astype(jnp.float32),
    )
    owned = (
        lax.psum_scatter(
            summed[0].astype(jnp.bfloat16), "ctx", scatter_dimension=1, tiled=True
        ).astype(jnp.float32),
        lax.psum_scatter(
            summed[1].astype(jnp.bfloat16), "ctx", scatter_dimension=1, tiled=True
        ).astype(jnp.float32),
        lax.psum_scatter(
            summed[2].astype(jnp.bfloat16), "ctx", scatter_dimension=1, tiled=True
        ).astype(jnp.float32),
        lax.psum_scatter(
            summed[3].astype(jnp.bfloat16), "ctx", scatter_dimension=1, tiled=True
        ).astype(jnp.float32),
        lax.psum_scatter(
            summed[4].astype(jnp.bfloat16), "ctx", scatter_dimension=0, tiled=True
        ).astype(jnp.float32),
        lax.psum_scatter(
            summed[5].astype(jnp.bfloat16), "ctx", scatter_dimension=0, tiled=True
        ).astype(jnp.float32),
        lax.psum_scatter(
            summed[6].astype(jnp.bfloat16), "ctx", scatter_dimension=0, tiled=True
        ).astype(jnp.float32),
        lax.psum_scatter(
            summed[7].astype(jnp.bfloat16), "ctx", scatter_dimension=0, tiled=True
        ).astype(jnp.float32),
        lax.psum_scatter(
            summed[8].astype(jnp.bfloat16), "ctx", scatter_dimension=0, tiled=True
        ).astype(jnp.float32),
        lax.psum_scatter(
            summed[9].astype(jnp.bfloat16), "ctx", scatter_dimension=0, tiled=True
        ).astype(jnp.float32),
        lax.psum_scatter(
            summed[10].astype(jnp.bfloat16), "ctx", scatter_dimension=0, tiled=True
        ).astype(jnp.float32),
        lax.psum_scatter(
            summed[11].astype(jnp.bfloat16), "ctx", scatter_dimension=0, tiled=True
        ).astype(jnp.float32),
    )
    return (
        block_out,
        tokens_grad,
        owned[4],
        owned[5],
        owned[0],
        owned[6],
        owned[1],
        owned[7],
        owned[8],
        owned[9],
        owned[2],
        owned[10],
        owned[3],
        owned[11],
    )


LOG2E = 1.4426950408889634
COST = 0.001
NT = (((1,), (1,)), ((), ()))
NN = (((1,), (0,)), ((), ()))
TN = (((0,), (0,)), ((), ()))
F32 = jnp.float32
BF16 = jnp.bfloat16
SWAP = [(0, 1), (1, 0)]
DIAGONAL = [(1, 2), (2, 1)]
ANYWHERE = pl.BlockSpec(memory_space=pl.ANY)
WHOLE = pl.BlockSpec(memory_space=pltpu.VMEM)
SHARES = 1
LINES = 128
SCALARS = pl.BlockSpec(memory_space=pltpu.SMEM)


def shape_of(shape, kind):
    return jax.ShapeDtypeStruct(shape, kind)


def half_lanes(number, shape):
    lane = lax.broadcasted_iota(jnp.int32, shape, 1)
    width = shape[1] // 2
    return (lane < width) if number == 0 else (lane >= width)


def keep(mask, values):
    return jnp.where(mask, values, jnp.zeros_like(values))


def dot(first, second, dims, to=F32):
    return lax.dot_general(first, second, dims, preferred_element_type=F32).astype(to)


def kernel_call(
    body, inputs, in_specs, out_shapes, scratch=(), grid=None, out_specs=None, flops=0, exps=0, room=8
):
    def size(item):
        return item.size * item.dtype.itemsize

    total = sum(size(a) for a in inputs) + sum(size(s) for s in out_shapes)
    if out_specs is None:
        out_specs = [WHOLE] * len(out_shapes)
    need = room << 20
    if grid is None:
        need += sum(size(a) for a, spec in zip(inputs, in_specs) if spec is WHOLE)
        need += sum(size(a) for a, spec in zip(out_shapes, out_specs) if spec is WHOLE)
    for item in scratch:
        if getattr(item, "memory_space", None) == pltpu.VMEM:
            need += math.prod(item.shape) * jnp.dtype(item.dtype).itemsize
    extra = {} if grid is None else {"grid": grid}
    return pl.pallas_call(
        body,
        in_specs=in_specs,
        out_specs=out_specs,
        out_shape=out_shapes,
        scratch_shapes=list(scratch),
        compiler_params=pltpu.CompilerParams(vmem_limit_bytes=min(need, 56 << 20)),
        cost_estimate=pl.CostEstimate(
            flops=int(flops * COST),
            bytes_accessed=int(total * COST),
            transcendentals=int(exps * COST),
        ),
        **extra,
    )(*inputs)


def merged_call(*steps, room=8):
    counts = [(len(a), len(o), len(c)) for _, a, _, o, c in steps]
    inputs = sum(c[0] for c in counts)
    outs = sum(c[1] for c in counts)

    def body(*refs):
        i, o, c = 0, inputs, inputs + outs
        for (step_body, *_), (ni, no, nc) in zip(steps, counts):
            step_body(*refs[i : i + ni], *refs[o : o + no], *refs[c : c + nc])
            i, o, c = i + ni, o + no, c + nc

    found = kernel_call(
        body,
        [a for step in steps for a in step[1]],
        [a for step in steps for a in step[2]],
        [a for step in steps for a in step[3]],
        scratch=[a for step in steps for a in step[4]],
        room=room,
    )
    results = []
    for _, no, _ in counts:
        results.append(found[:no])
        found = found[no:]
    return results


def after(values, *others):
    return lax.optimization_barrier((values,) + others)[0]


def swap(values, axis):
    return lax.ppermute(values, axis, SWAP)


def swap_each(pieces):
    return [swap(piece, "core") for piece in pieces]


def put_rows(refs, columns, value):
    rows = refs[0].shape[0]
    for k, ref in enumerate(refs):
        ref[:, columns] = value[k * rows : (k + 1) * rows].astype(ref.dtype)


def ring(values, depth):
    return lax.ppermute(values, "z", [(i, (i + 1) % depth) for i in range(depth)])


def place(depth, z, x):
    z_number = lax.rem(lax.axis_index("z") + (depth - z), depth)
    return 2 * z_number + lax.rem(lax.axis_index("x") + x, 2)


def y_place(y):
    return lax.rem(lax.axis_index("y") + y, 2)


def start_copies(pairs, sems):
    copies = [pltpu.make_async_copy(a, b, sems.at[n]) for n, (a, b) in enumerate(pairs)]
    for copy in copies:
        copy.start()
    return copies


def join_kernel(spans, *refs):
    out_ref, sems = refs[-2:]
    pairs = []
    spot = 0
    for n, begin, count in spans:
        pairs.append((refs[n].at[pl.ds(begin, count)], out_ref.at[pl.ds(spot, count)]))
        spot += count
    for copy in start_copies(pairs, sems):
        copy.wait()


def join(arrays, spans):
    total = sum(span[2] for span in spans)
    (out,) = kernel_call(
        functools.partial(join_kernel, spans),
        arrays,
        [ANYWHERE] * len(arrays),
        [shape_of((total,) + arrays[0].shape[1:], arrays[0].dtype)],
        out_specs=[ANYWHERE],
        scratch=[pltpu.SemaphoreType.DMA((len(spans),))],
    )
    return out


def choose_kernel(own_ref, other_ref, out_ref, sem):
    stays = lax.axis_index("core") == lax.axis_index("y")

    @pl.when(stays)
    def _():
        copy = pltpu.make_async_copy(own_ref, out_ref, sem)
        copy.start()
        copy.wait()

    @pl.when(jnp.logical_not(stays))
    def _():
        copy = pltpu.make_async_copy(other_ref, out_ref, sem)
        copy.start()
        copy.wait()


def trade(values):
    return lax.ppermute(values, ("core", "y"), DIAGONAL)


def choose(own, other):
    (out,) = kernel_call(
        choose_kernel,
        [own, other],
        [ANYWHERE] * 2,
        [shape_of(own.shape, own.dtype)],
        scratch=[pltpu.SemaphoreType.DMA],
    )
    return out


def add_kernel(*refs):
    total = None
    for ref in refs[:-1]:
        value = ref[(0,) * (len(ref.shape) - 2)].astype(F32)
        total = value if total is None else total + value
    refs[-1][0] = total.astype(refs[-1].dtype)


def add_blocks(terms, kind=BF16):
    array, prefix = terms[0]
    number, rows, columns = array.shape[len(prefix) :]

    def spec(prefix):
        return pl.BlockSpec((1,) * len(prefix) + (1, rows, columns), lambda i: prefix + (i, 0, 0))

    (out,) = kernel_call(
        add_kernel,
        [array for array, _ in terms],
        [spec(tuple(prefix)) for _, prefix in terms],
        [shape_of((number, rows, columns), kind)],
        grid=(number,),
        out_specs=[spec(())],
    )
    return out


def near_first(depth):
    order = [i % depth for i in range(1, depth + 1)]
    split = max(depth // 2, 1)
    return order[:split], order[split:]


class Scatter:
    def __init__(self, sends, first, last, depth):
        self.sends = sends
        self.arrived = []
        self.first = first
        self.last = last
        self.depth = depth
        self.spots = [(g, k) for g, group in enumerate(near_first(depth)) for k in range(len(group))]
        self.moving = None

    def send(self, *gates):
        block = after(self.sends[len(self.arrived)], *gates)
        self.arrived.append(swap(block, self.first))
        return self.arrived[-1]

    def terms(self, step):
        g, k = self.spots[step]
        found = [(self.keeps[g], (k,)), (self.arrived[g], (k,))]
        if self.moving is not None:
            found.append((self.moving, ()))
        return found

    def hop(self, step, *gates):
        terms = self.terms(step)
        terms[0] = (after(terms[0][0], *gates), terms[0][1])
        total = add_blocks(terms)
        self.moving = ring(total, self.depth)
        return total

    def finish(self, *gates):
        found = self.terms(self.depth - 1)
        found[0] = (after(found[0][0], *gates), found[0][1])
        far, near = [], []
        for array, prefix in found:
            rows, columns = array.shape[-2:]
            lead = 1
            for size in array.shape[:-2]:
                lead *= size
            begin = prefix[0] * 2 if prefix else 0
            flat = array.reshape(lead, 1, rows, columns)
            far.append((flat, (begin + 1,)))
            near.append((flat, (begin,)))
        total = add_blocks(far)
        self.near = near
        self.other = swap(total, self.last)
        return total

    def rest(self):
        return self.near + [(self.other, ())]


def turned(values, cosine, before, after):
    wide = cosine.shape[1]
    pieces = []
    for begin in range(0, values.shape[1], wide):
        piece = values[:, begin : begin + wide]
        pieces.append(
            piece * cosine
            + pltpu.roll(piece, wide - HALF, 1) * before
            + pltpu.roll(piece, HALF, 1) * after
        )
    return pieces


def turned_back(piece, cosine, before, after):
    wide = cosine.shape[1]
    return (
        piece * cosine
        + pltpu.roll(piece * before, HALF, 1)
        + pltpu.roll(piece * after, wide - HALF, 1)
    )


def normal(values):
    mean = jnp.mean(values, axis=-1, keepdims=True)
    centred = values - mean
    variance = jnp.mean(centred * centred, axis=-1, keepdims=True)
    inverse = lax.rsqrt(variance + EPS)
    return centred * inverse, inverse


def qkv_kernel(depth, parts, own_ref, other_ref, rows_ref, bias_ref,
               cosine_ref, before_ref, after_ref, *rest):
    count = 1 + max(p[0] for p in parts)
    arrays = rest[:count]
    normed_ref, query_ref, key_ref, value_ref, weight, sems = rest[count:]
    pairs = []
    rows = arrays[0].shape[1]
    wide = query_ref.shape[1]
    thin = wide // 2
    for n, i, half, z, x, y in parts:
        spot = pl.ds(pl.multiple_of(place(depth, z, x) * rows, rows), rows)
        y_spot = y_place(y)
        if half == 0:
            pairs.append((arrays[n].at[i], weight.at[y_spot, spot, pl.ds(0, wide)]))
        else:
            pairs.append((arrays[n].at[i, :, pl.ds(0, thin)], weight.at[y_spot, spot, pl.ds(wide, thin)]))
    copies = start_copies(pairs, sems)
    piece = own_ref.shape[0]
    for ref, base in ((own_ref, 0), (other_ref, piece)):
        for begin in range(0, piece, 256):
            hat, _ = normal(ref[pl.ds(begin, 256), :].astype(F32))
            normed_ref[pl.ds(base + begin, 256), :] = (hat * rows_ref[0:1, :] + rows_ref[1:2, :]).astype(BF16)
    for copy in copies:
        copy.wait()
    outs = [(query_ref, 0), (query_ref, thin), (key_ref, 0), (key_ref, thin), (value_ref, 0), (value_ref, thin)]
    for number, (ref, column) in enumerate(outs):
        y, spot = divmod(number, 3)
        for begin in range(0, 2 * piece, piece):
            lines = pl.ds(begin, piece)
            result = dot(normed_ref[lines, :], weight[y, :, pl.ds(spot * thin, thin)], NN)
            result = result + bias_ref[:, pl.ds(number * thin, thin)]
            if ref is value_ref:
                ref[lines, pl.ds(column, thin)] = result.astype(BF16)
            else:
                pieces = turned(result, cosine_ref[lines, :], before_ref[lines, :], after_ref[lines, :])
                for k, item in enumerate(pieces):
                    ref[lines, pl.ds(column + k * 128, 128)] = item.astype(BF16)


def attend_kernel(query_ref, key_ref, value_ref, out_ref, log_ref, *, block, scale):
    length, width = key_ref.shape
    keys = key_ref[...]
    values = value_ref[...]
    for number in range(2):
        mask = half_lanes(number, (length, width))
        key_half = keep(mask, keys)
        value_half = keep(mask, values)
        for start in range(0, length, block):
            rows = pl.ds(start, block)
            scores = dot(query_ref[rows, :], key_half, NT)
            top = jnp.max(scores, axis=1, keepdims=True)
            weights = jnp.exp2((scores - top) * scale)
            total = jnp.sum(weights, axis=1, keepdims=True)
            part = (dot(weights.astype(BF16), value_half, NN) / total).astype(BF16)
            if number == 0:
                out_ref[rows, :] = part
            else:
                out_ref[rows, :] = out_ref[rows, :] + part
            logs = top * scale + jnp.log2(total)
            turned_logs = jnp.transpose(jnp.broadcast_to(logs, (block, 128)))
            log_ref[0, number : number + 1, rows] = turned_logs[0:1, :]


def attend(queries, keys, values, head_size):
    length, width = queries.shape
    wide = 2 * head_size
    pairs = width // wide
    spec = pl.BlockSpec((length, wide), lambda i: (0, i))
    return kernel_call(
        functools.partial(attend_kernel, block=512, scale=LOG2E * head_size**-0.5),
        [queries, keys, values],
        [spec] * 3,
        [shape_of((length, width), BF16), shape_of((pairs, 2, length), F32)],
        grid=(pairs,),
        out_specs=[spec, pl.BlockSpec((1, 2, length), lambda i: (i, 0, 0))],
        flops=16 * length * length * width,
        exps=2 * pairs * length * length,
        room=28,
    )


def attend_back_kernel(
    query_ref, key_ref, value_ref, grad_ref, log_ref, cosine_ref, before_ref, after_ref,
    query_out, key_out, value_out, sum_out, key_sum, value_sum, query_sum, *, block, scale,
):
    length, width = key_ref.shape
    keys = key_ref[...]
    values = value_ref[...]
    for number in range(2):
        mask = half_lanes(number, (length, width))
        key_half = keep(mask, keys)
        value_half = keep(mask, values)
        block_mask = half_lanes(number, (block, width))
        for start in range(0, length, block):
            rows = pl.ds(start, block)
            query = query_ref[rows, :]
            grad = grad_ref[rows, :]
            scores = dot(key_half, query, NT)
            probs = jnp.exp2(scores * (scale * LOG2E) - log_ref[0, number : number + 1, rows])
            prob_grad = dot(value_half, grad, NT)
            mean = jnp.sum(probs * prob_grad, axis=0, keepdims=True)
            score_grad = (probs * (prob_grad - mean)).astype(BF16)
            value_part = dot(probs.astype(BF16), keep(block_mask, grad), NN)
            key_part = dot(score_grad, keep(block_mask, query), NN)
            query_part = dot(score_grad, key_half, TN)
            if number == 0 and start == 0:
                value_sum[...] = value_part
                key_sum[...] = key_part
            else:
                value_sum[...] += value_part
                key_sum[...] += key_part
            if number == 0:
                query_sum[rows, :] = query_part
            else:
                query_sum[rows, :] += query_part
    tables_here = (cosine_ref[...], before_ref[...], after_ref[...])
    for slot, (ref, value) in enumerate(
        (
            (query_out, turned_back(query_sum[...] * scale, *tables_here)),
            (key_out, turned_back(key_sum[...] * scale, *tables_here)),
            (value_out, value_sum[...]),
        )
    ):
        low = value.astype(BF16)
        ref[...] = low
        sum_out[slot : slot + 1, :] = jnp.sum(low.astype(F32), axis=0, keepdims=True)


def attend_back(queries, keys, values, grads, logs, turn, head_size, begin, end):
    length = queries.shape[0]
    wide = 2 * head_size
    width = (end - begin) * wide
    spec = pl.BlockSpec((length, wide), lambda i: (0, begin + i))
    out_spec = pl.BlockSpec((length, wide), lambda i: (0, i))
    whole = pl.BlockSpec((length, wide), lambda i: (0, 0))
    return kernel_call(
        functools.partial(attend_back_kernel, block=1024, scale=head_size**-0.5),
        [queries, keys, values, grads, logs, *turn],
        [spec] * 4 + [pl.BlockSpec((1, 2, length), lambda i: (begin + i, 0, 0))] + [whole] * 3,
        [shape_of((length, width), BF16)] * 3 + [shape_of((8, width), F32)],
        grid=(end - begin,),
        out_specs=[out_spec] * 3 + [pl.BlockSpec((8, wide), lambda i: (0, i))],
        scratch=[pltpu.VMEM((length, wide), F32)] * 3,
        flops=40 * length * length * width,
        exps=(end - begin) * 2 * length * length,
        room=28,
    )


def load_proj(depth, parts, arrays, weight, sems):
    pairs = []
    group = arrays[0].shape[1] // 2
    thin = weight.shape[2] // 2
    for n, i, half, z, x, y in parts:
        if half == 0:
            continue
        spot = pl.ds(pl.multiple_of(place(depth, z, x) * group, group), group)
        y_spot = y_place(y)
        for k in range(2):
            pairs.append(
                (
                    arrays[n].at[i, pl.ds(k * group, group), pl.ds(2 * thin - thin, thin)],
                    weight.at[y_spot, spot, pl.ds(k * thin, thin)],
                )
            )
    return start_copies(pairs, sems)


def proj_kernel(depth, parts, attended_ref, *rest):
    count = 1 + max(p[0] for p in parts)
    arrays = rest[:count]
    keep_ref, *sends = rest[count:-2]
    weight, sems = rest[-2:]
    piece, width = keep_ref.shape
    for copy in load_proj(depth, parts, arrays, weight, sems):
        copy.wait()
    half = width // 2
    for y in range(2):
        columns = pl.ds(y * half, half)
        put_rows(sends, columns, dot(attended_ref[pl.ds(piece, piece), :], weight[y], NN))
    for y in range(2):
        columns = pl.ds(y * half, half)
        keep_ref[:, columns] = dot(attended_ref[pl.ds(0, piece), :], weight[y], NN)


def proj_back_kernel(depth, parts, attended_ref, *rest):
    halves, rest = rest[: 2 * SHARES], rest[2 * SHARES :]
    count = 1 + max(p[0] for p in parts)
    arrays = rest[:count]
    out_ref, blocks_ref, weight, scratch, branch, sems, branch_sems = rest[count:]
    copies = start_copies(
        [(ref, branch.at[pl.ds(n * ref.shape[0], ref.shape[0])]) for n, ref in enumerate(halves)], branch_sems
    )
    copies += load_proj(depth, parts, arrays, weight, sems)
    for copy in copies:
        copy.wait()
    length, width = branch.shape
    group = blocks_ref.shape[3] // 2
    thin = blocks_ref.shape[4]
    for y_near in range(2):
        columns = pl.ds(pl.multiple_of(y_place(y_near) * 2 * thin, 128), 2 * thin)
        scratch[...] = dot(attended_ref[...], branch[:, columns], TN)
        for x in range(2):
            for z in range(depth):
                spot = pl.ds(pl.multiple_of(place(depth, z, x) * group, group), group)
                block = scratch[spot, :].astype(BF16)
                for k in range(2):
                    blocks_ref[x, y_near, z, pl.ds(k * group, group), :] = block[:, k * thin : (k + 1) * thin]
    half = width // 2
    for begin in range(0, length, length // 2):
        rows = pl.ds(begin, length // 2)
        total = dot(branch[rows, pl.ds(0, half)], weight[0], NT) + dot(branch[rows, pl.ds(half, half)], weight[1], NT)
        out_ref[rows, :] = total.astype(BF16)


def middle_kernel(own_ref, keep_ref, rows_ref, *rest):
    others, (middle_ref, *seconds) = rest[:SHARES], rest[SHARES:]
    size = others[0].shape[0]
    for begin in range(0, SHARES * size, LINES):
        k = begin // size
        rows = pl.ds(begin, LINES)
        lines = pl.ds(begin % size, LINES)
        middle = own_ref[rows, :].astype(F32) + keep_ref[rows, :] + others[k][lines, :].astype(F32) + rows_ref[4:5, :]
        middle_ref[rows, :] = middle
        hat, _ = normal(middle)
        seconds[k][lines, :] = (hat * rows_ref[2:3, :] + rows_ref[3:4, :]).astype(BF16)


def load_up(depth, parts, arrays, weight, sems):
    pairs = []
    rows, wide = arrays[0].shape[1:]
    for n, i, half, z, x, y in parts:
        spot = pl.ds(pl.multiple_of(place(depth, z, x) * rows, rows), rows)
        y_spot = y_place(y)
        pairs.append((arrays[n].at[i], weight.at[y_spot, spot, pl.ds(half * wide, wide)]))
    return start_copies(pairs, sems)


def up_kernel(depth, parts, bias_ref, *rest):
    halves, rest = rest[: 2 * SHARES], rest[2 * SHARES :]
    count = 1 + max(p[0] for p in parts)
    arrays = rest[:count]
    second_ref, active_ref, slope_ref, weight, sems = rest[count:]
    copies = load_up(depth, parts, arrays, weight, sems)
    size = halves[0].shape[0]
    piece = size * SHARES
    for n, ref in enumerate(halves):
        second_ref[pl.ds(n * size, size), :] = ref[...]
    for copy in copies:
        copy.wait()
    wide = weight.shape[2]
    for y in range(2):
        for column in range(0, wide, 256):
            for begin in range(0, 2 * piece, piece):
                rows = pl.ds(begin, piece)
                columns = pl.ds(y * wide + column, 256)
                hidden = dot(second_ref[rows, :], weight[y, :, pl.ds(column, 256)], NN) + bias_ref[:, columns]
                gate = 0.5 + 0.5 * lax.erf(hidden * 0.7071067811865476)
                active_ref[rows, columns] = (hidden * gate).astype(BF16)
                bell = jnp.exp2(hidden * hidden * (-0.5 * LOG2E)) * 0.3989422804014327
                slope_ref[rows, columns] = (gate + hidden * bell).astype(BF16)


def load_down(depth, parts, arrays, weight, sems):
    pairs = []
    rows = arrays[0].shape[1]
    for n, i, half, z, x, y in parts:
        line = place(depth, z, x) * (2 * rows) + half * rows
        spot = pl.ds(pl.multiple_of(line, rows), rows)
        pairs.append((arrays[n].at[i], weight.at[y_place(y), spot]))
    return start_copies(pairs, sems)


def hidden_kernel(depth, parts, rows, own_ref, other_ref, slope_ref, act_ref, *rest):
    count = 1 + max(p[0] for p in parts)
    arrays = rest[:count]
    out_ref, sum_ref, *blocks = rest[count:-6]
    weight, grad, scratch, sems, grad_sems, act_sems = rest[-6:]
    piece = own_ref.shape[0]
    copies = start_copies(
        [(own_ref, grad.at[pl.ds(0, piece)]), (other_ref, grad.at[pl.ds(piece, piece)])], grad_sems
    )
    copies += load_down(depth, parts, arrays, weight, sems)
    for copy in copies:
        copy.wait()
    half = own_ref.shape[1] // 2
    for column in range(0, out_ref.shape[1], 512):
        columns = pl.ds(column, 512)
        total = dot(grad[:, pl.ds(0, half)], weight[0, columns, :], NT)
        total = total + dot(grad[:, pl.ds(half, half)], weight[1, columns, :], NT)
        low = (total * slope_ref[:, columns].astype(F32)).astype(BF16)
        out_ref[:, columns] = low
        sum_ref[0:1, columns] = jnp.sum(low.astype(F32), axis=0, keepdims=True)
    columns_grad_kernel(depth, rows, 1, act_ref, out_ref, *blocks, scratch, act_sems)


def down_kernel(depth, parts, active_ref, *rest):
    count = 1 + max(p[0] for p in parts)
    arrays = rest[:count]
    keep_ref, *sends = rest[count:-2]
    weight, sems = rest[-2:]
    piece, width = keep_ref.shape
    for copy in load_down(depth, parts, arrays, weight, sems):
        copy.wait()
    half = width // 2
    for y in range(2):
        columns = pl.ds(y * half, half)
        put_rows(sends, columns, dot(active_ref[pl.ds(piece, piece), :], weight[y], NN))
        keep_ref[:, columns] = dot(active_ref[pl.ds(0, piece), :], weight[y], NN)


def up_back_kernel(depth, parts, grad_ref, *rest):
    count = 1 + max(p[0] for p in parts)
    arrays = rest[:count]
    keep_ref, *sends = rest[count:-2]
    weight, sems = rest[-2:]
    piece, width = keep_ref.shape
    for copy in load_up(depth, parts, arrays, weight, sems):
        copy.wait()
    wide = weight.shape[2]
    for refs, begin in ((sends, piece), ([keep_ref], 0)):
        rows = pl.ds(begin, piece)
        for column in range(0, width, 512):
            columns = pl.ds(column, 512)
            total = dot(grad_ref[rows, pl.ds(0, wide)], weight[0, columns, :], NT)
            total = total + dot(grad_ref[rows, pl.ds(wide, wide)], weight[1, columns, :], NT)
            put_rows(refs, columns, total)


def middle_back_kernel(keep_ref, middle_ref, grad_ref, rows_ref, *rest):
    others, (middle_out, *branches, sum_out) = rest[:SHARES], rest[SHARES:]
    totals = [jnp.zeros((1, keep_ref.shape[1]), F32) for _ in range(4)]
    size = others[0].shape[0]
    for begin in range(0, SHARES * size, LINES):
        k = begin // size
        rows = pl.ds(begin, LINES)
        lines = pl.ds(begin % size, LINES)
        grad = keep_ref[rows, :] + others[k][lines, :].astype(F32)
        hat, inverse = normal(middle_ref[rows, :])
        scaled = grad * rows_ref[2:3, :]
        first = jnp.mean(scaled, axis=-1, keepdims=True)
        second = jnp.mean(scaled * hat, axis=-1, keepdims=True)
        outer = grad_ref[rows, :].astype(F32)
        result = outer + inverse * (scaled - first - hat * second)
        middle_out[rows, :] = result
        low = result.astype(BF16)
        branches[k][lines, :] = low
        for n, value in enumerate((grad * hat, grad, low.astype(F32), outer)):
            totals[n] = totals[n] + jnp.sum(value, axis=0, keepdims=True)
    for n in range(4):
        sum_out[n : n + 1, :] = totals[n]


def out_kernel(middle_ref, keep_ref, rows_ref, *rest):
    others, (out_ref,) = rest[:SHARES], rest[SHARES:]
    size = others[0].shape[0]
    for begin in range(0, SHARES * size, LINES):
        k = begin // size
        rows = pl.ds(begin, LINES)
        lines = pl.ds(begin % size, LINES)
        total = middle_ref[rows, :] + (keep_ref[rows, :] + others[k][lines, :].astype(F32)) + rows_ref[5:6, :]
        out_ref[rows, :] = total.astype(BF16)


def tokens_back_kernel(keep_ref, own_ref, grad_ref, rows_ref, *rest):
    others, (out_ref, sum_out) = rest[:SHARES], rest[SHARES:]
    totals = [jnp.zeros((1, keep_ref.shape[1]), F32) for _ in range(2)]
    size = others[0].shape[0]
    for begin in range(0, SHARES * size, LINES):
        k = begin // size
        rows = pl.ds(begin, LINES)
        lines = pl.ds(begin % size, LINES)
        grad = keep_ref[rows, :] + others[k][lines, :].astype(F32)
        hat, inverse = normal(own_ref[rows, :].astype(F32))
        scaled = grad * rows_ref[0:1, :]
        first = jnp.mean(scaled, axis=-1, keepdims=True)
        second = jnp.mean(scaled * hat, axis=-1, keepdims=True)
        result = grad_ref[rows, :] + inverse * (scaled - first - hat * second)
        out_ref[rows, :] = result.astype(BF16)
        for n, value in enumerate((grad * hat, grad)):
            totals[n] = totals[n] + jnp.sum(value, axis=0, keepdims=True)
    for n in range(2):
        sum_out[n : n + 1, :] = totals[n]


def load_columns(depth, source, scratch, rows, sems):
    pairs = []
    for x in range(2):
        for z in range(depth):
            spot = pl.ds(pl.multiple_of(place(depth, z, x) * rows, rows), rows)
            pairs.append((source.at[:, spot], scratch.at[:, pl.ds((x * depth + z) * rows, rows)]))
    return start_copies(pairs, sems)


def rows_grad_kernel(depth, rows, sent, act_ref, own_ref, other_ref, *rest):
    outs, (scratch, grad, sems, grad_sems) = rest[:-4], rest[-4:]
    piece = own_ref.shape[0]
    copies = start_copies(
        [(own_ref, grad.at[pl.ds(0, piece)]), (other_ref, grad.at[pl.ds(piece, piece)])], grad_sems
    )
    pairs = []
    order = [z for group in near_first(depth) for z in group]
    for n, z in enumerate(order):
        spot = pl.ds(pl.multiple_of(place(depth, z, sent) * rows, rows), rows)
        pairs.append((act_ref.at[:, spot], scratch.at[:, pl.ds(n * rows, rows)]))
    copies += start_copies(pairs, sems)
    for copy in copies:
        copy.wait()
    part = grad.shape[1] // 2
    begin = 0
    for ref in outs:
        size = ref.shape[0]
        for y_near in range(2):
            columns = pl.ds(pl.multiple_of(y_place(y_near) * part, 128), part)
            result = dot(scratch[:, pl.ds(begin * rows, size * rows)], grad[:, columns], TN, BF16)
            for k in range(size):
                ref[k, y_near] = result[k * rows : (k + 1) * rows]
        begin += size


def rows_grad(act, grad_own, grad_other, depth, rows, sent):
    length = act.shape[0]
    width = grad_own.shape[1]
    return (
        functools.partial(rows_grad_kernel, depth, rows, sent),
        [act, grad_own, grad_other],
        [ANYWHERE] * 3,
        [shape_of((len(group), 2, rows, width // 2), BF16) for group in near_first(depth)],
        [
            pltpu.VMEM((length, depth * rows), BF16),
            pltpu.VMEM((length, width), BF16),
            pltpu.SemaphoreType.DMA((depth,)),
            pltpu.SemaphoreType.DMA((2,)),
        ],
    )


def columns_grad_kernel(depth, rows, sent, act_ref, grad_ref, *rest):
    outs, scratch, sems = rest[:-2], rest[-2], rest[-1]
    pairs = []
    order = [z for group in near_first(depth) for z in group]
    for n, z in enumerate(order):
        for x in range(2):
            spot = pl.ds(pl.multiple_of(place(depth, z, x) * rows, rows), rows)
            pairs.append((act_ref.at[:, spot], scratch.at[:, pl.ds((2 * n + x) * rows, rows)]))
    for copy in start_copies(pairs, sems):
        copy.wait()
    part = grad_ref.shape[1] // 2
    begin = 0
    half = part // 2
    y = y_place(sent)
    for ref in outs:
        size = ref.shape[0]
        for column in range(0, part, half):
            columns = pl.ds(pl.multiple_of(y * part + column, 128), half)
            result = dot(scratch[:, pl.ds(begin * rows, 2 * size * rows)], grad_ref[:, columns], TN, BF16)
            for k in range(size):
                for x in range(2):
                    line = (2 * k + x) * rows
                    ref[k, x, :, pl.ds(column, half)] = result[line : line + rows]
        begin += 2 * size


def columns_grad(act, grad, depth, rows, sent):
    length, total = act.shape
    part = grad.shape[1] // 2
    return (
        functools.partial(columns_grad_kernel, depth, rows, sent),
        [act, grad],
        [ANYWHERE, WHOLE],
        [shape_of((len(group), 2, rows, part), BF16) for group in near_first(depth)],
        [pltpu.VMEM((length, total), BF16), pltpu.SemaphoreType.DMA((2 * depth,))],
    )


def own_half(core, mine, other):
    first = core == 0
    return jnp.where(first, mine, other), jnp.where(first, other, mine)


def split_kernel(hidden_block, qkv_ref, up_ref, qkv_mine, qkv_other, up_mine, up_other):
    core = lax.axis_index("core")
    rows = qkv_ref.shape[0]
    low = lax.broadcasted_iota(jnp.int32, (rows, 128), 1) < 64
    for tile in range(qkv_ref.shape[1] // 256):
        one = qkv_ref[:, pl.ds(tile * 256, 128)].astype(F32)
        two = qkv_ref[:, pl.ds(tile * 256 + 128, 128)].astype(F32)
        even = jnp.where(low, one, pltpu.roll(two, 64, 1)).astype(BF16)
        odd = jnp.where(low, pltpu.roll(one, 64, 1), two).astype(BF16)
        mine, other = own_half(core, even, odd)
        qkv_mine[:, pl.ds(tile * 128, 128)] = mine
        qkv_other[:, pl.ds(tile * 128, 128)] = other
    for tile in range(up_ref.shape[1] // (2 * hidden_block)):
        even = up_ref[:, pl.ds(tile * 2 * hidden_block, hidden_block)]
        odd = up_ref[:, pl.ds((tile * 2 + 1) * hidden_block, hidden_block)]
        mine, other = own_half(core, even, odd)
        up_mine[:, pl.ds(tile * hidden_block, hidden_block)] = mine
        up_other[:, pl.ds(tile * hidden_block, hidden_block)] = other


def pack_kernel(mine_ref, other_ref, *rest):
    extra, out_ref = rest[:-1], rest[-1]
    rows, columns = mine_ref.shape
    half = out_ref.shape[2]
    for ref, number in ((mine_ref, lax.axis_index("core")), (other_ref, 1 - lax.axis_index("core"))):
        lines = pl.ds(pl.multiple_of(number * rows, rows), rows)
        out_ref[0, lines, :] = ref[:, pl.ds(0, half)]
        out_ref[1, lines, pl.ds(0, columns - half)] = ref[:, pl.ds(half, columns - half)]
    for ref in extra:
        thin = ref.shape[1] // 2
        for k in range(2):
            out_ref[1, pl.ds(k * rows, rows), pl.ds(half - thin, thin)] = ref[:, pl.ds(k * thin, thin)]


def join_heads_kernel(mine_ref, other_ref, out_ref):
    rows = mine_ref.shape[0]
    low = lax.broadcasted_iota(jnp.int32, (rows, 128), 1) < 64
    for tile in range(mine_ref.shape[1] // 128):
        columns = pl.ds(tile * 128, 128)
        even, odd = own_half(lax.axis_index("core"), mine_ref[:, columns].astype(F32), other_ref[:, columns].astype(F32))
        out_ref[:, pl.ds(tile * 256, 128)] = jnp.where(low, even, pltpu.roll(odd, 64, 1))
        out_ref[:, pl.ds(tile * 256 + 128, 128)] = jnp.where(low, pltpu.roll(even, 64, 1), odd)


def join_blocks_kernel(block, mine_ref, other_ref, out_ref):
    for tile in range(mine_ref.shape[1] // block):
        columns = pl.ds(tile * block, block)
        even, odd = own_half(lax.axis_index("core"), mine_ref[:, columns].astype(F32), other_ref[:, columns].astype(F32))
        out_ref[:, pl.ds(2 * tile * block, block)] = even
        out_ref[:, pl.ds((2 * tile + 1) * block, block)] = odd


def mixed_grad_kernel(depth, sent, act_ref, *rest):
    count = len(rest) - 9
    pieces, (proj_ref, *outs) = rest[:count], rest[count : count + 5]
    scratch, mixed, sems, mixed_sems = rest[count + 5 :]
    rows = outs[0].shape[1]
    copies = load_columns(depth, act_ref, scratch, rows, sems)
    size = pieces[0].shape[1]
    wide = size * count // 3
    thin = wide // 2
    copies += start_copies(
        [(ref, mixed.at[:, pl.ds(n * size, size)]) for n, ref in enumerate(pieces)],
        mixed_sems,
    )
    for copy in copies:
        copy.wait()
    part = wide + thin
    half = depth * rows
    columns = pl.ds(pl.multiple_of(y_place(sent) * part, 128), wide)
    for x in range(2):
        result = dot(scratch[:, pl.ds(x * half, half)], mixed[:, columns], TN, BF16)
        for z in range(depth):
            outs[1 - x][z] = result[z * rows : (z + 1) * rows]
    for y_near in range(2):
        columns = pl.ds(pl.multiple_of(y_place(y_near) * part + wide, 128), thin)
        result = dot(scratch[:, pl.ds(sent * half, half)], mixed[:, columns], TN, BF16)
        for z in range(depth):
            outs[3 - y_near][z, :, pl.ds(0, thin)] = result[z * rows : (z + 1) * rows]
            outs[3 - y_near][z, :, pl.ds(thin, thin)] = proj_ref[sent, y_near, z]


def mixed_back_kernel(depth, parts, count, *rest):
    pieces, rest = rest[:count], rest[count:]
    arrays = rest[: 1 + max(p[0] for p in parts)]
    keep_ref, *sends = rest[len(arrays) : -4]
    weight, mixed, sems, mixed_sems = rest[-4:]
    pairs = []
    rows = arrays[0].shape[1]
    size = pieces[0].shape[1]
    wide = size * count // 3
    thin = wide // 2
    copies = start_copies(
        [(ref, mixed.at[:, pl.ds(n * size, size)]) for n, ref in enumerate(pieces)], mixed_sems
    )
    for n, i, half, z, x, y in parts:
        spot = pl.ds(pl.multiple_of(place(depth, z, x) * rows, rows), rows)
        y_spot = y_place(y)
        if half == 0:
            pairs.append((arrays[n].at[i], weight.at[y_spot, spot, pl.ds(0, wide)]))
        else:
            pairs.append((arrays[n].at[i, :, pl.ds(0, thin)], weight.at[y_spot, spot, pl.ds(wide, thin)]))
    copies += start_copies(pairs, sems)
    for copy in copies:
        copy.wait()
    piece, width = keep_ref.shape
    part = wide + thin
    for refs, begin in ((sends, piece), ([keep_ref], 0)):
        lines = pl.ds(begin, piece)
        for column in range(0, width, 512):
            columns = pl.ds(column, 512)
            total = dot(mixed[lines, pl.ds(0, part)], weight[0, columns, :], NT)
            total = total + dot(mixed[lines, pl.ds(part, part)], weight[1, columns, :], NT)
            put_rows(refs, columns, total)


def sum_of(refs):
    total = None
    for ref in refs:
        value = ref[(0,) * (len(ref.shape) - 2)].astype(F32)
        total = value if total is None else total + value
    return total


def core_rows(values_ref, rows, mine_ref, send_ref):
    core = lax.axis_index("core")
    mine_ref[...] = values_ref[pl.ds(pl.multiple_of(core * rows, rows), rows), :]
    send_ref[...] = values_ref[pl.ds(pl.multiple_of((1 - core) * rows, rows), rows), :].astype(BF16)


def finish_up_kernel(*refs):
    mine_ref, send_ref, total = refs[-3:]
    total[...] = sum_of(refs[:-3])
    core_rows(total, mine_ref.shape[0], mine_ref, send_ref)


def finish_down_kernel(*refs):
    refs[-1][...] = sum_of(refs[:-1])


def hop_first_kernel(*refs):
    out_ref = refs[-1]
    ones, twos = refs[0:3], refs[3:6]
    for half, group in ((0, ones), (1, twos)):
        total = sum_of(group)
        if len(refs) > 7:
            total = total + refs[6][half].astype(F32)
        out_ref[half] = total.astype(BF16)


def finish_first_kernel(*refs):
    moving = refs[6]
    mine_ref, send_ref, proj_ref, total = refs[7:]
    one = sum_of(refs[0:3]) + moving[0].astype(F32)
    two = sum_of(refs[3:6]) + moving[1].astype(F32)
    wide = one.shape[1]
    thin = total.shape[1] - wide
    total[:, pl.ds(0, wide)] = one
    total[:, pl.ds(wide, thin)] = two[:, :thin]
    core_rows(total, mine_ref.shape[0], mine_ref, send_ref)
    group = proj_ref.shape[0]
    for k in range(2):
        proj_ref[:, pl.ds(k * (wide - thin), wide - thin)] = two[k * group : (k + 1) * group, thin:]


def first_terms(keeps, nears, lasts, z):
    arrays, specs = [], []
    for keep_one, near, last in zip(keeps, nears, lasts):
        rows, columns = last.shape[-2:]
        arrays += [keep_one, near, last]
        specs += [pl.BlockSpec((1, rows, columns), lambda i: (z, 0, 0))] * 3
    return arrays, specs


def same(shape):
    return pl.BlockSpec(shape, lambda i: (0,) * len(shape))


EACH = 32
ROW = 512


def params_kernel(count, head_size, hidden_block, in_ref, rows_ref, qkv_ref, up_ref):
    core = lax.axis_index("core")
    row = lax.broadcasted_iota(jnp.int32, (count, 128), 0)
    lane = lax.broadcasted_iota(jnp.int32, (count, 128), 1)
    per = 128 // EACH
    for i in range(6):
        tile = in_ref[:, pl.ds(i // per * 128, 128)]
        shift = (128 - i % per * EACH) % 128
        first = jnp.where(lane < EACH, pltpu.roll(tile, shift, 1) if shift else tile, 0.0)
        wide = first
        for k in range(1, per):
            wide = wide + pltpu.roll(first, k * EACH, 1)
        for k in range(count // per):
            picked = jnp.where(row == k * per + lane // EACH, wide, 0.0)
            rows_ref[i : i + 1, pl.ds(k * 128, 128)] = jnp.sum(picked, axis=0, keepdims=True)
    one_lane = lax.broadcasted_iota(jnp.int32, (1, 128), 1)
    size = 3 * EACH
    low = one_lane < head_size
    for t in range(qkv_ref.shape[1] // 128):
        pair = []
        for k in (2 * t, 2 * t + 1):
            tile = jnp.zeros((1, 128), F32)
            for d in range(k * 128 // size, (k * 128 + 127) // size + 1):
                offset = d * size - k * 128
                value = in_ref[d : d + 1, pl.ds(256, 128)]
                value = pltpu.roll(value, offset % 128, 1) if offset % 128 else value
                tile = jnp.where((one_lane >= offset) & (one_lane < offset + size), value, tile)
            pair.append(tile)
        even = jnp.where(low, pair[0], pltpu.roll(pair[1], head_size, 1))
        odd = jnp.where(low, pltpu.roll(pair[0], head_size, 1), pair[1])
        qkv_ref[:, pl.ds(t * 128, 128)] = jnp.where(core == 0, even, odd)
    tiles = hidden_block // 128
    for t in range(up_ref.shape[1] // 128):
        m, q = divmod(t, tiles)
        spots = [2 * m * tiles + q, (2 * m + 1) * tiles + q]
        even, odd = [in_ref[d : d + 1, pl.ds(384, 128)] for d in spots]
        up_ref[:, pl.ds(t * 128, 128)] = jnp.where(core == 0, even, odd)


def small_kernel(count, head_size, hidden_block, mixed_count, *refs):
    first_ref, middle_ref, up_ref = refs[:3]
    mixed_refs = refs[3 : 3 + mixed_count]
    out_ref = refs[-1]
    core = lax.axis_index("core")
    row = lax.broadcasted_iota(jnp.int32, (count, 128), 0)
    lane = lax.broadcasted_iota(jnp.int32, (count, 128), 1)
    per = 128 // EACH
    vectors = [(first_ref, 0), (first_ref, 1), (middle_ref, 0), (middle_ref, 1), (middle_ref, 2), (middle_ref, 3)]
    tiles = [jnp.zeros((count, 128), F32) for _ in range(2)]
    for i, (ref, line) in enumerate(vectors):
        spread = jnp.zeros((count, 128), F32)
        for k in range(count // per):
            spread = jnp.where(row // per == k, ref[line : line + 1, pl.ds(k * 128, 128)], spread)
        moved = spread
        for k in range(per):
            shift = (i % per - k) * EACH % 128
            if shift:
                moved = jnp.where(row % per == k, pltpu.roll(spread, shift, 1), moved)
        tiles[i // per] = jnp.where(lane // EACH == i % per, moved, tiles[i // per])
    for n, tile in enumerate(tiles):
        out_ref[:, pl.ds(n * 128, 128)] = tile
    one_lane = lax.broadcasted_iota(jnp.int32, (1, 128), 1)
    low = one_lane < head_size
    size = 3 * EACH
    globals_ = []
    for line in range(3):
        for ref in mixed_refs:
            for k in range(ref.shape[1] // 128):
                value = ref[line : line + 1, pl.ds(k * 128, 128)]
                other = pltpu.roll(value, head_size, 1)
                even = core == 0
                globals_.append(jnp.where(low == even, jnp.where(even, value, other), 0.0))
                globals_.append(jnp.where(low == even, jnp.where(even, other, value), 0.0))
    for d in range(count):
        total = jnp.zeros((1, 128), F32)
        for k in range(d * size // 128, (d * size + size - 1) // 128 + 1):
            offset = k * 128 - d * size
            value = pltpu.roll(globals_[k], offset % 128, 1) if offset % 128 else globals_[k]
            inside = (one_lane >= offset) & (one_lane < offset + 128) & (one_lane < size)
            total = jnp.where(inside, value, total)
        out_ref[d : d + 1, pl.ds(256, 128)] = total
    steps = hidden_block // 128
    for t in range(up_ref.shape[1] // 128):
        m, q = divmod(t, steps)
        value = up_ref[0:1, pl.ds(t * 128, 128)]
        for p in range(2):
            d = (2 * m + p) * steps + q
            out_ref[d : d + 1, pl.ds(384, 128)] = jnp.where(core == p, value, 0.0)


HALF = 10


def turn_tables(places, head_size, wide):
    section = 2 * (head_size // 3 // 2)
    half_size = section // 2
    lane = jnp.arange(wide) % head_size
    number = lane // section
    spot = lane % section
    frequency = 1.0 / 10000.0 ** ((spot % half_size).astype(F32) / half_size)
    place_of = jnp.where(
        number[None, :] == 0,
        places[:, 0:1],
        jnp.where(number[None, :] == 1, places[:, 1:2], places[:, 2:3]),
    )
    angles = place_of.astype(F32) * frequency[None, :]
    live = (number < 3)[None, :]
    cosine = jnp.where(live, jnp.cos(angles), 1.0)
    sine = jnp.where(live, jnp.sin(angles), 0.0)
    low = (spot < half_size)[None, :]
    return cosine, jnp.where(low, -sine, 0.0), jnp.where(low, 0.0, sine)


def fast_shards(
    tokens,
    frame_index,
    row_index,
    column_index,
    norm1_gain,
    norm1_bias,
    qkv_weight,
    qkv_bias,
    proj_weight,
    proj_bias,
    norm2_gain,
    norm2_bias,
    up_weight,
    up_bias,
    down_weight,
    down_bias,
    cotangent,
):
    depth = lax.axis_size("z")
    everyone = ("z", "x", "core", "y")
    count = 8 * depth
    piece, width = tokens.shape
    length = 2 * piece
    head_size = width // HEADS
    local = width // 2
    hidden_block = down_weight.shape[0]
    hidden_size = up_weight.shape[1]
    up_rows = width // (2 * depth)
    shard_rows = qkv_weight.shape[0]
    part_qkv = 3 * local // 2
    part_up = up_weight.shape[1] // 2
    block_kind = shape_of((2, up_rows, local), BF16)
    step = max(depth // 2, 1)
    dma = pltpu.SemaphoreType.DMA
    shares = [shape_of((piece // SHARES, width), BF16)] * SHARES
    partial = [shape_of((piece, width), F32)] + shares

    qkv_mine, qkv_other, up_mine, up_other = kernel_call(
        functools.partial(split_kernel, hidden_block),
        [qkv_weight, up_weight],
        [WHOLE, WHOLE],
        [shape_of((shard_rows, part_qkv), BF16)] * 2 + [shape_of((shard_rows, part_up), BF16)] * 2,
    )
    (first_block,) = kernel_call(
        pack_kernel, [qkv_mine, swap(qkv_other, "core"), proj_weight], [WHOLE] * 3, [block_kind]
    )
    now = (first_block,)

    def at(values):
        return after(values, *now)

    def packed_small():
        return jnp.concatenate(
            [
                at(item)
                for item in (norm1_gain, norm1_bias, norm2_gain, norm2_bias, proj_bias, down_bias)
            ]
            + [jnp.zeros((256 - 6 * EACH,), BF16), qkv_bias, jnp.zeros((EACH,), BF16), up_bias]
        )

    hops = [first_block, ring(first_block, depth)]
    tokens_traded = trade(at(tokens))
    places = jnp.stack([frame_index, row_index, column_index], axis=0)
    places_traded = trade(at(places))
    small = packed_small()
    up_other = swap(at(up_other), "core")
    now = (hops[1], up_other, small)
    hops.append(ring(at(hops[1]), depth))
    grad_traded = trade(at(cotangent))
    (up_block,) = kernel_call(pack_kernel, [at(up_mine), up_other], [WHOLE] * 2, [block_kind])
    now = (hops[2], up_block, tokens_traded)
    while len(hops) < depth:
        hops.append(ring(at(hops[-1]), depth))

    def far_halves(block):
        block = at(block)
        return [block, swap(block[0], "x")[None], swap(block[1], "y")[None]]

    def doubled(parts):
        return join([at(parts[0])] + parts[1:], [(0, 0, 1), (1, 0, 1), (0, 1, 1), (2, 0, 1)])

    def two_halves(hops):
        return [join([at(hops[0])] + hops[1:], [(n, half, 1) for n in range(depth)]) for half in range(2)]

    small = jnp.broadcast_to(at(small).astype(F32), (count, ROW))
    small = lax.all_to_all(small, everyone, split_axis=0, concat_axis=0, tiled=True)
    places = choose(at(places), places_traded)
    places = jnp.concatenate([places, swap(places, "core")], axis=1).T
    grad_own = choose(at(cotangent), grad_traded)
    tokens_own = choose(at(tokens), tokens_traded)
    tokens_other = swap(tokens_own, "core")
    now = (hops[-1], tokens_other, places, grad_own, small)

    one, two = two_halves(hops)
    one_x = swap(one, "x")
    two_y = swap(two, "y")
    one_y = swap(one, "y")
    two_x = swap(two, "x")
    up_hops = [up_block, ring(at(up_block), depth)]
    turn = turn_tables(at(places), head_size, 2 * head_size)
    grad_other = swap(at(grad_own), "core")
    now = (one_x, two_y, up_hops[-1], grad_other, *turn)
    one_xy = swap(at(one_x), "y")
    two_xy = swap(at(two_y), "x")
    up_hops.append(ring(at(up_hops[-1]), depth))
    params, bias_qkv, bias_up = kernel_call(
        functools.partial(params_kernel, count, head_size, hidden_block),
        [at(small)],
        [WHOLE],
        [shape_of((8, width), F32), shape_of((1, 3 * local), F32), shape_of((1, hidden_size), F32)],
    )
    now = (one_y, two_x, up_hops[-1], params)
    while len(up_hops) < depth:
        up_hops.append(ring(at(up_hops[-1]), depth))
    down_far = far_halves(down_weight.reshape(2, hidden_block // 2, -1))
    now = (one_xy, two_xy, up_hops[-1], *down_far)

    first_arrays = [one, two, one_x, two_y, one_y, two_x, one_xy, two_xy]
    marks = [(0, 0, 0), (1, 0, 0), (0, 1, 0), (1, 0, 1), (0, 0, 1), (1, 1, 0), (0, 1, 1), (1, 1, 1)]
    first_parts = [
        (n, z, half, z, x, y) for n, (half, x, y) in enumerate(marks) for z in range(depth)
    ]
    part_count = len(first_parts)
    pair_parts = []
    for z in range(depth):
        pair_parts += [(z, 0, 0, z, 0, 0), (z, 1, 0, z, 1, 0), (z, 2, 1, z, 0, 0), (z, 3, 1, z, 0, 1)]
        array = depth + 2 * (z // step)
        k = z % step
        pair_parts += [
            (array, 2 * k, 0, z, 0, 1),
            (array, 2 * k + 1, 0, z, 1, 1),
            (array + 1, 2 * k, 1, z, 1, 0),
            (array + 1, 2 * k + 1, 1, z, 1, 1),
        ]
    pair_count = len(pair_parts)

    up_one, up_two = two_halves(up_hops)
    down_hops = [doubled(down_far)]
    up_one_x = swap(up_one, "x")
    up_two_y = swap(up_two, "y")
    up_one_y = swap(up_one, "y")
    up_two_x = swap(up_two, "x")
    down_hops.append(ring(down_hops[0], depth))
    normed, queries, keys, values = kernel_call(
        functools.partial(qkv_kernel, depth, first_parts),
        [after(tokens_own, up_one, up_two, down_hops[0]), tokens_other, params, bias_qkv, *turn, *first_arrays],
        [WHOLE] * 7 + [ANYWHERE] * len(first_arrays),
        [shape_of((length, width), BF16)] + [shape_of((length, local), BF16)] * 3,
        scratch=[pltpu.VMEM((2, width, 3 * local // 2), BF16), dma((part_count,))],
    )
    now = (normed, up_one_x, up_two_y, down_hops[-1])
    up_one_xy = swap(at(up_one_x), "y")
    up_two_xy = swap(at(up_two_y), "x")
    up_arrays = [up_one, up_two, up_one_x, up_two_y, up_one_y, up_two_x, up_one_xy, up_two_xy]
    down_hops.append(ring(at(down_hops[-1]), depth))
    attended, logs = attend(at(queries), keys, values, head_size)
    now = (attended, up_one_y, up_two_x, up_one_xy, up_two_xy, down_hops[-1])

    def last_pair(group):
        ones = join([at(group[0])] + group[1:], [(n, 0, 2) for n in range(len(group))])
        twos = join([at(group[0])] + group[1:], [(n, 2, 2) for n in range(len(group))])
        return ones, twos

    def last_swaps(pair):
        return [swap(at(pair[0]), "y"), swap(at(pair[1]), "x")]

    while len(down_hops) < depth:
        down_hops.append(ring(at(down_hops[-1]), depth))
    near_pair = last_pair(down_hops[:step])
    near = last_swaps(near_pair)
    proj_scratch = [pltpu.VMEM((2, local, width // 2), BF16), dma((part_count,))]
    kept, *sent = kernel_call(
        functools.partial(proj_kernel, depth, first_parts),
        [after(attended, *near_pair), *first_arrays],
        [WHOLE] + [ANYWHERE] * len(first_arrays),
        partial,
        scratch=proj_scratch,
    )
    middle, *second_own = kernel_call(
        middle_kernel, [tokens_own, kept, params, *swap_each(sent)], [WHOLE] * (3 + SHARES), partial
    )
    second_other = swap_each(second_own)
    now = (*second_own, down_hops[-1])
    far_pair = last_pair(down_hops[step:])
    far = last_swaps(far_pair)
    down_arrays = down_hops + near + far
    up_scratch = [pltpu.VMEM((2, width, hidden_size // 2), BF16), dma((part_count,))]
    second, active, slope = kernel_call(
        functools.partial(up_kernel, depth, first_parts),
        [after(bias_up, *far_pair), *second_own, *second_other, *up_arrays],
        [WHOLE] * (1 + 2 * SHARES) + [ANYWHERE] * len(up_arrays),
        [shape_of((length, width), BF16)] + [shape_of((length, hidden_size), BF16)] * 2,
        scratch=up_scratch,
    )
    (down_sends,) = merged_call(
        rows_grad(active, grad_own, grad_other, depth, hidden_block, 1)
    )
    down_sum = Scatter(down_sends, "x", "y", depth)
    now = (*down_sends, *far_pair)
    down_sum.send()
    down_sum.send()
    down_scratch = [pltpu.VMEM((2, hidden_size, width // 2), BF16), dma((pair_count,))]
    hidden_grad, up_sums, *up_sends = kernel_call(
        functools.partial(hidden_kernel, depth, pair_parts, up_rows),
        [grad_own, grad_other, at(slope), second, *down_arrays],
        [ANYWHERE] * 2 + [WHOLE] + [ANYWHERE] * (1 + len(down_arrays)),
        [shape_of((length, hidden_size), BF16), shape_of((8, hidden_size), F32)]
        + [shape_of((len(group), 2, up_rows, hidden_size // 2), BF16) for group in near_first(depth)],
        scratch=[
            down_scratch[0],
            pltpu.VMEM((length, width), BF16),
            pltpu.VMEM((length, width), BF16),
            down_scratch[1],
            dma((2,)),
            dma((2 * depth,)),
        ],
    )
    up_sum = Scatter(up_sends, "y", "x", depth)
    up_sum.send()
    up_sum.send()
    now = tuple(up_sends)
    (kept, *sent), down_sum.keeps = merged_call(
        (
            functools.partial(up_back_kernel, depth, first_parts),
            [at(hidden_grad), *up_arrays],
            [WHOLE] + [ANYWHERE] * len(up_arrays),
            partial,
            up_scratch,
        ),
        rows_grad(active, grad_own, grad_other, depth, hidden_block, 0),
    )
    sent_other = swap_each(sent)
    gate = down_sum.hop(0, down_sum.keeps[0])
    (middle_grad, *branch_own, middle_sums), up_sum.keeps = merged_call(
        (
            middle_back_kernel,
            [after(kept, gate), middle, grad_own, params, *sent_other],
            [WHOLE] * (4 + SHARES),
            partial + [shape_of((8, width), F32)],
            [],
        ),
        columns_grad(second, hidden_grad, depth, up_rows, 0),
    )
    branch_other = swap_each(branch_own)
    attended_grad, proj_blocks = kernel_call(
        functools.partial(proj_back_kernel, depth, first_parts),
        [after(attended, *up_sum.keeps), *branch_own, *branch_other, *first_arrays],
        [WHOLE] + [ANYWHERE] * (2 * SHARES + len(first_arrays)),
        [shape_of((length, local), BF16), shape_of((2, 2, depth, up_rows, width // 4), BF16)],
        scratch=[
            proj_scratch[0],
            pltpu.VMEM((local, width // 2), F32),
            pltpu.VMEM((length, width), BF16),
            proj_scratch[1],
            dma((2 * SHARES,)),
        ],
    )
    pairs = local // (2 * head_size)
    groups = []

    def attend_next(*gates):
        k = len(groups)
        grads = after(attended_grad, *gates)
        groups.append(attend_back(queries, keys, values, grads, logs, turn, head_size, k, k + 1))
        return groups[-1][0]

    gate = attended_grad
    while len(groups) < pairs - 3:
        gate = attend_next(gate)
    gate = attend_next(down_sum.hop(1, gate))
    gate = attend_next(gate)
    gate = attend_next(down_sum.hop(2, gate), up_sum.arrived[0])
    mixed_pieces = [group[n] for n in range(3) for group in groups]

    def mixed_weight_grad(sent_number, *gates):
        block = (depth, up_rows, local)
        return (
            functools.partial(mixed_grad_kernel, depth, sent_number),
            [after(normed, *gates), *mixed_pieces, proj_blocks],
            [ANYWHERE] * (1 + len(mixed_pieces)) + [WHOLE],
            [shape_of(block, BF16)] * 4,
            [
                pltpu.VMEM((length, width), BF16),
                pltpu.VMEM((length, 3 * local), BF16),
                dma((2 * depth,)),
                dma((len(mixed_pieces),)),
            ],
        )

    ((one_far, one_near, two_far, two_near),) = merged_call(mixed_weight_grad(1, gate))
    now = (one_far,)
    fars = [swap(one_far, "y"), swap(two_far, "x")]
    gate = up_sum.hop(0, *now, down_sum.moving)
    (kept, *sent), keeps = merged_call(
        (
            functools.partial(mixed_back_kernel, depth, first_parts, len(mixed_pieces)),
            [after(mixed_pieces[0], gate, up_sum.arrived[1]), *mixed_pieces[1:], *first_arrays],
            [ANYWHERE] * (len(mixed_pieces) + len(first_arrays)),
            partial,
            [
                pltpu.VMEM((2, width, 3 * local // 2), BF16),
                pltpu.VMEM((length, 3 * local), BF16),
                dma((part_count,)),
                dma((len(mixed_pieces),)),
            ],
        ),
        mixed_weight_grad(0),
    )
    sent_other = swap_each([after(item, *fars, up_sum.moving) for item in sent])
    now = (keeps[0], *fars, up_sum.moving)
    fars = [add_blocks([(at(keep_one), ()), (arrived, ())]) for keep_one, arrived in zip(keeps[::2], fars)]
    lasts = [swap(fars[0], "x"), swap(fars[1], "y")]
    nears = [swap(after(one_near, *fars), "y"), swap(after(two_near, *fars), "x")]
    up_sum.hop(1, *now)
    (tokens_grad, first_sums), (kept, *sent) = merged_call(
        (
            tokens_back_kernel,
            [after(kept, *fars), tokens_own, middle_grad, params, *sent_other],
            [WHOLE] * (4 + SHARES),
            [shape_of((piece, width), BF16), shape_of((8, width), F32)],
            [],
        ),
        (
            functools.partial(down_kernel, depth, pair_parts),
            [active, *down_arrays],
            [WHOLE] + [ANYWHERE] * len(down_arrays),
            partial,
            down_scratch,
        ),
    )
    now = (tokens_grad, *lasts, *nears, up_sum.moving)
    keeps = keeps[1::2]
    moving = None

    def first_hop(n):
        arrays, specs = first_terms(keeps, nears, lasts, n)
        if moving is not None:
            arrays.append(moving)
            specs.append(same(block_kind.shape))
        arrays[0] = at(arrays[0])
        (total,) = kernel_call(
            hop_first_kernel, arrays, specs, [block_kind], grid=(1,), out_specs=[same(block_kind.shape)]
        )
        return total, ring(total, depth)

    sent_other = swap_each([at(item) for item in sent])
    (small,) = kernel_call(
        functools.partial(small_kernel, count, head_size, hidden_block, len(groups)),
        [at(first_sums), middle_sums, up_sums] + [group[3] for group in groups],
        [WHOLE] * (3 + len(groups)),
        [shape_of((count, ROW), F32)],
    )
    for n in range(1, depth):
        total, moving = first_hop(n)
        if n == 1:
            small = lax.all_to_all(after(small, total), everyone, split_axis=0, concat_axis=0, tiled=True)
            (block_out,) = kernel_call(
                out_kernel,
                [middle, after(kept, total, small), params, *sent_other],
                [WHOLE] * (3 + SHARES),
                [shape_of((piece, width), BF16)],
            )
            now = (moving, block_out, small)
        elif n == 2:
            block_traded = trade(after(block_out, total))
            tokens_traded = trade(after(tokens_grad, total))
            up_sum.hop(2, total)
            now = (moving, down_sum.finish(total), tokens_traded, block_traded)
        else:
            tokens_out = choose(tokens_grad, after(tokens_traded, total))
            block_done = choose(block_out, after(block_traded, total))
            now = (moving, up_sum.finish(total), tokens_out, block_done)
    arrays, specs = first_terms(keeps, nears, lasts, 0)
    arrays[0] = at(arrays[0])
    out_shapes = [
        shape_of((shard_rows, part_qkv), F32),
        shape_of((shard_rows, part_qkv), BF16),
        shape_of(proj_weight.shape, F32),
    ]
    mine, sent, grad_proj = kernel_call(
        finish_first_kernel,
        arrays + [moving],
        specs + [same(block_kind.shape)],
        out_shapes,
        grid=(1,),
        out_specs=[same(kind.shape) for kind in out_shapes],
        scratch=[pltpu.VMEM((2 * shard_rows, part_qkv), F32)],
    )
    (grad_qkv,) = kernel_call(
        join_heads_kernel,
        [mine, swap(sent, "core")],
        [WHOLE] * 2,
        [shape_of(qkv_weight.shape, F32)],
    )
    small = jnp.sum(small, axis=0)

    def rest_of(scatter):
        arrays, specs = [], []
        for array, prefix in scatter.rest():
            lead = tuple(prefix) + (0,) * (array.ndim - len(prefix) - 2)
            arrays.append(array)
            specs.append(
                pl.BlockSpec((1,) * len(lead) + array.shape[-2:], lambda i, lead=lead: lead + (0, 0))
            )
        return arrays, specs

    arrays, specs = rest_of(up_sum)
    out_shapes = [shape_of((shard_rows, part_up), F32), shape_of((shard_rows, part_up), BF16)]
    mine, sent = kernel_call(
        finish_up_kernel,
        arrays,
        specs,
        out_shapes,
        grid=(1,),
        out_specs=[same(kind.shape) for kind in out_shapes],
        scratch=[pltpu.VMEM((2 * shard_rows, part_up), F32)],
    )
    (grad_up,) = kernel_call(
        functools.partial(join_blocks_kernel, hidden_block),
        [mine, swap(sent, "core")],
        [WHOLE] * 2,
        [shape_of(up_weight.shape, F32)],
    )
    arrays, specs = rest_of(down_sum)
    (grad_down,) = kernel_call(
        finish_down_kernel,
        arrays,
        specs,
        [shape_of(down_weight.shape, F32)],
        grid=(1,),
        out_specs=[same(down_weight.shape)],
    )

    def part(begin, size):
        return small[begin : begin + size]

    return (
        block_done,
        tokens_out,
        part(0, EACH),
        part(EACH, EACH),
        grad_qkv,
        part(256, 3 * EACH),
        grad_proj,
        part(4 * EACH, EACH),
        part(2 * EACH, EACH),
        part(3 * EACH, EACH),
        grad_up,
        part(384, 4 * EACH),
        grad_down,
        part(5 * EACH, EACH),
    )


def solution(mesh):
    ctx_count = mesh.shape["ctx"]
    dp_count = mesh.shape["dp"]
    if ctx_count == 2 and dp_count % 4 == 0:
        mesh = Mesh(
            mesh.devices.reshape(dp_count // 4, 2, 2, 2), ("z", "x", "core", "y")
        )
        dp = ("z", "x", "core")
        ctx = "y"
        every = P(dp + (ctx,))
        body = fast_shards
    else:
        dp = "dp"
        ctx = "ctx"
        every = P((dp, ctx))
        body = shards
    rows = P(every[0], None)
    matrix = P(dp, ctx)
    return jax.shard_map(
        body,
        mesh=mesh,
        in_specs=(
            rows,
            every,
            every,
            every,
            every,
            every,
            matrix,
            every,
            matrix,
            every,
            every,
            every,
            matrix,
            every,
            matrix,
            every,
            rows,
        ),
        out_specs=(
            rows,
            rows,
            every,
            every,
            matrix,
            every,
            matrix,
            every,
            every,
            every,
            matrix,
            every,
            matrix,
            every,
        ),
        check_vma=False,
    )
```
